32 devices in a mesh: group: 2 (over x), seq: 16 (over z, y, core).
Axes of the slice: x: 2, y: 2, z: 4, core: 2. Of those that a mesh axis runs over, the one named last changes fastest.
Arguments:
- query_rows: bfloat16 [8192, 1536], P(('group', 'seq')), parts along dimension 0, may hold values from -120 to 120
- key_rows: bfloat16 [8192, 1536], P(('group', 'seq')), parts along dimension 0, may hold values from -6.6 to 6.6
- value_rows: bfloat16 [8192, 1536], P(('group', 'seq')), parts along dimension 0, may hold values from -60 to 60
- block_list: int32 [64, 27], P(('group', 'seq')), parts along dimension 0, may hold values from -1 to 31, as said below
- out_weight: bfloat16 [1536, 3072], P('seq'), may hold values from -4 to 4
Outputs:
- projected: bfloat16 [8192, 3072], P(('group', 'seq')), parts along dimension 0
The draws below stay inside these ranges and needn't reach their ends.
There are 2 independent parts, one for each index of `group`. The reference program is written for one: setup_inputs(seed, part) draws one part's arguments, and reference() takes and returns one part's arrays. A program takes and returns all parts, laid end to end along the dimension named above; an argument that names none is the same for every part. Nothing has to cross between parts.
Inputs may be any that keep to these rules, and one draw needn't show every extreme that they name: `block_list`: tile t lies at grid row (t // 2) // 8, grid column (t // 2) % 8 and frame group t % 2. Row t lists distinct key tiles whose grid row, grid column and frame group each differ from t's by at most one; every such tile that shares t's grid row or grid column is listed, t itself among them; the other slots hold -1.
All inputs are finite; a program needn't handle non-finite values.
Results may differ from the reference program's by a relative error of at most 0.0056.
Values may be sent and summed in bfloat16 or wider, within the bound.
No kernel may reach another device: no remote copies, remote signals or barrier semaphores. Data moves between devices by JAX's collectives and lax.ppermute only.
A program may use at most 128 MiB of HBM per device.

```python
import jax
import jax.numpy as jnp
from jax import lax

D = 3072
HEADS = 12
HD = 128
TILE = 128
FRAMES = 2
GRID_COLS = 8
TILES = 32
TOKENS = 4096
NB = 27


def key_table(key):
    base = jnp.clip(jax.random.normal(jax.random.fold_in(key, 11), (TOKENS, HEADS * HD), jnp.float32), -6.0, 6.0)
    return base


def draw_key_rows(key, part):
    return key_table(key).astype(jnp.bfloat16)


def draw_query_rows(key, part):
    base = jnp.clip(jax.random.normal(jax.random.fold_in(key, 12), (TOKENS, HEADS * HD), jnp.float32), -6.0, 6.0)
    return base.astype(jnp.bfloat16)


def draw_value_rows(key, part):
    base = jnp.clip(jax.random.normal(jax.random.fold_in(key, 14), (TOKENS, HEADS * HD), jnp.float32), -6.0, 6.0)
    return base.astype(jnp.bfloat16)


def draw_block_list(key, part):
    tiles = jnp.arange(TILES, dtype=jnp.int32)[:, None]
    slots = jnp.arange(NB, dtype=jnp.int32)[None, :]
    place = tiles // FRAMES
    frame = tiles % FRAMES
    grid_row = place // GRID_COLS
    grid_col = place % GRID_COLS
    rows_total = TILES // (FRAMES * GRID_COLS)
    spatial_slot = slots % 9
    frame_step = slots // 9 - 1
    row_step = spatial_slot // 3 - 1
    col_step = spatial_slot % 3 - 1
    other_row = grid_row + row_step
    other_col = grid_col + col_step
    other_frame = frame + frame_step
    valid = (other_row >= 0) & (other_row < rows_total) & (other_col >= 0) & (other_col < GRID_COLS)
    valid = valid & (other_frame >= 0) & (other_frame < FRAMES)
    coin = jax.random.randint(jax.random.fold_in(key, 16), (TILES, NB), 0, 2)
    keep = (row_step == 0) | (col_step == 0) | (coin == 1)
    listed = (other_row * GRID_COLS + other_col) * FRAMES + other_frame
    return jnp.where(valid & keep, listed, -1).astype(jnp.int32)


def shard_levels(rng, shape, cuts, smallest, largest):
    gain = 1.0
    for dim, blocks in cuts:
        heights = jax.random.uniform(jax.random.fold_in(jax.random.fold_in(rng, 6), dim), (blocks,), jnp.float32, smallest / len(cuts), largest / len(cuts))
        gain = gain * jnp.repeat(jnp.exp(heights), shape[dim] // blocks).reshape((-1,) + (1,) * (len(shape) - 1 - dim))
    return gain


def gaussian(rng, dims, width, bound, cuts=(), kind=jnp.bfloat16):
    level = shard_levels(rng, dims, cuts, -0.22, 0.18) if cuts else 1.0
    entries = jax.random.normal(rng, dims, jnp.float32) * width * level
    return jnp.minimum(jnp.maximum(entries, -bound), bound).astype(kind)


def setup_inputs(seed: int = 0, part: int = 0) -> dict:
    key_of = jax.random.split(jax.random.key(seed), 6)
    own_keys = jax.random.split(jax.random.fold_in(key_of[5], part), 6)
    return {
        "query_rows": draw_query_rows(jax.random.fold_in(jax.random.fold_in(key_of[5], part), 71), part),
        "key_rows": draw_key_rows(jax.random.fold_in(jax.random.fold_in(key_of[5], part), 71), part),
        "value_rows": draw_value_rows(jax.random.fold_in(jax.random.fold_in(key_of[5], part), 71), part),
        "block_list": draw_block_list(jax.random.fold_in(jax.random.fold_in(key_of[5], part), 71), part),
        "out_weight": gaussian(key_of[4], (HEADS * HD, D), 0.7, 4.0, ((0, 16),)),
    }


def reference(query_rows, key_rows, value_rows, block_list, out_weight):
    features = HEADS * HD
    scale = HD ** -0.5
    queries_tiled = query_rows.reshape(TILES, TILE, HEADS, HD)
    keys_tiled = key_rows.reshape(TILES, TILE, HEADS, HD)
    values_tiled = value_rows.reshape(TILES, TILE, HEADS, HD)

    def one_tile(index):
        listed = block_list[index]
        safe = jnp.maximum(listed, 0).astype(jnp.int32)
        keys_here = keys_tiled[safe].reshape(NB * TILE, HEADS, HD).astype(jnp.float32)
        values_here = values_tiled[safe].reshape(NB * TILE, HEADS, HD).astype(jnp.float32)
        live = jnp.repeat(listed >= 0, TILE)
        queries_here = queries_tiled[index].astype(jnp.float32)
        scores = jnp.einsum("qhd,khd->hqk", queries_here, keys_here) * scale
        scores = jnp.where(live[None, None, :], scores, -jnp.inf)
        peak = jnp.max(scores, axis=-1, keepdims=True)
        weights = jnp.exp(scores - peak)
        totals = jnp.sum(weights, axis=-1, keepdims=True)
        probs = lax.optimization_barrier(weights.astype(jnp.bfloat16))
        mixed = jnp.einsum("hqk,khd->qhd", probs.astype(jnp.float32), values_here)
        mixed = mixed / jnp.transpose(totals, (1, 0, 2))
        return mixed.astype(jnp.bfloat16).reshape(TILE, features)

    attention = lax.map(one_tile, jnp.arange(TILES, dtype=jnp.int32)).reshape(TILES * TILE, features)
    return jnp.dot(attention, out_weight, preferred_element_type=jnp.float32).astype(jnp.bfloat16)
```

```python
import functools
import math

import jax
import jax.numpy as jnp
from jax import lax
from jax.experimental import pallas as pl
from jax.experimental.pallas import tpu as pltpu
from jax.sharding import PartitionSpec as P

HD = 128
FRAMES = 2
GRID_COLS = 8
EXTRA = 16
PIECES = 3
LOG2E = math.log2(math.e)
VMEM_BYTES = 48 * 1024 * 1024


def swap_bit(value, bit):
    count = lax.axis_size("seq")
    return lax.ppermute(value, "seq", [(s, s ^ bit) for s in range(count)])


def swap_group(value, groups):
    return lax.ppermute(value, "group", [(s, s ^ 1) for s in range(groups)])


def column_shift(value, steps):
    count = lax.axis_size("seq")
    pairs = [(s, s + steps) for s in range(count) if 0 <= s % GRID_COLS + steps < GRID_COLS]
    return lax.ppermute(value, "seq", pairs)


def row_pairs(parity):
    count = lax.axis_size("seq")
    rows = count // GRID_COLS
    pairs = []
    for s in range(count):
        row = s // GRID_COLS
        other = row + 1 if row % 2 == parity else row - 1
        if 0 <= other < rows:
            pairs.append((s, s + (other - row) * GRID_COLS))
    return pairs


def attend_kernel(rows, per_block, bias_ref, q_ref, k0, ka, kb, v0, va, vb, out_ref):
    factor = HD ** (-0.5) * LOG2E
    tile = rows // FRAMES
    nt = (((1,), (1,)), ((), ()))
    lse = jnp.zeros((rows, HD), jnp.float32)
    lane = lax.broadcasted_iota(jnp.int32, (rows, HD), 1)
    for head in range(per_block):
        cols = slice(head * HD, (head + 1) * HD)
        keys = [k0[:, cols], ka[0, :, cols], kb[0, :, cols]]
        values = [v0[:, cols], va[0, :, cols], vb[0, :, cols]]
        parts = []
        for frame in range(FRAMES):
            here = slice(frame * tile, (frame + 1) * tile)
            q = q_ref[here, cols]
            bias = bias_ref[frame : frame + 1, :].astype(jnp.float32)
            scores = [
                lax.dot_general(q, key, nt, preferred_element_type=jnp.float32)
                + bias[:, i * rows : (i + 1) * rows]
                for i, key in enumerate(keys)
            ]
            peak = functools.reduce(jnp.maximum, scores)
            peak = jnp.max(peak, axis=1, keepdims=True)
            weights = [jnp.exp2((s - peak) * factor) for s in scores]
            total = jnp.sum(functools.reduce(jnp.add, weights), axis=1, keepdims=True)
            mixed = functools.reduce(
                jnp.add,
                [
                    jnp.dot(w.astype(jnp.bfloat16), v, preferred_element_type=jnp.float32)
                    for w, v in zip(weights, values)
                ],
            )
            out_ref[here, cols] = (mixed / total).astype(out_ref.dtype)
            parts.append(peak * factor + jnp.log2(total))
        lse = jnp.where(lane == head, jnp.concatenate(parts, axis=0), lse)
    turned = jnp.transpose(lse)
    stats = []
    for head in range(per_block):
        rest = turned[head : head + 1, :]
        for _ in range(PIECES):
            piece = rest.astype(out_ref.dtype)
            stats.append(piece.astype(jnp.float32))
            rest = rest - stats[-1]
    stats.append(jnp.zeros((EXTRA - len(stats), rows), jnp.float32))
    out_ref[rows:, :] = jnp.concatenate(stats, axis=0).astype(out_ref.dtype)


def attend(bias, q, q_first, heads, keys, values, kv_up, kv_down, first, kind):
    rows = keys.shape[0]
    per_block = rows // HD
    width = per_block * HD
    lo, q_lo = first * HD // width, q_first * HD // width
    here = pl.BlockSpec((rows, width), lambda i: (0, lo + i))
    key_spec = pl.BlockSpec((1, rows, width), lambda i: (0, 0, lo + i))
    value_spec = pl.BlockSpec((1, rows, width), lambda i: (1, 0, lo + i))
    span = 3 * rows
    return pl.pallas_call(
        functools.partial(attend_kernel, rows, per_block),
        grid=(heads // per_block,),
        in_specs=[
            pl.BlockSpec(bias.shape, lambda i: (0, 0)),
            pl.BlockSpec((rows, width), lambda i: (0, q_lo + i)),
            here,
            key_spec,
            key_spec,
            here,
            value_spec,
            value_spec,
        ],
        out_specs=pl.BlockSpec((rows + EXTRA, width), lambda i: (0, i)),
        out_shape=jax.ShapeDtypeStruct((rows + EXTRA, heads * HD), kind),
        compiler_params=pltpu.CompilerParams(vmem_limit_bytes=VMEM_BYTES),
        cost_estimate=pl.CostEstimate(
            flops=4 * heads * rows * span * HD,
            bytes_accessed=heads * HD * 2 * (2 * span + 2 * rows),
            transcendentals=heads * rows * span,
        ),
    )(bias, q, keys, kv_up, kv_down, values, kv_up, kv_down)


def project_kernel(rows, plan, chunk_counts, *refs):
    sources = len(plan)
    weights = refs[:sources]
    partner_ref = refs[sources]
    cursor = sources + 1
    own = refs[cursor]
    cursor += 1
    others = []
    for count in chunk_counts:
        others.append(refs[cursor : cursor + count])
        cursor += count
    out_ref, held, attention, sems = refs[cursor:]
    copies = []
    for source, moves in zip(weights, plan):
        for from_row, count, place in moves:
            into = pl.multiple_of(place(), 16)
            copy = pltpu.make_async_copy(
                source.at[pl.ds(from_row, count), :],
                held.at[pl.ds(into, count), :],
                sems.at[len(copies)],
            )
            copy.start()
            copies.append(copy)
    per_block = rows // HD
    width = per_block * HD
    features = own.shape[1]
    for block in range(features // width):
        cols = slice(block * width, (block + 1) * width)
        tiles = [own[:, cols].astype(jnp.float32)]
        for number, chunks in enumerate(others):
            chunk_width = chunks[0].shape[1]
            index, offset = divmod(block * width, chunk_width)
            tiles.append(chunks[index][:, offset : offset + width].astype(jnp.float32))
        shares = []
        for head in range(per_block):
            lses = []
            for number, t in enumerate(tiles):
                row = rows + PIECES * head
                lse = functools.reduce(
                    jnp.add, [t[row + i : row + i + 1, :] for i in range(PIECES)]
                )
                if number:
                    lse = jnp.where(partner_ref[number - 1] == 1, lse, -jnp.inf)
                lses.append(lse)
            top = functools.reduce(jnp.maximum, lses)
            raw = [jnp.exp2(lse - top) for lse in lses]
            total = functools.reduce(jnp.add, raw)
            shares.extend(r / total for r in raw)
        shares.append(jnp.zeros((HD - len(shares), rows), jnp.float32))
        turned = jnp.transpose(jnp.concatenate(shares, axis=0))
        for head in range(per_block):
            inner = slice(head * HD, (head + 1) * HD)
            mixed = functools.reduce(
                jnp.add,
                [
                    t[:rows, inner] * turned[:, head * len(tiles) + n : head * len(tiles) + n + 1]
                    for n, t in enumerate(tiles)
                ],
            )
            start = block * width + head * HD
            attention[:, start : start + HD] = mixed.astype(jnp.bfloat16)
    for copy in copies:
        copy.wait()
    columns = out_ref.shape[1]
    step = math.gcd(columns, 512)

    @pl.loop(0, columns // step)
    def _(i):
        there = pl.ds(pl.multiple_of(i * step, step), step)
        out_ref[:, there] = jnp.dot(
            attention[...], held[:, there], preferred_element_type=jnp.float32
        ).astype(out_ref.dtype)


def project(pieces, partner, own, others):
    arrays = [array for array, _ in pieces]
    plan = [moves for _, moves in pieces]
    rows, features = own.shape[0] - EXTRA, own.shape[1]
    columns = arrays[0].shape[1]
    flat = [chunk for chunks in others for chunk in chunks]
    vmem = pl.BlockSpec(memory_space=pltpu.VMEM)
    return pl.pallas_call(
        functools.partial(project_kernel, rows, plan, [len(c) for c in others]),
        in_specs=[pl.BlockSpec(memory_space=pl.ANY)] * len(arrays)
        + [pl.BlockSpec(memory_space=pltpu.SMEM)]
        + [vmem] * (1 + len(flat)),
        out_specs=vmem,
        out_shape=jax.ShapeDtypeStruct((rows, columns), jnp.bfloat16),
        scratch_shapes=[
            pltpu.VMEM((features, columns), jnp.bfloat16),
            pltpu.VMEM((rows, features), jnp.bfloat16),
            pltpu.SemaphoreType.DMA((sum(len(m) for m in plan),)),
        ],
        compiler_params=pltpu.CompilerParams(vmem_limit_bytes=VMEM_BYTES),
        cost_estimate=pl.CostEstimate(
            flops=2 * rows * features * columns,
            bytes_accessed=2 * features * columns,
            transcendentals=0,
        ),
    )(*arrays, partner, own, *flat)


def gather_weight(out_weight, groups, devices):
    shard = out_weight.shape[0]
    if devices != 16 or groups != 2 or shard % 32:
        whole = lax.all_gather(out_weight, "seq", axis=0, tiled=True)
        return [(whole, [(0, whole.shape[0], lambda: 0)])]
    half = shard // 2

    def full(*bits):
        def at(bit):
            return lambda: (lax.axis_index("seq") ^ bit) * shard

        return [(i * shard, shard, at(bit)) for i, bit in enumerate(bits)]

    def halves(*bits):
        def at(bit, turn):
            return lambda: (lax.axis_index("seq") ^ bit) * shard + (
                lax.axis_index("group") ^ turn
            ) * half

        return [(i * half, half, at(bit, turn)) for i, (bit, turn) in enumerate(bits)]

    mine = lax.dynamic_slice_in_dim(out_weight, lax.axis_index("group") * half, half, 0)
    c0 = swap_bit(mine, 8)
    wz = swap_bit(out_weight, 4)
    cz = swap_bit(c0, 4)
    near = jnp.concatenate([out_weight, wz], axis=0)
    wy = swap_bit(near, 2)
    far = jnp.concatenate([c0, cz], axis=0)
    cy = swap_bit(far, 2)
    quad = jnp.concatenate([near, wy], axis=0)
    wc = swap_bit(quad, 1)
    four = jnp.concatenate([far, cy], axis=0)
    cx = swap_group(four, groups)
    eight = jnp.concatenate([four, cx], axis=0)
    cc = swap_bit(eight, 1)
    return [
        (quad, full(0, 4, 2, 6)),
        (wc, full(1, 5, 3, 7)),
        (eight, halves((8, 0), (12, 0), (10, 0), (14, 0), (8, 1), (12, 1), (10, 1), (14, 1))),
        (cc, halves((9, 0), (13, 0), (11, 0), (15, 0), (9, 1), (13, 1), (11, 1), (15, 1))),
    ]


def body(groups, query_rows, key_rows, value_rows, block_list, out_weight):
    rows, features = query_rows.shape
    heads = features // HD
    devices = lax.axis_size("seq")
    grid_rows = devices // GRID_COLS
    position = lax.axis_index("seq")
    row = position // GRID_COLS
    tile = rows // FRAMES
    chunk_heads = heads // 2
    chunk = chunk_heads * HD

    def bias_for(there):
        centre = there * GRID_COLS + position % GRID_COLS
        places = centre + jnp.array([0, -1, 1], jnp.int32)
        ids = (places[:, None] * FRAMES + jnp.arange(FRAMES, dtype=jnp.int32)[None, :]).reshape(-1)
        ids = jnp.where(ids >= 0, ids, -2)
        member = jnp.any(block_list[:, :, None] == ids[None, None, :], axis=1)
        return jnp.repeat(jnp.where(member, 0.0, -jnp.inf), tile, axis=1)

    kv = jnp.stack([key_rows, value_rows])
    pieces = gather_weight(out_weight, groups, devices)
    phases = [parity for parity in range(2) if parity + 1 < grid_rows]
    sent = []
    for parity in phases:
        there = jnp.where(row % 2 == parity, row + 1, row - 1)
        bias = bias_for(there).reshape(-1).astype(jnp.bfloat16)
        bias = jnp.pad(bias, (0, EXTRA * chunk - bias.shape[0])).reshape(EXTRA, chunk)
        pairs = row_pairs(parity)
        first = jnp.concatenate([query_rows[:, :chunk], bias], axis=0)
        sent.append(
            [
                lax.ppermute(first, "seq", pairs),
                lax.ppermute(query_rows[:, chunk:], "seq", pairs),
            ]
        )
    kv_up = column_shift(kv, 1)
    kv_down = column_shift(kv, -1)
    common = (key_rows, value_rows, kv_up, kv_down)
    others = []
    for parity, asked in zip(phases, sent):
        bias = asked[0][rows:, :].reshape(-1)[: FRAMES * 3 * rows].reshape(FRAMES, 3 * rows)
        pairs = row_pairs(parity)
        back = []
        for number, q in enumerate(asked):
            part = attend(bias, q, 0, chunk_heads, *common, number * chunk_heads, jnp.bfloat16)
            back.append(lax.ppermute(part, "seq", pairs))
        others.append(back)
    own = attend(bias_for(row), query_rows, 0, heads, *common, 0, jnp.float32)
    partner = jnp.stack(
        [
            jnp.where(row % 2 == parity, row + 1 < grid_rows, row > 0).astype(jnp.int32)
            for parity in phases
        ]
        or [jnp.int32(0)]
    )
    return project(pieces, partner, own, others)


def solution(mesh):
    placed = (
        P(("group", "seq"), None),
        P(("group", "seq"), None),
        P(("group", "seq"), None),
        P(("group", "seq"), None),
        P("seq", None),
    )
    return jax.shard_map(
        functools.partial(body, mesh.shape["group"]),
        mesh=mesh,
        in_specs=placed,
        out_specs=P(("group", "seq"), None),
        check_vma=False,
    )
```

```python
import functools
import math

import jax
import jax.numpy as jnp
from jax import lax
from jax.experimental import pallas as pl
from jax.experimental.pallas import tpu as pltpu
from jax.sharding import PartitionSpec as P

HD = 128
FRAMES = 2
GRID_COLS = 8
EXTRA = 16
PIECES = 3
LOG2E = math.log2(math.e)
VMEM_BYTES = 48 * 1024 * 1024
WEIGHTY = 10**12


def swap_bit(value, bit):
    count = lax.axis_size("seq")
    return lax.ppermute(value, "seq", [(s, s ^ bit) for s in range(count)])


def swap_group(value, groups):
    return lax.ppermute(value, "group", [(s, s ^ 1) for s in range(groups)])


def column_shift(value, steps):
    count = lax.axis_size("seq")
    pairs = [(s, s + steps) for s in range(count) if 0 <= s % GRID_COLS + steps < GRID_COLS]
    return lax.ppermute(value, "seq", pairs)


def row_pairs(parity):
    count = lax.axis_size("seq")
    rows = count // GRID_COLS
    pairs = []
    for s in range(count):
        row = s // GRID_COLS
        other = row + 1 if row % 2 == parity else row - 1
        if 0 <= other < rows:
            pairs.append((s, s + (other - row) * GRID_COLS))
    return pairs


def attend_kernel(rows, per_block, bias_ref, q_ref, k0, ka, kb, v0, va, vb, out_ref):
    factor = HD ** (-0.5) * LOG2E
    tile = rows // FRAMES
    nt = (((1,), (1,)), ((), ()))
    lse = jnp.zeros((rows, HD), jnp.float32)
    lane = lax.broadcasted_iota(jnp.int32, (rows, HD), 1)
    for head in range(per_block):
        cols = slice(head * HD, (head + 1) * HD)
        keys = [k0[:, cols], ka[0, :, cols], kb[0, :, cols]]
        values = [v0[:, cols], va[0, :, cols], vb[0, :, cols]]
        parts = []
        for frame in range(FRAMES):
            here = slice(frame * tile, (frame + 1) * tile)
            q = q_ref[here, cols]
            bias = bias_ref[frame : frame + 1, :].astype(jnp.float32)
            scores = [
                lax.dot_general(q, key, nt, preferred_element_type=jnp.float32)
                + bias[:, i * rows : (i + 1) * rows]
                for i, key in enumerate(keys)
            ]
            peak = functools.reduce(jnp.maximum, scores)
            peak = jnp.max(peak, axis=1, keepdims=True)
            weights = [jnp.exp2((s - peak) * factor) for s in scores]
            total = jnp.sum(functools.reduce(jnp.add, weights), axis=1, keepdims=True)
            mixed = functools.reduce(
                jnp.add,
                [
                    jnp.dot(w.astype(jnp.bfloat16), v, preferred_element_type=jnp.float32)
                    for w, v in zip(weights, values)
                ],
            )
            out_ref[here, cols] = (mixed / total).astype(out_ref.dtype)
            parts.append(peak * factor + jnp.log2(total))
        lse = jnp.where(lane == head, jnp.concatenate(parts, axis=0), lse)
    turned = jnp.transpose(lse)
    stats = []
    for head in range(per_block):
        rest = turned[head : head + 1, :]
        for _ in range(PIECES):
            piece = rest.astype(out_ref.dtype)
            stats.append(piece.astype(jnp.float32))
            rest = rest - stats[-1]
    stats.append(jnp.zeros((EXTRA - len(stats), rows), jnp.float32))
    out_ref[rows:, :] = jnp.concatenate(stats, axis=0).astype(out_ref.dtype)


def attend(bias, q, q_first, heads, keys, values, kv_up, kv_down, first, kind, cost=WEIGHTY):
    rows = keys.shape[0]
    per_block = rows // HD
    width = per_block * HD
    lo, q_lo = first * HD // width, q_first * HD // width
    here = pl.BlockSpec((rows, width), lambda i: (0, lo + i))
    key_spec = pl.BlockSpec((1, rows, width), lambda i: (0, 0, lo + i))
    value_spec = pl.BlockSpec((1, rows, width), lambda i: (1, 0, lo + i))
    span = 3 * rows
    return pl.pallas_call(
        functools.partial(attend_kernel, rows, per_block),
        grid=(heads // per_block,),
        in_specs=[
            pl.BlockSpec(bias.shape, lambda i: (0, 0)),
            pl.BlockSpec((rows, width), lambda i: (0, q_lo + i)),
            here,
            key_spec,
            key_spec,
            here,
            value_spec,
            value_spec,
        ],
        out_specs=pl.BlockSpec((rows + EXTRA, width), lambda i: (0, i)),
        out_shape=jax.ShapeDtypeStruct((rows + EXTRA, heads * HD), kind),
        compiler_params=pltpu.CompilerParams(vmem_limit_bytes=VMEM_BYTES),
        cost_estimate=pl.CostEstimate(
            flops=cost, bytes_accessed=0, transcendentals=0
        ),
    )(bias, q, keys, kv_up, kv_down, values, kv_up, kv_down)


def merge_kernel(rows, chunk_counts, partner_ref, *refs):
    parts, cursor = [], 0
    for count in chunk_counts:
        parts.append(refs[cursor : cursor + count])
        cursor += count
    attention = refs[cursor]
    per_block = rows // HD
    width = per_block * HD
    for block in range(attention.shape[1] // width):
        tiles = []
        for chunks in parts:
            offset = block * width
            for chunk in chunks:
                if offset < chunk.shape[1]:
                    break
                offset -= chunk.shape[1]
            tiles.append(chunk[:, offset : offset + width].astype(jnp.float32))
        shares = []
        for head in range(per_block):
            lses = []
            for number, t in enumerate(tiles):
                row = rows + PIECES * head
                lse = functools.reduce(
                    jnp.add, [t[row + i : row + i + 1, :] for i in range(PIECES)]
                )
                if number:
                    lse = jnp.where(partner_ref[number - 1] == 1, lse, -jnp.inf)
                lses.append(lse)
            top = functools.reduce(jnp.maximum, lses)
            raw = [jnp.exp2(lse - top) for lse in lses]
            total = functools.reduce(jnp.add, raw)
            shares.extend(r / total for r in raw)
        shares.append(jnp.zeros((HD - len(shares), rows), jnp.float32))
        turned = jnp.transpose(jnp.concatenate(shares, axis=0))
        for head in range(per_block):
            inner = slice(head * HD, (head + 1) * HD)
            mixed = functools.reduce(
                jnp.add,
                [
                    t[:rows, inner] * turned[:, head * len(tiles) + n : head * len(tiles) + n + 1]
                    for n, t in enumerate(tiles)
                ],
            )
            start = block * width + head * HD
            attention[:, start : start + HD] = mixed.astype(jnp.bfloat16)


def merge(partner, parts):
    flat = [chunk for chunks in parts for chunk in chunks]
    rows = flat[0].shape[0] - EXTRA
    features = sum(chunk.shape[1] for chunk in parts[0])
    vmem = pl.BlockSpec(memory_space=pltpu.VMEM)
    return pl.pallas_call(
        functools.partial(merge_kernel, rows, [len(c) for c in parts]),
        in_specs=[pl.BlockSpec(memory_space=pltpu.SMEM)] + [vmem] * len(flat),
        out_specs=vmem,
        out_shape=jax.ShapeDtypeStruct((rows, features), jnp.bfloat16),
        compiler_params=pltpu.CompilerParams(vmem_limit_bytes=VMEM_BYTES),
        cost_estimate=pl.CostEstimate(flops=WEIGHTY, bytes_accessed=0, transcendentals=0),
    )(partner, *flat)


def project_kernel(plan, *refs):
    weights = refs[: len(plan)]
    attention, out_ref, held, sems = refs[len(plan) :]
    copies = []
    for source, moves in zip(weights, plan):
        for from_row, count, place in moves:
            into = pl.multiple_of(place(), 16)
            copy = pltpu.make_async_copy(
                source.at[pl.ds(from_row, count), :],
                held.at[pl.ds(into, count), :],
                sems.at[len(copies)],
            )
            copy.start()
            copies.append(copy)
    for copy in copies:
        copy.wait()
    columns = out_ref.shape[1]
    step = math.gcd(columns, 512)

    @pl.loop(0, columns // step)
    def _(i):
        there = pl.ds(pl.multiple_of(i * step, step), step)
        out_ref[:, there] = jnp.dot(
            attention[...], held[:, there], preferred_element_type=jnp.float32
        ).astype(out_ref.dtype)


def project(pieces, attention):
    arrays = [array for array, _ in pieces]
    plan = [moves for _, moves in pieces]
    rows, features = attention.shape
    columns = arrays[0].shape[1]
    vmem = pl.BlockSpec(memory_space=pltpu.VMEM)
    return pl.pallas_call(
        functools.partial(project_kernel, plan),
        in_specs=[pl.BlockSpec(memory_space=pl.ANY)] * len(arrays) + [vmem],
        out_specs=vmem,
        out_shape=jax.ShapeDtypeStruct((rows, columns), jnp.bfloat16),
        scratch_shapes=[
            pltpu.VMEM((features, columns), jnp.bfloat16),
            pltpu.SemaphoreType.DMA((sum(len(m) for m in plan),)),
        ],
        compiler_params=pltpu.CompilerParams(vmem_limit_bytes=VMEM_BYTES),
    )(*arrays, attention)


def after(value, *done):
    return lax.optimization_barrier((value, *done))[0]


class Cube:
    def __init__(self, out_weight):
        self.near = out_weight
        self.shard = out_weight.shape[0]
        self.half = self.shard // 2

    def cross(self):
        first = lax.axis_index("group") * self.half
        self.c0 = swap_bit(lax.dynamic_slice_in_dim(self.near, first, self.half, 0), 8)

    def full(self, *bits):
        def at(bit):
            return lambda: (lax.axis_index("seq") ^ bit) * self.shard

        return [(i * self.shard, self.shard, at(bit)) for i, bit in enumerate(bits)]

    def halves(self, *bits):
        def at(bit, turn):
            return lambda: (lax.axis_index("seq") ^ bit) * self.shard + (
                lax.axis_index("group") ^ turn
            ) * self.half

        return [(i * self.half, self.half, at(bit, turn)) for i, (bit, turn) in enumerate(bits)]

    def pieces(self):
        return [
            (self.quad, self.full(0, 4, 2, 6)),
            (self.wc, self.full(1, 5, 3, 7)),
            (self.eight, self.halves(*[(b, t) for t in (0, 1) for b in (8, 12, 10, 14)])),
            (self.cc, self.halves(*[(b, t) for t in (0, 1) for b in (9, 13, 11, 15)])),
        ]


def join(*arrays):
    return jnp.concatenate(arrays, axis=0)


def body(groups, query_rows, key_rows, value_rows, block_list, out_weight):
    rows, features = query_rows.shape
    heads = features // HD
    devices = lax.axis_size("seq")
    grid_rows = devices // GRID_COLS
    position = lax.axis_index("seq")
    row = position // GRID_COLS
    tile = rows // FRAMES
    chunk_heads = heads // 2
    chunk = chunk_heads * HD

    def bias_for(there):
        centre = there * GRID_COLS + position % GRID_COLS
        places = centre + jnp.array([0, -1, 1], jnp.int32)
        ids = (places[:, None] * FRAMES + jnp.arange(FRAMES, dtype=jnp.int32)[None, :]).reshape(-1)
        ids = jnp.where(ids >= 0, ids, -2)
        member = jnp.any(block_list[:, :, None] == ids[None, None, :], axis=1)
        return jnp.repeat(jnp.where(member, 0.0, -jnp.inf), tile, axis=1)

    cube = None
    if devices == 16 and groups == 2 and out_weight.shape[0] % 32 == 0:
        cube = Cube(out_weight)
        cube.cross()
    kv = jnp.stack([key_rows, value_rows])
    kv_up = column_shift(kv, 1)
    kv_down = column_shift(kv, -1)
    if cube:
        wz = swap_bit(out_weight, 4)
    phases = [parity for parity in range(2) if parity + 1 < grid_rows]
    sent = []
    for parity in phases:
        there = jnp.where(row % 2 == parity, row + 1, row - 1)
        bias = bias_for(there).reshape(-1).astype(jnp.bfloat16)
        bias = jnp.pad(bias, (0, EXTRA * chunk - bias.shape[0])).reshape(EXTRA, chunk)
        pairs = row_pairs(parity)
        first = lax.ppermute(join(query_rows[:, :chunk], bias), "seq", pairs)
        second = query_rows[:, chunk:]
        if cube:
            cz = swap_bit(cube.c0, 4)
            second = after(second, wz)
        sent.append([first, lax.ppermute(second, "seq", pairs)])
    if cube:
        far = join(cube.c0, cz)
        cy = swap_bit(far, 2)
        sent[0][0] = after(sent[0][0], far)
    common = (key_rows, value_rows, kv_up, kv_down)
    others = []
    for parity, asked in zip(phases, sent):
        bias = asked[0][rows:, :].reshape(-1)[: FRAMES * 3 * rows].reshape(FRAMES, 3 * rows)
        back = []
        for number, q in enumerate(asked):
            if number:
                q = after(q, part, near, four) if cube else after(q, part)
            part = attend(bias, q, 0, chunk_heads, *common, number * chunk_heads, jnp.bfloat16)
            if cube and not number:
                four = join(far, after(cy, part))
                cx = swap_group(four, groups)
                near = join(out_weight, after(wz, part))
                wy = swap_bit(near, 2)
            back.append(lax.ppermute(part, "seq", row_pairs(parity)))
            last = part
        others.append(back)
    own_bias = bias_for(row)
    early = heads - rows // HD
    awaited = [others[0][0]] if phases else []
    if cube:
        awaited += [cx, wy]
    q = after(query_rows, last) if phases else query_rows
    own = [attend(own_bias, q, 0, early, *common, 0, jnp.float32, 0)]
    q = after(query_rows, *awaited)
    own.append(attend(own_bias, q, early, heads - early, *common, early, jnp.float32))
    partner = jnp.stack(
        [
            jnp.where(row % 2 == parity, row + 1 < grid_rows, row > 0).astype(jnp.int32)
            for parity in phases
        ]
        or [jnp.int32(0)]
    )
    attention = merge(partner, [own] + others)
    if cube:
        cube.quad = join(near, after(wy, own[0]))
        cube.wc = after(swap_bit(cube.quad, 1), attention)
        cube.eight = join(four, after(cx, own[0]))
        cube.cc = after(swap_bit(cube.eight, 1), attention)
        pieces = cube.pieces()
    else:
        whole = lax.all_gather(out_weight, "seq", axis=0, tiled=True)
        pieces = [(whole, [(0, whole.shape[0], lambda: 0)])]
    return project(pieces, attention)


def solution(mesh):
    placed = (
        P(("group", "seq"), None),
        P(("group", "seq"), None),
        P(("group", "seq"), None),
        P(("group", "seq"), None),
        P("seq", None),
    )
    return jax.shard_map(
        functools.partial(body, mesh.shape["group"]),
        mesh=mesh,
        in_specs=placed,
        out_specs=P(("group", "seq"), None),
        check_vma=False,
    )
```

```python
import functools
import math

import jax
import jax.numpy as jnp
from jax import lax
from jax.experimental import pallas as pl
from jax.experimental.pallas import tpu as pltpu
from jax.sharding import PartitionSpec as P

HD = 128
FRAMES = 2
GRID_COLS = 8
EXTRA = 16
PIECES = 3
LOG2E = math.log2(math.e)
VMEM_BYTES = 48 * 1024 * 1024
WEIGHTY = 10**12


def swap_bit(value, bit):
    count = lax.axis_size("seq")
    return lax.ppermute(value, "seq", [(s, s ^ bit) for s in range(count)])


def swap_group(value, groups):
    return lax.ppermute(value, "group", [(s, s ^ 1) for s in range(groups)])


def column_shift(value, steps):
    count = lax.axis_size("seq")
    pairs = [(s, s + steps) for s in range(count) if 0 <= s % GRID_COLS + steps < GRID_COLS]
    return lax.ppermute(value, "seq", pairs)


def row_pairs(parity):
    count = lax.axis_size("seq")
    rows = count // GRID_COLS
    pairs = []
    for s in range(count):
        row = s // GRID_COLS
        other = row + 1 if row % 2 == parity else row - 1
        if 0 <= other < rows:
            pairs.append((s, s + (other - row) * GRID_COLS))
    return pairs


def join_kernel(count, *refs):
    sources, (out_ref, sems) = refs[:count], refs[count:]
    copies, first = [], 0
    for i, source in enumerate(sources):
        size = source.shape[0]
        copy = pltpu.make_async_copy(source, out_ref.at[pl.ds(first, size), :], sems.at[i])
        copy.start()
        copies.append(copy)
        first += size
    for copy in copies:
        copy.wait()


def join(*arrays):
    rows = sum(array.shape[0] for array in arrays)
    hbm = pl.BlockSpec(memory_space=pltpu.HBM)
    return pl.pallas_call(
        functools.partial(join_kernel, len(arrays)),
        in_specs=[hbm] * len(arrays),
        out_specs=hbm,
        out_shape=jax.ShapeDtypeStruct((rows, arrays[0].shape[1]), arrays[0].dtype),
        scratch_shapes=[pltpu.SemaphoreType.DMA((len(arrays),))],
        cost_estimate=pl.CostEstimate(flops=0, bytes_accessed=0, transcendentals=0),
    )(*arrays)


def attend_kernel(rows, per_block, list_ref, q_ref, k0, ka, kb, v0, va, vb, out_ref):
    factor = HD ** (-0.5) * LOG2E
    tile = rows // FRAMES
    position = lax.axis_index("seq")
    lists = list_ref[...].astype(jnp.float32)
    masks = []
    for step in (0, -1, 1):
        bits = []
        for frame in range(FRAMES):
            tile_id = (position + step) * FRAMES + frame
            tile_id = jnp.where(tile_id >= 0, tile_id, -2).astype(jnp.float32)
            hit = jnp.max(jnp.where(lists == tile_id, 0.0, -jnp.inf), axis=1, keepdims=True)
            bits.append(jnp.broadcast_to(hit, (hit.shape[0], tile)))
        masks.append(jnp.concatenate(bits, axis=1))
    nt = (((1,), (1,)), ((), ()))
    lse = jnp.zeros((rows, HD), jnp.float32)
    lane = lax.broadcasted_iota(jnp.int32, (rows, HD), 1)
    for head in range(per_block):
        cols = slice(head * HD, (head + 1) * HD)
        keys = [k0[:, cols], ka[0, :, cols], kb[0, :, cols]]
        values = [v0[:, cols], va[0, :, cols], vb[0, :, cols]]
        parts = []
        for frame in range(FRAMES):
            here = slice(frame * tile, (frame + 1) * tile)
            q = q_ref[here, cols]
            scores = [
                lax.dot_general(q, key, nt, preferred_element_type=jnp.float32)
                + mask[frame : frame + 1, :]
                for key, mask in zip(keys, masks)
            ]
            peak = functools.reduce(jnp.maximum, scores)
            peak = jnp.max(peak, axis=1, keepdims=True)
            weights = [jnp.exp2((s - peak) * factor) for s in scores]
            total = jnp.sum(functools.reduce(jnp.add, weights), axis=1, keepdims=True)
            mixed = functools.reduce(
                jnp.add,
                [
                    jnp.dot(w.astype(jnp.bfloat16), v, preferred_element_type=jnp.float32)
                    for w, v in zip(weights, values)
                ],
            )
            out_ref[here, cols] = (mixed / total).astype(out_ref.dtype)
            parts.append(peak * factor + jnp.log2(total))
        lse = jnp.where(lane == head, jnp.concatenate(parts, axis=0), lse)
    turned = jnp.transpose(lse)
    stats = []
    for head in range(per_block):
        rest = turned[head : head + 1, :]
        for _ in range(PIECES):
            piece = rest.astype(out_ref.dtype)
            stats.append(piece.astype(jnp.float32))
            rest = rest - stats[-1]
    stats.append(jnp.zeros((EXTRA - len(stats), rows), jnp.float32))
    out_ref[rows:, :] = jnp.concatenate(stats, axis=0).astype(out_ref.dtype)


def attend(lists, q, q_first, heads, keys, values, kv_up, kv_down, first, kind, cost=WEIGHTY):
    rows = keys.shape[0]
    per_block = rows // HD
    width = per_block * HD
    lo, q_lo = first * HD // width, q_first * HD // width
    here = pl.BlockSpec((rows, width), lambda i: (0, lo + i))
    key_spec = pl.BlockSpec((1, rows, width), lambda i: (0, 0, lo + i))
    value_spec = pl.BlockSpec((1, rows, width), lambda i: (1, 0, lo + i))
    span = 3 * rows
    return pl.pallas_call(
        functools.partial(attend_kernel, rows, per_block),
        grid=(heads // per_block,),
        in_specs=[
            pl.BlockSpec((EXTRA, HD), lambda i: (lists.shape[0] // EXTRA - 1, 0)),
            pl.BlockSpec((rows, width), lambda i: (0, q_lo + i)),
            here,
            key_spec,
            key_spec,
            here,
            value_spec,
            value_spec,
        ],
        out_specs=pl.BlockSpec((rows + EXTRA, width), lambda i: (0, i)),
        out_shape=jax.ShapeDtypeStruct((rows + EXTRA, heads * HD), kind),
        compiler_params=pltpu.CompilerParams(vmem_limit_bytes=VMEM_BYTES),
        cost_estimate=pl.CostEstimate(
            flops=cost, bytes_accessed=0, transcendentals=0
        ),
    )(lists, q, keys, kv_up, kv_down, values, kv_up, kv_down)


def merge_kernel(rows, chunk_counts, partner_ref, *refs):
    parts, cursor = [], 0
    for count in chunk_counts:
        parts.append(refs[cursor : cursor + count])
        cursor += count
    attention = refs[cursor]
    per_block = rows // HD
    width = per_block * HD
    for block in range(attention.shape[1] // width):
        tiles = []
        for chunks in parts:
            offset = block * width
            for chunk in chunks:
                if offset < chunk.shape[1]:
                    break
                offset -= chunk.shape[1]
            tiles.append(chunk[:, offset : offset + width].astype(jnp.float32))
        shares = []
        for head in range(per_block):
            lses = []
            for number, t in enumerate(tiles):
                row = rows + PIECES * head
                lse = functools.reduce(
                    jnp.add, [t[row + i : row + i + 1, :] for i in range(PIECES)]
                )
                if number:
                    lse = jnp.where(partner_ref[number - 1] == 1, lse, -jnp.inf)
                lses.append(lse)
            top = functools.reduce(jnp.maximum, lses)
            raw = [jnp.exp2(lse - top) for lse in lses]
            total = functools.reduce(jnp.add, raw)
            shares.extend(r / total for r in raw)
        shares.append(jnp.zeros((HD - len(shares), rows), jnp.float32))
        turned = jnp.transpose(jnp.concatenate(shares, axis=0))
        for head in range(per_block):
            inner = slice(head * HD, (head + 1) * HD)
            mixed = functools.reduce(
                jnp.add,
                [
                    t[:rows, inner] * turned[:, head * len(tiles) + n : head * len(tiles) + n + 1]
                    for n, t in enumerate(tiles)
                ],
            )
            start = block * width + head * HD
            attention[:, start : start + HD] = mixed.astype(jnp.bfloat16)


def merge(partner, parts):
    flat = [chunk for chunks in parts for chunk in chunks]
    rows = flat[0].shape[0] - EXTRA
    features = sum(chunk.shape[1] for chunk in parts[0])
    vmem = pl.BlockSpec(memory_space=pltpu.VMEM)
    return pl.pallas_call(
        functools.partial(merge_kernel, rows, [len(c) for c in parts]),
        in_specs=[pl.BlockSpec(memory_space=pltpu.SMEM)] + [vmem] * len(flat),
        out_specs=vmem,
        out_shape=jax.ShapeDtypeStruct((rows, features), jnp.bfloat16),
        compiler_params=pltpu.CompilerParams(vmem_limit_bytes=VMEM_BYTES),
        cost_estimate=pl.CostEstimate(flops=WEIGHTY, bytes_accessed=0, transcendentals=0),
    )(partner, *flat)


def project_kernel(plan, *refs):
    weights = refs[: len(plan)]
    attention, out_ref, held, sems = refs[len(plan) :]
    copies = []
    for source, moves in zip(weights, plan):
        for from_row, count, place in moves:
            into = pl.multiple_of(place(), 16)
            copy = pltpu.make_async_copy(
                source.at[pl.ds(from_row, count), :],
                held.at[pl.ds(into, count), :],
                sems.at[len(copies)],
            )
            copy.start()
            copies.append(copy)
    for copy in copies:
        copy.wait()
    columns = out_ref.shape[1]
    step = math.gcd(columns, 512)

    @pl.loop(0, columns // step)
    def _(i):
        there = pl.ds(pl.multiple_of(i * step, step), step)
        out_ref[:, there] = jnp.dot(
            attention[...], held[:, there], preferred_element_type=jnp.float32
        ).astype(out_ref.dtype)


def project(pieces, attention):
    arrays = [array for array, _ in pieces]
    plan = [moves for _, moves in pieces]
    rows, features = attention.shape
    columns = arrays[0].shape[1]
    vmem = pl.BlockSpec(memory_space=pltpu.VMEM)
    return pl.pallas_call(
        functools.partial(project_kernel, plan),
        in_specs=[pl.BlockSpec(memory_space=pl.ANY)] * len(arrays) + [vmem],
        out_specs=vmem,
        out_shape=jax.ShapeDtypeStruct((rows, columns), jnp.bfloat16),
        scratch_shapes=[
            pltpu.VMEM((features, columns), jnp.bfloat16),
            pltpu.SemaphoreType.DMA((sum(len(m) for m in plan),)),
        ],
        compiler_params=pltpu.CompilerParams(vmem_limit_bytes=VMEM_BYTES),
    )(*arrays, attention)


def after(value, *done):
    return lax.optimization_barrier((value, *done))[0]


class Cube:
    def __init__(self, out_weight):
        self.near = out_weight
        self.shard = out_weight.shape[0]
        self.half = self.shard // 2

    def cross(self):
        first = lax.axis_index("group") * self.half
        self.c0 = swap_bit(lax.dynamic_slice_in_dim(self.near, first, self.half, 0), 8)

    def full(self, *bits):
        def at(bit):
            return lambda: (lax.axis_index("seq") ^ bit) * self.shard

        return [(i * self.shard, self.shard, at(bit)) for i, bit in enumerate(bits)]

    def halves(self, *bits):
        def at(bit, turn):
            return lambda: (lax.axis_index("seq") ^ bit) * self.shard + (
                lax.axis_index("group") ^ turn
            ) * self.half

        return [(i * self.half, self.half, at(bit, turn)) for i, (bit, turn) in enumerate(bits)]

    def pieces(self, near, wy, four, cx, swapped):
        far = (8, 12, 10, 14)
        return [
            (near, self.full(0, 4)),
            (wy, self.full(2, 6)),
            (four, self.halves(*[(b, 0) for b in far])),
            (cx, self.halves(*[(b, 1) for b in far])),
            (swapped[0], self.full(1, 5)),
            (swapped[1], self.full(3, 7)),
            (swapped[2], self.halves(*[(b ^ 1, 0) for b in far])),
            (swapped[3], self.halves(*[(b ^ 1, 1) for b in far])),
        ]


def body(groups, query_rows, key_rows, value_rows, block_list, out_weight):
    rows, features = query_rows.shape
    heads = features // HD
    devices = lax.axis_size("seq")
    grid_rows = devices // GRID_COLS
    row = lax.axis_index("seq") // GRID_COLS
    chunk_heads = heads // 2
    chunk = chunk_heads * HD
    phases = [parity for parity in range(2) if parity + 1 < grid_rows]
    cube = None
    if devices == 16 and groups == 2 and out_weight.shape[0] % 32 == 0:
        cube = Cube(out_weight)
        cube.cross()
    lists = jnp.pad(
        block_list.astype(jnp.bfloat16),
        ((0, EXTRA - FRAMES), (0, HD - block_list.shape[1])),
        constant_values=-1,
    )
    asking = jnp.concatenate([query_rows[:, :chunk], jnp.tile(lists, (1, chunk_heads))], axis=0)
    kv = join(key_rows, value_rows).reshape(2, rows, features)
    kv_up = column_shift(kv, 1)
    kv_down = column_shift(kv, -1)
    if cube:
        wz = swap_bit(out_weight, 4)
    sent = []
    for parity in phases:
        pairs = row_pairs(parity)
        first = lax.ppermute(asking, "seq", pairs)
        second = query_rows[:, chunk:]
        if cube:
            cz = swap_bit(cube.c0, 4)
            second = after(second, wz, cube.c0)
        sent.append([first, lax.ppermute(second, "seq", pairs)])
    if cube:
        far = join(cube.c0, cz)
        cy = swap_bit(far, 2)
        sent[0][0] = after(sent[0][0], far)
    common = (key_rows, value_rows, kv_up, kv_down)
    others = []
    for parity, asked in zip(phases, sent):
        back = []
        for number, q in enumerate(asked):
            if number:
                q = after(q, part, near, four) if cube else after(q, part)
            part = attend(asked[0], q, 0, chunk_heads, *common, number * chunk_heads, jnp.bfloat16)
            if cube and not number:
                four = join(far, after(cy, part))
                cx = swap_group(four, groups)
                near = join(out_weight, after(wz, part))
                wy = swap_bit(near, 2)
            back.append(lax.ppermute(part, "seq", row_pairs(parity)))
            last = part
        others.append(back)
    early = heads - rows // HD
    awaited = [others[0][0]] if phases else []
    if cube:
        awaited += [cx, wy]
    q = after(query_rows, last) if phases else query_rows
    own = [attend(lists, q, 0, early, *common, 0, jnp.float32, 0)]
    q = after(query_rows, *awaited)
    own.append(attend(lists, q, early, heads - early, *common, early, jnp.float32))
    partner = jnp.stack(
        [
            jnp.where(row % 2 == parity, row + 1 < grid_rows, row > 0).astype(jnp.int32)
            for parity in phases
        ]
        or [jnp.int32(0)]
    )
    attention = merge(partner, [own] + others)
    if cube:
        swapped = [swap_bit(after(piece, own[0]), 1) for piece in (near, wy, four, cx)]
        swapped = [after(piece, attention) for piece in swapped]
        pieces = cube.pieces(near, wy, four, cx, swapped)
    else:
        whole = lax.all_gather(out_weight, "seq", axis=0, tiled=True)
        pieces = [(whole, [(0, whole.shape[0], lambda: 0)])]
    return project(pieces, attention)


def solution(mesh):
    placed = (
        P(("group", "seq"), None),
        P(("group", "seq"), None),
        P(("group", "seq"), None),
        P(("group", "seq"), None),
        P("seq", None),
    )
    return jax.shard_map(
        functools.partial(body, mesh.shape["group"]),
        mesh=mesh,
        in_specs=placed,
        out_specs=P(("group", "seq"), None),
        check_vma=False,
    )
```

```python
import functools
import math

import jax
import jax.numpy as jnp
from jax import lax
from jax.experimental import pallas as pl
from jax.experimental.pallas import tpu as pltpu
from jax.sharding import PartitionSpec as P

HD = 128
FRAMES = 2
GRID_COLS = 8
EXTRA = 16
PIECES = 3
LOG2E = math.log2(math.e)
VMEM_BYTES = 48 * 1024 * 1024
WEIGHTY = 10**12


def swap_bit(value, bit):
    count = lax.axis_size("seq")
    return lax.ppermute(value, "seq", [(s, s ^ bit) for s in range(count)])


def swap_group(value, groups):
    return lax.ppermute(value, "group", [(s, s ^ 1) for s in range(groups)])


def column_shift(value, steps):
    count = lax.axis_size("seq")
    pairs = [(s, s + steps) for s in range(count) if 0 <= s % GRID_COLS + steps < GRID_COLS]
    return lax.ppermute(value, "seq", pairs)


def row_pairs(parity):
    count = lax.axis_size("seq")
    rows = count // GRID_COLS
    pairs = []
    for s in range(count):
        row = s // GRID_COLS
        other = row + 1 if row % 2 == parity else row - 1
        if 0 <= other < rows:
            pairs.append((s, s + (other - row) * GRID_COLS))
    return pairs


def join_kernel(count, *refs):
    sources, (out_ref, sems) = refs[:count], refs[count:]
    copies, first = [], 0
    for i, source in enumerate(sources):
        size = source.shape[0]
        copy = pltpu.make_async_copy(source, out_ref.at[pl.ds(first, size), :], sems.at[i])
        copy.start()
        copies.append(copy)
        first += size
    for copy in copies:
        copy.wait()


def join(*arrays):
    rows = sum(array.shape[0] for array in arrays)
    return pl.pallas_call(
        functools.partial(join_kernel, len(arrays)),
        in_specs=[pl.BlockSpec(memory_space=pl.ANY)] * len(arrays),
        out_specs=pl.BlockSpec(memory_space=pltpu.VMEM),
        out_shape=jax.ShapeDtypeStruct((rows, arrays[0].shape[1]), arrays[0].dtype),
        scratch_shapes=[pltpu.SemaphoreType.DMA((len(arrays),))],
        compiler_params=pltpu.CompilerParams(vmem_limit_bytes=VMEM_BYTES),
        cost_estimate=pl.CostEstimate(flops=0, bytes_accessed=0, transcendentals=0),
    )(*arrays)


def attend_kernel(rows, per_block, list_ref, q_ref, k0, ka, kb, v0, va, vb, out_ref):
    factor = HD ** (-0.5) * LOG2E
    tile = rows // FRAMES
    position = lax.axis_index("seq")
    lists = list_ref[...].astype(jnp.float32)
    masks = []
    for step in (0, -1, 1):
        bits = []
        for frame in range(FRAMES):
            tile_id = (position + step) * FRAMES + frame
            tile_id = jnp.where(tile_id >= 0, tile_id, -2).astype(jnp.float32)
            hit = jnp.max(jnp.where(lists == tile_id, 0.0, -jnp.inf), axis=1, keepdims=True)
            bits.append(jnp.broadcast_to(hit, (hit.shape[0], tile)))
        masks.append(jnp.concatenate(bits, axis=1))
    nt = (((1,), (1,)), ((), ()))
    lse = jnp.zeros((rows, HD), jnp.float32)
    lane = lax.broadcasted_iota(jnp.int32, (rows, HD), 1)
    for head in range(per_block):
        cols = slice(head * HD, (head + 1) * HD)
        keys = [k0[:, cols], ka[0, :, cols], kb[0, :, cols]]
        values = [v0[:, cols], va[0, :, cols], vb[0, :, cols]]
        parts = []
        for frame in range(FRAMES):
            here = slice(frame * tile, (frame + 1) * tile)
            q = q_ref[here, cols]
            scores = [
                lax.dot_general(q, key, nt, preferred_element_type=jnp.float32)
                + mask[frame : frame + 1, :]
                for key, mask in zip(keys, masks)
            ]
            peak = functools.reduce(jnp.maximum, scores)
            peak = jnp.max(peak, axis=1, keepdims=True)
            weights = [jnp.exp2((s - peak) * factor) for s in scores]
            total = jnp.sum(functools.reduce(jnp.add, weights), axis=1, keepdims=True)
            mixed = functools.reduce(
                jnp.add,
                [
                    jnp.dot(w.astype(jnp.bfloat16), v, preferred_element_type=jnp.float32)
                    for w, v in zip(weights, values)
                ],
            )
            out_ref[here, cols] = (mixed / total).astype(out_ref.dtype)
            parts.append(peak * factor + jnp.log2(total))
        lse = jnp.where(lane == head, jnp.concatenate(parts, axis=0), lse)
    turned = jnp.transpose(lse)
    stats = []
    for head in range(per_block):
        rest = turned[head : head + 1, :]
        for _ in range(PIECES):
            piece = rest.astype(out_ref.dtype)
            stats.append(piece.astype(jnp.float32))
            rest = rest - stats[-1]
    stats.append(jnp.zeros((EXTRA - len(stats), rows), jnp.float32))
    out_ref[rows:, :] = jnp.concatenate(stats, axis=0).astype(out_ref.dtype)


def attend(lists, q, q_first, heads, keys, values, kv_up, kv_down, first, kind, cost=WEIGHTY):
    rows = keys.shape[0]
    per_block = rows // HD
    width = per_block * HD
    lo, q_lo = first * HD // width, q_first * HD // width
    here = pl.BlockSpec((rows, width), lambda i: (0, lo + i))
    key_spec = pl.BlockSpec((1, rows, width), lambda i: (0, 0, lo + i))
    value_spec = pl.BlockSpec((1, rows, width), lambda i: (1, 0, lo + i))
    span = 3 * rows
    return pl.pallas_call(
        functools.partial(attend_kernel, rows, per_block),
        grid=(heads // per_block,),
        in_specs=[
            pl.BlockSpec((EXTRA, HD), lambda i: (lists.shape[0] // EXTRA - 1, 0)),
            pl.BlockSpec((rows, width), lambda i: (0, q_lo + i)),
            here,
            key_spec,
            key_spec,
            here,
            value_spec,
            value_spec,
        ],
        out_specs=pl.BlockSpec((rows + EXTRA, width), lambda i: (0, i)),
        out_shape=jax.ShapeDtypeStruct((rows + EXTRA, heads * HD), kind),
        compiler_params=pltpu.CompilerParams(vmem_limit_bytes=VMEM_BYTES),
        cost_estimate=pl.CostEstimate(
            flops=cost, bytes_accessed=0, transcendentals=0
        ),
    )(lists, q, keys, kv_up, kv_down, values, kv_up, kv_down)


def merge_kernel(rows, chunk_counts, partner_ref, *refs):
    parts, cursor = [], 0
    for count in chunk_counts:
        parts.append(refs[cursor : cursor + count])
        cursor += count
    attention = refs[cursor]
    per_block = rows // HD
    width = per_block * HD
    for block in range(attention.shape[1] // width):
        tiles = []
        for chunks in parts:
            offset = block * width
            for chunk in chunks:
                if offset < chunk.shape[1]:
                    break
                offset -= chunk.shape[1]
            tiles.append(chunk[:, offset : offset + width].astype(jnp.float32))
        shares = []
        for head in range(per_block):
            lses = []
            for number, t in enumerate(tiles):
                row = rows + PIECES * head
                lse = functools.reduce(
                    jnp.add, [t[row + i : row + i + 1, :] for i in range(PIECES)]
                )
                if number:
                    lse = jnp.where(partner_ref[number - 1] == 1, lse, -jnp.inf)
                lses.append(lse)
            top = functools.reduce(jnp.maximum, lses)
            raw = [jnp.exp2(lse - top) for lse in lses]
            total = functools.reduce(jnp.add, raw)
            shares.extend(r / total for r in raw)
        shares.append(jnp.zeros((HD - len(shares), rows), jnp.float32))
        turned = jnp.transpose(jnp.concatenate(shares, axis=0))
        for head in range(per_block):
            inner = slice(head * HD, (head + 1) * HD)
            mixed = functools.reduce(
                jnp.add,
                [
                    t[:rows, inner] * turned[:, head * len(tiles) + n : head * len(tiles) + n + 1]
                    for n, t in enumerate(tiles)
                ],
            )
            start = block * width + head * HD
            attention[:, start : start + HD] = mixed.astype(jnp.bfloat16)


def merge(partner, parts):
    flat = [chunk for chunks in parts for chunk in chunks]
    rows = flat[0].shape[0] - EXTRA
    features = sum(chunk.shape[1] for chunk in parts[0])
    vmem = pl.BlockSpec(memory_space=pltpu.VMEM)
    return pl.pallas_call(
        functools.partial(merge_kernel, rows, [len(c) for c in parts]),
        in_specs=[pl.BlockSpec(memory_space=pltpu.SMEM)] + [vmem] * len(flat),
        out_specs=vmem,
        out_shape=jax.ShapeDtypeStruct((rows, features), jnp.bfloat16),
        compiler_params=pltpu.CompilerParams(vmem_limit_bytes=VMEM_BYTES),
        cost_estimate=pl.CostEstimate(flops=WEIGHTY, bytes_accessed=0, transcendentals=0),
    )(partner, *flat)


def project_kernel(plan, *refs):
    weights = refs[: len(plan)]
    attention, out_ref, held, sems = refs[len(plan) :]
    copies = []
    for source, moves in zip(weights, plan):
        for from_row, count, place in moves:
            into = pl.multiple_of(place(), 16)
            copy = pltpu.make_async_copy(
                source.at[pl.ds(from_row, count), :],
                held.at[pl.ds(into, count), :],
                sems.at[len(copies)],
            )
            copy.start()
            copies.append(copy)
    for copy in copies:
        copy.wait()
    columns = out_ref.shape[1]
    step = math.gcd(columns, 512)

    @pl.loop(0, columns // step)
    def _(i):
        there = pl.ds(pl.multiple_of(i * step, step), step)
        out_ref[:, there] = jnp.dot(
            attention[...], held[:, there], preferred_element_type=jnp.float32
        ).astype(out_ref.dtype)


def project(pieces, attention):
    arrays = [array for array, _ in pieces]
    plan = [moves for _, moves in pieces]
    rows, features = attention.shape
    columns = arrays[0].shape[1]
    vmem = pl.BlockSpec(memory_space=pltpu.VMEM)
    return pl.pallas_call(
        functools.partial(project_kernel, plan),
        in_specs=[pl.BlockSpec(memory_space=pl.ANY)] * len(arrays) + [vmem],
        out_specs=vmem,
        out_shape=jax.ShapeDtypeStruct((rows, columns), jnp.bfloat16),
        scratch_shapes=[
            pltpu.VMEM((features, columns), jnp.bfloat16),
            pltpu.SemaphoreType.DMA((sum(len(m) for m in plan),)),
        ],
        compiler_params=pltpu.CompilerParams(vmem_limit_bytes=VMEM_BYTES),
    )(*arrays, attention)


def after(value, *done):
    return lax.optimization_barrier((value, *done))[0]


class Cube:
    def __init__(self, out_weight):
        self.near = out_weight
        self.shard = out_weight.shape[0]
        self.half = self.shard // 2

    def cross(self):
        first = lax.axis_index("group") * self.half
        self.c0 = swap_bit(lax.dynamic_slice_in_dim(self.near, first, self.half, 0), 8)

    def full(self, *bits):
        def at(bit):
            return lambda: (lax.axis_index("seq") ^ bit) * self.shard

        return [(i * self.shard, self.shard, at(bit)) for i, bit in enumerate(bits)]

    def halves(self, *bits):
        def at(bit, turn):
            return lambda: (lax.axis_index("seq") ^ bit) * self.shard + (
                lax.axis_index("group") ^ turn
            ) * self.half

        return [(i * self.half, self.half, at(bit, turn)) for i, (bit, turn) in enumerate(bits)]

    def pieces(self, near, wy, four, cx, swapped):
        far = (8, 12, 10, 14)
        return [
            (near, self.full(0, 4)),
            (wy, self.full(2, 6)),
            (four, self.halves(*[(b, 0) for b in far])),
            (cx, self.halves(*[(b, 1) for b in far])),
            (swapped[0], self.full(1, 5)),
            (swapped[1], self.full(3, 7)),
            (swapped[2], self.halves(*[(b ^ 1, 0) for b in far])),
            (swapped[3], self.halves(*[(b ^ 1, 1) for b in far])),
        ]


def body(groups, query_rows, key_rows, value_rows, block_list, out_weight):
    rows, features = query_rows.shape
    heads = features // HD
    devices = lax.axis_size("seq")
    grid_rows = devices // GRID_COLS
    row = lax.axis_index("seq") // GRID_COLS
    chunk_heads = heads // 2
    chunk = chunk_heads * HD
    phases = [parity for parity in range(2) if parity + 1 < grid_rows]
    cube = None
    if devices == 16 and groups == 2 and out_weight.shape[0] % 32 == 0:
        cube = Cube(out_weight)
        cube.cross()
    lists = jnp.pad(
        block_list.astype(jnp.bfloat16),
        ((0, EXTRA - FRAMES), (0, HD - block_list.shape[1])),
        constant_values=-1,
    )
    asking = jnp.concatenate([query_rows[:, :chunk], jnp.tile(lists, (1, chunk_heads))], axis=0)
    kv = join(key_rows, value_rows).reshape(2, rows, features)
    kv_up = column_shift(kv, 1)
    kv_down = column_shift(kv, -1)
    if cube:
        wz = swap_bit(after(out_weight, cube.c0), 4)
    sent = []
    for parity in phases:
        pairs = row_pairs(parity)
        first = lax.ppermute(asking, "seq", pairs)
        second = query_rows[:, chunk:]
        if cube:
            cz = swap_bit(cube.c0, 4)
            far = join(cube.c0, cz)
            cy = swap_bit(far, 2)
            second = after(second, first, far)
        sent.append([first, lax.ppermute(second, "seq", pairs)])
    common = (key_rows, value_rows, kv_up, kv_down)
    others = []
    for parity, asked in zip(phases, sent):
        back = []
        for number, q in enumerate(asked):
            if number:
                q = after(q, part, near, four) if cube else after(q, part)
            part = attend(asked[0], q, 0, chunk_heads, *common, number * chunk_heads, jnp.bfloat16)
            if cube and not number:
                four = join(far, after(cy, part))
                cx = swap_group(four, groups)
                near = join(out_weight, after(wz, part))
                wy = swap_bit(near, 2)
            back.append(lax.ppermute(part, "seq", row_pairs(parity)))
            last = part
        others.append(back)
    early = heads - rows // HD
    awaited = [others[0][0]] if phases else []
    if cube:
        awaited += [cx, wy]
    q = after(query_rows, last) if phases else query_rows
    own = [attend(lists, q, 0, early, *common, 0, jnp.float32, 0)]
    q = after(query_rows, *awaited)
    own.append(attend(lists, q, early, heads - early, *common, early, jnp.float32))
    partner = jnp.stack(
        [
            jnp.where(row % 2 == parity, row + 1 < grid_rows, row > 0).astype(jnp.int32)
            for parity in phases
        ]
        or [jnp.int32(0)]
    )
    attention = merge(partner, [own] + others)
    if cube:
        swapped = [swap_bit(after(piece, own[0]), 1) for piece in (near, wy, four, cx)]
        swapped = [after(piece, attention) for piece in swapped]
        pieces = cube.pieces(near, wy, four, cx, swapped)
    else:
        whole = lax.all_gather(out_weight, "seq", axis=0, tiled=True)
        pieces = [(whole, [(0, whole.shape[0], lambda: 0)])]
    return project(pieces, attention)


def solution(mesh):
    placed = (
        P(("group", "seq"), None),
        P(("group", "seq"), None),
        P(("group", "seq"), None),
        P(("group", "seq"), None),
        P("seq", None),
    )
    return jax.shard_map(
        functools.partial(body, mesh.shape["group"]),
        mesh=mesh,
        in_specs=placed,
        out_specs=P(("group", "seq"), None),
        check_vma=False,
    )
```

```python
import functools
import math

import jax
import jax.numpy as jnp
from jax import lax
from jax.experimental import pallas as pl
from jax.experimental.pallas import tpu as pltpu
from jax.sharding import PartitionSpec as P

HD = 128
FRAMES = 2
GRID_COLS = 8
EXTRA = 16
PIECES = 3
LOG2E = math.log2(math.e)
VMEM_BYTES = 48 * 1024 * 1024
WEIGHTY = 10**12


def swap_bit(value, bit):
    count = lax.axis_size("seq")
    return lax.ppermute(value, "seq", [(s, s ^ bit) for s in range(count)])


def swap_group(value, groups):
    return lax.ppermute(value, "group", [(s, s ^ 1) for s in range(groups)])


def column_shift(value, steps):
    count = lax.axis_size("seq")
    pairs = [(s, s + steps) for s in range(count) if 0 <= s % GRID_COLS + steps < GRID_COLS]
    return lax.ppermute(value, "seq", pairs)


def row_pairs(parity):
    count = lax.axis_size("seq")
    rows = count // GRID_COLS
    pairs = []
    for s in range(count):
        row = s // GRID_COLS
        other = row + 1 if row % 2 == parity else row - 1
        if 0 <= other < rows:
            pairs.append((s, s + (other - row) * GRID_COLS))
    return pairs


def join_kernel(count, *refs):
    sources, (out_ref, sems) = refs[:count], refs[count:]
    copies, first = [], 0
    for i, source in enumerate(sources):
        size = source.shape[0]
        copy = pltpu.make_async_copy(source, out_ref.at[pl.ds(first, size), :], sems.at[i])
        copy.start()
        copies.append(copy)
        first += size
    for copy in copies:
        copy.wait()


def join(*arrays, cost=0):
    rows = sum(array.shape[0] for array in arrays)
    return pl.pallas_call(
        functools.partial(join_kernel, len(arrays)),
        in_specs=[pl.BlockSpec(memory_space=pl.ANY)] * len(arrays),
        out_specs=pl.BlockSpec(memory_space=pltpu.VMEM),
        out_shape=jax.ShapeDtypeStruct((rows, arrays[0].shape[1]), arrays[0].dtype),
        scratch_shapes=[pltpu.SemaphoreType.DMA((len(arrays),))],
        compiler_params=pltpu.CompilerParams(vmem_limit_bytes=VMEM_BYTES),
        cost_estimate=pl.CostEstimate(flops=cost, bytes_accessed=0, transcendentals=0),
    )(*arrays)


def fence_kernel(in_ref, out_ref):
    out_ref[...] = in_ref[...]


def fence(value):
    vmem = pl.BlockSpec(memory_space=pltpu.VMEM)
    return pl.pallas_call(
        fence_kernel,
        in_specs=[vmem],
        out_specs=vmem,
        out_shape=jax.ShapeDtypeStruct(value.shape, value.dtype),
        cost_estimate=pl.CostEstimate(flops=WEIGHTY, bytes_accessed=0, transcendentals=0),
    )(value)


def attend_kernel(rows, per_block, list_ref, q_ref, k0, ka, kb, v0, va, vb, out_ref):
    factor = HD ** (-0.5) * LOG2E
    tile = rows // FRAMES
    position = lax.axis_index("seq")
    lists = list_ref[...].astype(jnp.float32)
    masks = []
    for step in (0, -1, 1):
        bits = []
        for frame in range(FRAMES):
            tile_id = (position + step) * FRAMES + frame
            tile_id = jnp.where(tile_id >= 0, tile_id, -2).astype(jnp.float32)
            hit = jnp.max(jnp.where(lists == tile_id, 0.0, -jnp.inf), axis=1, keepdims=True)
            bits.append(jnp.broadcast_to(hit, (hit.shape[0], tile)))
        masks.append(jnp.concatenate(bits, axis=1))
    nt = (((1,), (1,)), ((), ()))
    lse = jnp.zeros((rows, HD), jnp.float32)
    lane = lax.broadcasted_iota(jnp.int32, (rows, HD), 1)
    for head in range(per_block):
        cols = slice(head * HD, (head + 1) * HD)
        keys = [k0[:, cols], ka[0, :, cols], kb[0, :, cols]]
        values = [v0[:, cols], va[0, :, cols], vb[0, :, cols]]
        parts = []
        for frame in range(FRAMES):
            here = slice(frame * tile, (frame + 1) * tile)
            q = q_ref[here, cols]
            scores = [
                lax.dot_general(q, key, nt, preferred_element_type=jnp.float32)
                + mask[frame : frame + 1, :]
                for key, mask in zip(keys, masks)
            ]
            peak = functools.reduce(jnp.maximum, scores)
            peak = jnp.max(peak, axis=1, keepdims=True)
            weights = [jnp.exp2((s - peak) * factor) for s in scores]
            total = jnp.sum(functools.reduce(jnp.add, weights), axis=1, keepdims=True)
            mixed = functools.reduce(
                jnp.add,
                [
                    jnp.dot(w.astype(jnp.bfloat16), v, preferred_element_type=jnp.float32)
                    for w, v in zip(weights, values)
                ],
            )
            out_ref[here, cols] = (mixed / total).astype(out_ref.dtype)
            parts.append(peak * factor + jnp.log2(total))
        lse = jnp.where(lane == head, jnp.concatenate(parts, axis=0), lse)
    turned = jnp.transpose(lse)
    stats = []
    for head in range(per_block):
        rest = turned[head : head + 1, :]
        for _ in range(PIECES):
            piece = rest.astype(out_ref.dtype)
            stats.append(piece.astype(jnp.float32))
            rest = rest - stats[-1]
    stats.append(jnp.zeros((EXTRA - len(stats), rows), jnp.float32))
    out_ref[rows:, :] = jnp.concatenate(stats, axis=0).astype(out_ref.dtype)


def attend(lists, q, q_first, heads, keys, values, kv_up, kv_down, first, kind, cost=WEIGHTY):
    rows = keys.shape[0]
    per_block = rows // HD
    width = per_block * HD
    lo, q_lo = first * HD // width, q_first * HD // width
    here = pl.BlockSpec((rows, width), lambda i: (0, lo + i))
    key_spec = pl.BlockSpec((1, rows, width), lambda i: (0, 0, lo + i))
    value_spec = pl.BlockSpec((1, rows, width), lambda i: (1, 0, lo + i))
    span = 3 * rows
    return pl.pallas_call(
        functools.partial(attend_kernel, rows, per_block),
        grid=(heads // per_block,),
        in_specs=[
            pl.BlockSpec((EXTRA, HD), lambda i: (lists.shape[0] // EXTRA - 1, 0)),
            pl.BlockSpec((rows, width), lambda i: (0, q_lo + i)),
            here,
            key_spec,
            key_spec,
            here,
            value_spec,
            value_spec,
        ],
        out_specs=pl.BlockSpec((rows + EXTRA, width), lambda i: (0, i)),
        out_shape=jax.ShapeDtypeStruct((rows + EXTRA, heads * HD), kind),
        compiler_params=pltpu.CompilerParams(vmem_limit_bytes=VMEM_BYTES),
        cost_estimate=pl.CostEstimate(
            flops=cost, bytes_accessed=0, transcendentals=0
        ),
    )(lists, q, keys, kv_up, kv_down, values, kv_up, kv_down)


def merge_kernel(rows, chunk_counts, partner_ref, *refs):
    parts, cursor = [], 0
    for count in chunk_counts:
        parts.append(refs[cursor : cursor + count])
        cursor += count
    attention = refs[cursor]
    per_block = rows // HD
    width = per_block * HD
    for block in range(attention.shape[1] // width):
        tiles = []
        for chunks in parts:
            offset = block * width
            for chunk in chunks:
                if offset < chunk.shape[1]:
                    break
                offset -= chunk.shape[1]
            tiles.append(chunk[:, offset : offset + width].astype(jnp.float32))
        shares = []
        for head in range(per_block):
            lses = []
            for number, t in enumerate(tiles):
                row = rows + PIECES * head
                lse = functools.reduce(
                    jnp.add, [t[row + i : row + i + 1, :] for i in range(PIECES)]
                )
                if number:
                    lse = jnp.where(partner_ref[number - 1] == 1, lse, -jnp.inf)
                lses.append(lse)
            top = functools.reduce(jnp.maximum, lses)
            raw = [jnp.exp2(lse - top) for lse in lses]
            total = functools.reduce(jnp.add, raw)
            shares.extend(r / total for r in raw)
        shares.append(jnp.zeros((HD - len(shares), rows), jnp.float32))
        turned = jnp.transpose(jnp.concatenate(shares, axis=0))
        for head in range(per_block):
            inner = slice(head * HD, (head + 1) * HD)
            mixed = functools.reduce(
                jnp.add,
                [
                    t[:rows, inner] * turned[:, head * len(tiles) + n : head * len(tiles) + n + 1]
                    for n, t in enumerate(tiles)
                ],
            )
            start = block * width + head * HD
            attention[:, start : start + HD] = mixed.astype(jnp.bfloat16)


def merge(partner, parts):
    flat = [chunk for chunks in parts for chunk in chunks]
    rows = flat[0].shape[0] - EXTRA
    features = sum(chunk.shape[1] for chunk in parts[0])
    vmem = pl.BlockSpec(memory_space=pltpu.VMEM)
    return pl.pallas_call(
        functools.partial(merge_kernel, rows, [len(c) for c in parts]),
        in_specs=[pl.BlockSpec(memory_space=pltpu.SMEM)] + [vmem] * len(flat),
        out_specs=vmem,
        out_shape=jax.ShapeDtypeStruct((rows, features), jnp.bfloat16),
        compiler_params=pltpu.CompilerParams(vmem_limit_bytes=VMEM_BYTES),
        cost_estimate=pl.CostEstimate(flops=WEIGHTY, bytes_accessed=0, transcendentals=0),
    )(partner, *flat)


def project_kernel(plan, *refs):
    weights = refs[: len(plan)]
    attention, out_ref, held, sems = refs[len(plan) :]
    copies = []
    for source, moves in zip(weights, plan):
        for from_row, count, place in moves:
            into = pl.multiple_of(place(), 16)
            copy = pltpu.make_async_copy(
                source.at[pl.ds(from_row, count), :],
                held.at[pl.ds(into, count), :],
                sems.at[len(copies)],
            )
            copy.start()
            copies.append(copy)
    for copy in copies:
        copy.wait()
    columns = out_ref.shape[1]
    step = math.gcd(columns, 512)

    @pl.loop(0, columns // step)
    def _(i):
        there = pl.ds(pl.multiple_of(i * step, step), step)
        out_ref[:, there] = jnp.dot(
            attention[...], held[:, there], preferred_element_type=jnp.float32
        ).astype(out_ref.dtype)


def project(pieces, attention):
    arrays = [array for array, _ in pieces]
    plan = [moves for _, moves in pieces]
    rows, features = attention.shape
    columns = arrays[0].shape[1]
    vmem = pl.BlockSpec(memory_space=pltpu.VMEM)
    return pl.pallas_call(
        functools.partial(project_kernel, plan),
        in_specs=[pl.BlockSpec(memory_space=pl.ANY)] * len(arrays) + [vmem],
        out_specs=vmem,
        out_shape=jax.ShapeDtypeStruct((rows, columns), jnp.bfloat16),
        scratch_shapes=[
            pltpu.VMEM((features, columns), jnp.bfloat16),
            pltpu.SemaphoreType.DMA((sum(len(m) for m in plan),)),
        ],
        compiler_params=pltpu.CompilerParams(vmem_limit_bytes=VMEM_BYTES),
    )(*arrays, attention)


def after(value, *done):
    return lax.optimization_barrier((value, *done))[0]


class Cube:
    def __init__(self, out_weight):
        self.near = out_weight
        self.shard = out_weight.shape[0]
        self.half = self.shard // 2

    def cross(self):
        first = lax.axis_index("group") * self.half
        self.mine = lax.dynamic_slice_in_dim(self.near, first, self.half, 0)
        self.c0 = swap_bit(self.mine, 8)

    def full(self, *bits):
        def at(bit):
            return lambda: (lax.axis_index("seq") ^ bit) * self.shard

        return [(i * self.shard, self.shard, at(bit)) for i, bit in enumerate(bits)]

    def halves(self, *bits):
        def at(bit, turn):
            return lambda: (lax.axis_index("seq") ^ bit) * self.shard + (
                lax.axis_index("group") ^ turn
            ) * self.half

        return [(i * self.half, self.half, at(bit, turn)) for i, (bit, turn) in enumerate(bits)]

    def pieces(self, near, wy, four, cx, swapped):
        far = (8, 12, 10, 14)
        return [
            (near, self.full(0, 4)),
            (wy, self.full(2, 6)),
            (four, self.halves(*[(b, 0) for b in far])),
            (cx, self.halves(*[(b, 1) for b in far])),
            (swapped[0], self.full(1, 5)),
            (swapped[1], self.full(3, 7)),
            (swapped[2], self.halves(*[(b ^ 1, 0) for b in far])),
            (swapped[3], self.halves(*[(b ^ 1, 1) for b in far])),
        ]


def body(groups, query_rows, key_rows, value_rows, block_list, out_weight):
    rows, features = query_rows.shape
    heads = features // HD
    devices = lax.axis_size("seq")
    grid_rows = devices // GRID_COLS
    row = lax.axis_index("seq") // GRID_COLS
    chunk_heads = heads // 2
    chunk = chunk_heads * HD
    phases = [parity for parity in range(2) if parity + 1 < grid_rows]
    cube = None
    if devices == 16 and groups == 2 and out_weight.shape[0] % 32 == 0:
        cube = Cube(out_weight)
        cube.cross()
    lists = jnp.pad(
        block_list.astype(jnp.bfloat16),
        ((0, EXTRA - FRAMES), (0, HD - block_list.shape[1])),
        constant_values=-1,
    )
    asking = jnp.concatenate([query_rows[:, :chunk], jnp.tile(lists, (1, chunk_heads))], axis=0)
    ahead = [asking] + ([cube.mine] if cube else [])
    kv = join(after(key_rows, *ahead), value_rows, cost=WEIGHTY).reshape(2, rows, features)
    kv_up = column_shift(kv, 1)
    kv_down = column_shift(kv, -1)
    sent = []
    for parity in phases:
        pairs = row_pairs(parity)
        first = lax.ppermute(asking, "seq", pairs)
        second = query_rows[:, chunk:]
        if cube:
            cube.c0 = fence(after(cube.c0, kv))
            cz = swap_bit(cube.c0, 4)
            far = join(cube.c0, cz)
            wz = swap_bit(after(out_weight, first), 4)
            cy = swap_bit(far, 2)
            second = after(second, cube.c0)
        sent.append([first, lax.ppermute(second, "seq", pairs)])
    common = (key_rows, value_rows, kv_up, kv_down)
    others = []
    for parity, asked in zip(phases, sent):
        back = []
        for number, q in enumerate(asked):
            if number:
                q = after(q, part, near, four) if cube else after(q, part)
            part = attend(asked[0], q, 0, chunk_heads, *common, number * chunk_heads, jnp.bfloat16)
            if cube and not number:
                four = join(far, after(cy, part))
                cx = swap_group(four, groups)
                near = join(out_weight, after(wz, part))
                wy = swap_bit(near, 2)
            back.append(lax.ppermute(part, "seq", row_pairs(parity)))
            last = part
        others.append(back)
    early = heads - rows // HD
    awaited = [others[0][0]] if phases else []
    if cube:
        awaited += [cx, wy]
    q = after(query_rows, last) if phases else query_rows
    own = [attend(lists, q, 0, early, *common, 0, jnp.float32, 0)]
    q = after(query_rows, *awaited)
    own.append(attend(lists, q, early, heads - early, *common, early, jnp.float32))
    partner = jnp.stack(
        [
            jnp.where(row % 2 == parity, row + 1 < grid_rows, row > 0).astype(jnp.int32)
            for parity in phases
        ]
        or [jnp.int32(0)]
    )
    attention = merge(partner, [own] + others)
    if cube:
        swapped = [swap_bit(after(piece, own[0]), 1) for piece in (near, wy, four, cx)]
        swapped = [after(piece, attention) for piece in swapped]
        pieces = cube.pieces(near, wy, four, cx, swapped)
    else:
        whole = lax.all_gather(out_weight, "seq", axis=0, tiled=True)
        pieces = [(whole, [(0, whole.shape[0], lambda: 0)])]
    return project(pieces, attention)


def solution(mesh):
    placed = (
        P(("group", "seq"), None),
        P(("group", "seq"), None),
        P(("group", "seq"), None),
        P(("group", "seq"), None),
        P("seq", None),
    )
    return jax.shard_map(
        functools.partial(body, mesh.shape["group"]),
        mesh=mesh,
        in_specs=placed,
        out_specs=P(("group", "seq"), None),
        check_vma=False,
    )
```

```python
import functools
import math

import jax
import jax.numpy as jnp
from jax import lax
from jax.experimental import pallas as pl
from jax.experimental.pallas import tpu as pltpu
from jax.sharding import PartitionSpec as P

HD = 128
FRAMES = 2
GRID_COLS = 8
EXTRA = 16
PIECES = 3
LOG2E = math.log2(math.e)
VMEM_BYTES = 48 * 1024 * 1024
WEIGHTY = 10**12


def swap_bit(value, bit):
    count = lax.axis_size("seq")
    return lax.ppermute(value, "seq", [(s, s ^ bit) for s in range(count)])


def swap_group(value, groups):
    return lax.ppermute(value, "group", [(s, s ^ 1) for s in range(groups)])


def column_shift(value, steps):
    count = lax.axis_size("seq")
    pairs = [(s, s + steps) for s in range(count) if 0 <= s % GRID_COLS + steps < GRID_COLS]
    return lax.ppermute(value, "seq", pairs)


def row_pairs(parity):
    count = lax.axis_size("seq")
    rows = count // GRID_COLS
    pairs = []
    for s in range(count):
        row = s // GRID_COLS
        other = row + 1 if row % 2 == parity else row - 1
        if 0 <= other < rows:
            pairs.append((s, s + (other - row) * GRID_COLS))
    return pairs


def join_kernel(count, *refs):
    sources, (out_ref, sems) = refs[:count], refs[count:]
    copies, first = [], 0
    for i, source in enumerate(sources):
        size = source.shape[0]
        copy = pltpu.make_async_copy(source, out_ref.at[pl.ds(first, size), :], sems.at[i])
        copy.start()
        copies.append(copy)
        first += size
    for copy in copies:
        copy.wait()


def join(*arrays, cost=0):
    rows = sum(array.shape[0] for array in arrays)
    return pl.pallas_call(
        functools.partial(join_kernel, len(arrays)),
        in_specs=[pl.BlockSpec(memory_space=pl.ANY)] * len(arrays),
        out_specs=pl.BlockSpec(memory_space=pltpu.VMEM),
        out_shape=jax.ShapeDtypeStruct((rows, arrays[0].shape[1]), arrays[0].dtype),
        scratch_shapes=[pltpu.SemaphoreType.DMA((len(arrays),))],
        compiler_params=pltpu.CompilerParams(vmem_limit_bytes=VMEM_BYTES),
        cost_estimate=pl.CostEstimate(flops=cost, bytes_accessed=0, transcendentals=0),
    )(*arrays)


def fence_kernel(in_ref, out_ref):
    out_ref[...] = in_ref[...]


def fence(value):
    vmem = pl.BlockSpec(memory_space=pltpu.VMEM)
    return pl.pallas_call(
        fence_kernel,
        in_specs=[vmem],
        out_specs=vmem,
        out_shape=jax.ShapeDtypeStruct(value.shape, value.dtype),
        cost_estimate=pl.CostEstimate(flops=WEIGHTY, bytes_accessed=0, transcendentals=0),
    )(value)


def attend_kernel(rows, per_block, list_ref, q_ref, k0, ka, kb, v0, va, vb, out_ref):
    factor = HD ** (-0.5) * LOG2E
    tile = rows // FRAMES
    position = lax.axis_index("seq")
    lists = list_ref[...].astype(jnp.float32)
    masks = []
    for step in (0, -1, 1):
        bits = []
        for frame in range(FRAMES):
            tile_id = (position + step) * FRAMES + frame
            tile_id = jnp.where(tile_id >= 0, tile_id, -2).astype(jnp.float32)
            hit = jnp.max(jnp.where(lists == tile_id, 0.0, -jnp.inf), axis=1, keepdims=True)
            bits.append(jnp.broadcast_to(hit, (hit.shape[0], tile)))
        masks.append(jnp.concatenate(bits, axis=1))
    nt = (((1,), (1,)), ((), ()))
    lse = jnp.zeros((rows, HD), jnp.float32)
    lane = lax.broadcasted_iota(jnp.int32, (rows, HD), 1)
    for head in range(per_block):
        cols = slice(head * HD, (head + 1) * HD)
        keys = [k0[:, cols], ka[0, :, cols], kb[0, :, cols]]
        values = [v0[:, cols], va[0, :, cols], vb[0, :, cols]]
        parts = []
        for frame in range(FRAMES):
            here = slice(frame * tile, (frame + 1) * tile)
            q = q_ref[here, cols]
            scores = [
                lax.dot_general(q, key, nt, preferred_element_type=jnp.float32)
                + mask[frame : frame + 1, :]
                for key, mask in zip(keys, masks)
            ]
            peak = functools.reduce(jnp.maximum, scores)
            peak = jnp.max(peak, axis=1, keepdims=True)
            weights = [jnp.exp2((s - peak) * factor) for s in scores]
            total = jnp.sum(functools.reduce(jnp.add, weights), axis=1, keepdims=True)
            mixed = functools.reduce(
                jnp.add,
                [
                    jnp.dot(w.astype(jnp.bfloat16), v, preferred_element_type=jnp.float32)
                    for w, v in zip(weights, values)
                ],
            )
            out_ref[here, cols] = (mixed / total).astype(out_ref.dtype)
            parts.append(peak * factor + jnp.log2(total))
        lse = jnp.where(lane == head, jnp.concatenate(parts, axis=0), lse)
    turned = jnp.transpose(lse)
    stats = []
    for head in range(per_block):
        rest = turned[head : head + 1, :]
        for _ in range(PIECES):
            piece = rest.astype(out_ref.dtype)
            stats.append(piece.astype(jnp.float32))
            rest = rest - stats[-1]
    stats.append(jnp.zeros((EXTRA - len(stats), rows), jnp.float32))
    out_ref[rows:, :] = jnp.concatenate(stats, axis=0).astype(out_ref.dtype)


def attend(lists, q, q_first, heads, keys, values, kv_up, kv_down, first, kind, cost=WEIGHTY):
    rows = keys.shape[0]
    per_block = rows // HD
    width = per_block * HD
    lo, q_lo = first * HD // width, q_first * HD // width
    here = pl.BlockSpec((rows, width), lambda i: (0, lo + i))
    key_spec = pl.BlockSpec((1, rows, width), lambda i: (0, 0, lo + i))
    value_spec = pl.BlockSpec((1, rows, width), lambda i: (1, 0, lo + i))
    span = 3 * rows
    return pl.pallas_call(
        functools.partial(attend_kernel, rows, per_block),
        grid=(heads // per_block,),
        in_specs=[
            pl.BlockSpec((EXTRA, HD), lambda i: (lists.shape[0] // EXTRA - 1, 0)),
            pl.BlockSpec((rows, width), lambda i: (0, q_lo + i)),
            here,
            key_spec,
            key_spec,
            here,
            value_spec,
            value_spec,
        ],
        out_specs=pl.BlockSpec((rows + EXTRA, width), lambda i: (0, i)),
        out_shape=jax.ShapeDtypeStruct((rows + EXTRA, heads * HD), kind),
        compiler_params=pltpu.CompilerParams(vmem_limit_bytes=VMEM_BYTES),
        cost_estimate=pl.CostEstimate(
            flops=cost, bytes_accessed=0, transcendentals=0
        ),
    )(lists, q, keys, kv_up, kv_down, values, kv_up, kv_down)


def merge_kernel(rows, count, partner_ref, *refs):
    parts, refs = refs[:count], refs[count:]
    attention = refs[-1]
    first = 0
    if len(refs) > 1:
        first = refs[0].shape[1]
        attention[:, :first] = refs[0][...]
    per_block = rows // HD
    width = per_block * HD
    for block in range((attention.shape[1] - first) // width):
        tiles = []
        for part in parts:
            tiles.append(part[:, block * width : (block + 1) * width].astype(jnp.float32))
        shares = []
        for head in range(per_block):
            lses = []
            for number, t in enumerate(tiles):
                row = rows + PIECES * head
                lse = functools.reduce(
                    jnp.add, [t[row + i : row + i + 1, :] for i in range(PIECES)]
                )
                if number:
                    lse = jnp.where(partner_ref[number - 1] == 1, lse, -jnp.inf)
                lses.append(lse)
            top = functools.reduce(jnp.maximum, lses)
            raw = [jnp.exp2(lse - top) for lse in lses]
            total = functools.reduce(jnp.add, raw)
            shares.extend(r / total for r in raw)
        shares.append(jnp.zeros((HD - len(shares), rows), jnp.float32))
        turned = jnp.transpose(jnp.concatenate(shares, axis=0))
        for head in range(per_block):
            inner = slice(head * HD, (head + 1) * HD)
            mixed = functools.reduce(
                jnp.add,
                [
                    t[:rows, inner] * turned[:, head * len(tiles) + n : head * len(tiles) + n + 1]
                    for n, t in enumerate(tiles)
                ],
            )
            start = first + block * width + head * HD
            attention[:, start : start + HD] = mixed.astype(jnp.bfloat16)


def merge(partner, parts, width, merged=None):
    rows = parts[0].shape[0] - EXTRA
    vmem = pl.BlockSpec(memory_space=pltpu.VMEM)
    before = [] if merged is None else [merged]
    total = width + sum(array.shape[1] for array in before)
    return pl.pallas_call(
        functools.partial(merge_kernel, rows, len(parts)),
        in_specs=[pl.BlockSpec(memory_space=pltpu.SMEM)] + [vmem] * (len(parts) + len(before)),
        out_specs=vmem,
        out_shape=jax.ShapeDtypeStruct((rows, total), jnp.bfloat16),
        compiler_params=pltpu.CompilerParams(vmem_limit_bytes=VMEM_BYTES),
        cost_estimate=pl.CostEstimate(flops=WEIGHTY, bytes_accessed=0, transcendentals=0),
    )(partner, *parts, *before)


def project_kernel(plan, steps, *refs):
    weights = refs[: len(plan)]
    attention, out_ref, held, total, sems = refs[len(plan) :]
    moves = [(source, move) for source, moves in zip(weights, plan) for move in moves]
    copies = []
    for step in range(len(steps)):
        for source, (from_row, count, place, wanted) in moves:
            if wanted == step:
                into = pl.multiple_of(place(), 16)
                copy = pltpu.make_async_copy(
                    source.at[pl.ds(from_row, count), :],
                    held.at[pl.ds(into, count), :],
                    sems.at[len(copies)],
                )
                copy.start()
                copies.append((step, copy))
    columns = out_ref.shape[1]
    width = math.gcd(columns, 512)
    depth = attention.shape[1] // len(steps)
    for step, place in enumerate(steps):
        for wanted, copy in copies:
            if wanted == step:
                copy.wait()
        base = pl.multiple_of(place(), HD)
        features = attention[:, pl.ds(base, depth)]

        @pl.loop(0, columns // width)
        def _(i):
            there = pl.ds(pl.multiple_of(i * width, width), width)
            sums = jnp.dot(
                features, held[pl.ds(base, depth), there], preferred_element_type=jnp.float32
            )
            if step:
                sums += total[:, there]
            if step + 1 < len(steps):
                total[:, there] = sums
            else:
                out_ref[:, there] = sums.astype(out_ref.dtype)


def project(pieces, steps, attention):
    arrays = [array for array, _ in pieces]
    plan = [moves for _, moves in pieces]
    rows, features = attention.shape
    columns = arrays[0].shape[1]
    vmem = pl.BlockSpec(memory_space=pltpu.VMEM)
    return pl.pallas_call(
        functools.partial(project_kernel, plan, steps),
        in_specs=[pl.BlockSpec(memory_space=pl.ANY)] * len(arrays) + [vmem],
        out_specs=vmem,
        out_shape=jax.ShapeDtypeStruct((rows, columns), jnp.bfloat16),
        scratch_shapes=[
            pltpu.VMEM((features, columns), jnp.bfloat16),
            pltpu.VMEM((rows, columns), jnp.float32),
            pltpu.SemaphoreType.DMA((sum(len(m) for m in plan),)),
        ],
        compiler_params=pltpu.CompilerParams(vmem_limit_bytes=VMEM_BYTES),
    )(*arrays, attention)


def after(value, *done):
    return lax.optimization_barrier((value, *done))[0]


class Cube:
    def __init__(self, out_weight):
        self.shard = out_weight.shape[0]
        self.half = self.shard // 2
        self.list = []

    def add(self, array, *places):
        moves, row = [], 0
        for bit, turn in places:
            count = self.shard if turn is None else self.half

            def place(bit=bit, turn=turn):
                base = (lax.axis_index("seq") ^ bit) * self.shard
                if turn is None:
                    return base
                return base + (lax.axis_index("group") ^ turn) * self.half

            moves.append((row, count, place, bit // 8))
            row += count
        self.list.append((array, moves))

    def steps(self):
        depth = 8 * self.shard
        return [lambda r=r: (lax.axis_index("seq") // 8 ^ r) * depth for r in range(2)]


def body(groups, query_rows, key_rows, value_rows, block_list, out_weight):
    rows, features = query_rows.shape
    heads = features // HD
    devices = lax.axis_size("seq")
    grid_rows = devices // GRID_COLS
    row = lax.axis_index("seq") // GRID_COLS
    chunk_heads = heads // 2
    chunk = chunk_heads * HD
    phases = [parity for parity in range(2) if parity + 1 < grid_rows]
    cube = None
    if devices == 16 and groups == 2 and out_weight.shape[0] % 32 == 0:
        cube = Cube(out_weight)
        first = lax.axis_index("group") * cube.half
        mine = lax.dynamic_slice_in_dim(out_weight, first, cube.half, 0)
        mz = swap_bit(mine, 4)
        c0 = swap_bit(mine, 8)
    lists = jnp.pad(
        block_list.astype(jnp.bfloat16),
        ((0, EXTRA - FRAMES), (0, HD - block_list.shape[1])),
        constant_values=-1,
    )
    asking = jnp.concatenate([query_rows[:, :chunk], jnp.tile(lists, (1, chunk_heads))], axis=0)
    ahead = [asking] + ([mine] if cube else [])
    kv = join(after(key_rows, *ahead), value_rows, cost=WEIGHTY).reshape(2, rows, features)
    kv_up = column_shift(kv, 1)
    kv_down = column_shift(kv, -1)
    if cube:
        mz = fence(after(mz, kv))
    sent = []
    for parity in phases:
        pairs = row_pairs(parity)
        first = lax.ppermute(asking, "seq", pairs)
        second = query_rows[:, chunk:]
        if cube:
            second = after(second, mz)
            c0 = after(c0, mz)
            cz = swap_bit(c0, 4)
            first = after(first, c0)
            x0 = swap_group(after(mz, first), groups)
        sent.append([first, lax.ppermute(second, "seq", pairs)])
    common = (key_rows, value_rows, kv_up, kv_down)
    others = []
    for parity, asked in zip(phases, sent):
        back = []
        for number, q in enumerate(asked):
            if number:
                q = after(q, part, far) if cube else after(q, part)
            part = attend(asked[0], q, 0, chunk_heads, *common, number * chunk_heads, jnp.bfloat16)
            if cube and not number:
                far = join(c0, after(cz, part))
                cy = swap_bit(far, 2)
                x1 = swap_group(far, groups)
                near = join(out_weight, mz, after(x0, part))
                wy = swap_bit(near, 2)
            back.append(lax.ppermute(part, "seq", row_pairs(parity)))
            last = part
        others.append(back)
    if cube:
        cy = after(cy, last)
        x2 = swap_group(cy, groups)
    own = []
    for number in range(2):
        q, begin = query_rows, number * chunk_heads
        if phases:
            q = after(q, last, *own, *([cy] if cube and number else []))
        own.append(attend(lists, q, begin, chunk_heads, *common, begin, jnp.float32, 0))
    partner = jnp.stack(
        [
            jnp.where(row % 2 == parity, row + 1 < grid_rows, row > 0).astype(jnp.int32)
            for parity in phases
        ]
        or [jnp.int32(0)]
    )
    attention = merge(partner, [own[0]] + [b[0] for b in others], chunk)
    attention = merge(partner, [own[1]] + [b[1] for b in others], features - chunk, attention)
    if cube:
        spread = [
            (near, [(0, None), (4, 0), (4, 1)]),
            (far, [(8, 0), (12, 0)]),
            (wy, [(2, None), (6, 0), (6, 1)]),
            (x1, [(8, 1), (12, 1)]),
            (cy, [(10, 0), (14, 0)]),
            (x2, [(10, 1), (14, 1)]),
        ]
        landed = []
        for number, (array, _) in enumerate(spread):
            ready = after(array, own[1], *(landed[:2] if number in (2, 5) else []))
            landed.append(swap_bit(ready, 1))
        landed = [after(array, attention) for array in landed]
        for (array, places), turned in zip(spread, landed):
            cube.add(array, *places)
            cube.add(turned, *[(bit ^ 1, turn) for bit, turn in places])
        pieces, steps = cube.list, cube.steps()
    else:
        gathered = lax.all_gather(out_weight, "seq", axis=0, tiled=True)
        pieces, steps = [(gathered, [(0, gathered.shape[0], lambda: 0, 0)])], [lambda: 0]
    return project(pieces, steps, attention)


def solution(mesh):
    placed = (
        P(("group", "seq"), None),
        P(("group", "seq"), None),
        P(("group", "seq"), None),
        P(("group", "seq"), None),
        P("seq", None),
    )
    return jax.shard_map(
        functools.partial(body, mesh.shape["group"]),
        mesh=mesh,
        in_specs=placed,
        out_specs=P(("group", "seq"), None),
        check_vma=False,
    )
```

```python
import functools
import math

import jax
import jax.numpy as jnp
from jax import lax
from jax.experimental import pallas as pl
from jax.experimental.pallas import tpu as pltpu
from jax.sharding import PartitionSpec as P

HD = 128
FRAMES = 2
GRID_COLS = 8
EXTRA = 16
PIECES = 3
LOG2E = math.log2(math.e)
VMEM_BYTES = 48 * 1024 * 1024
WEIGHTY = 10**12


def swap_bit(value, bit):
    count = lax.axis_size("seq")
    return lax.ppermute(value, "seq", [(s, s ^ bit) for s in range(count)])


def swap_group(value, groups):
    return lax.ppermute(value, "group", [(s, s ^ 1) for s in range(groups)])


def column_shift(value, steps):
    count = lax.axis_size("seq")
    pairs = [(s, s + steps) for s in range(count) if 0 <= s % GRID_COLS + steps < GRID_COLS]
    return lax.ppermute(value, "seq", pairs)


def row_pairs(parity):
    count = lax.axis_size("seq")
    rows = count // GRID_COLS
    pairs = []
    for s in range(count):
        row = s // GRID_COLS
        other = row + 1 if row % 2 == parity else row - 1
        if 0 <= other < rows:
            pairs.append((s, s + (other - row) * GRID_COLS))
    return pairs


def join_kernel(count, *refs):
    sources, (out_ref, sems) = refs[:count], refs[count:]
    copies, first = [], 0
    for i, source in enumerate(sources):
        size = source.shape[0]
        copy = pltpu.make_async_copy(source, out_ref.at[pl.ds(first, size), :], sems.at[i])
        copy.start()
        copies.append(copy)
        first += size
    for copy in copies:
        copy.wait()


def join(*arrays, cost=0):
    rows = sum(array.shape[0] for array in arrays)
    return pl.pallas_call(
        functools.partial(join_kernel, len(arrays)),
        in_specs=[pl.BlockSpec(memory_space=pl.ANY)] * len(arrays),
        out_specs=pl.BlockSpec(memory_space=pltpu.VMEM),
        out_shape=jax.ShapeDtypeStruct((rows, arrays[0].shape[1]), arrays[0].dtype),
        scratch_shapes=[pltpu.SemaphoreType.DMA((len(arrays),))],
        compiler_params=pltpu.CompilerParams(vmem_limit_bytes=VMEM_BYTES),
        cost_estimate=pl.CostEstimate(flops=cost, bytes_accessed=0, transcendentals=0),
    )(*arrays)


def fence_kernel(in_ref, out_ref):
    out_ref[...] = in_ref[...]


def fence(value):
    vmem = pl.BlockSpec(memory_space=pltpu.VMEM)
    return pl.pallas_call(
        fence_kernel,
        in_specs=[vmem],
        out_specs=vmem,
        out_shape=jax.ShapeDtypeStruct(value.shape, value.dtype),
        cost_estimate=pl.CostEstimate(flops=WEIGHTY, bytes_accessed=0, transcendentals=0),
    )(value)


def attend_kernel(rows, per_block, list_ref, q_ref, k0, ka, kb, v0, va, vb, out_ref):
    factor = HD ** (-0.5) * LOG2E
    tile = rows // FRAMES
    position = lax.axis_index("seq")
    lists = list_ref[...].astype(jnp.float32)
    masks = []
    for step in (0, -1, 1):
        bits = []
        for frame in range(FRAMES):
            tile_id = (position + step) * FRAMES + frame
            tile_id = jnp.where(tile_id >= 0, tile_id, -2).astype(jnp.float32)
            hit = jnp.max(jnp.where(lists == tile_id, 0.0, -jnp.inf), axis=1, keepdims=True)
            bits.append(jnp.broadcast_to(hit, (hit.shape[0], tile)))
        masks.append(jnp.concatenate(bits, axis=1))
    nt = (((1,), (1,)), ((), ()))
    lse = jnp.zeros((rows, HD), jnp.float32)
    lane = lax.broadcasted_iota(jnp.int32, (rows, HD), 1)
    for head in range(per_block):
        cols = slice(head * HD, (head + 1) * HD)
        keys = [k0[:, cols], ka[0, :, cols], kb[0, :, cols]]
        values = [v0[:, cols], va[0, :, cols], vb[0, :, cols]]
        parts = []
        for frame in range(FRAMES):
            here = slice(frame * tile, (frame + 1) * tile)
            q = q_ref[here, cols]
            scores = [
                lax.dot_general(q, key, nt, preferred_element_type=jnp.float32)
                + mask[frame : frame + 1, :]
                for key, mask in zip(keys, masks)
            ]
            peak = functools.reduce(jnp.maximum, scores)
            peak = jnp.max(peak, axis=1, keepdims=True)
            weights = [jnp.exp2((s - peak) * factor) for s in scores]
            total = jnp.sum(functools.reduce(jnp.add, weights), axis=1, keepdims=True)
            mixed = functools.reduce(
                jnp.add,
                [
                    jnp.dot(w.astype(jnp.bfloat16), v, preferred_element_type=jnp.float32)
                    for w, v in zip(weights, values)
                ],
            )
            out_ref[here, cols] = (mixed / total).astype(out_ref.dtype)
            parts.append(peak * factor + jnp.log2(total))
        lse = jnp.where(lane == head, jnp.concatenate(parts, axis=0), lse)
    turned = jnp.transpose(lse)
    stats = []
    for head in range(per_block):
        rest = turned[head : head + 1, :]
        for _ in range(PIECES):
            piece = rest.astype(out_ref.dtype)
            stats.append(piece.astype(jnp.float32))
            rest = rest - stats[-1]
    stats.append(jnp.zeros((EXTRA - len(stats), rows), jnp.float32))
    out_ref[rows:, :] = jnp.concatenate(stats, axis=0).astype(out_ref.dtype)


def attend(lists, q, q_first, heads, keys, values, kv_up, kv_down, first, kind, cost=WEIGHTY):
    rows = keys.shape[0]
    per_block = rows // HD
    width = per_block * HD
    lo, q_lo = first * HD // width, q_first * HD // width
    here = pl.BlockSpec((rows, width), lambda i: (0, lo + i))
    key_spec = pl.BlockSpec((1, rows, width), lambda i: (0, 0, lo + i))
    value_spec = pl.BlockSpec((1, rows, width), lambda i: (1, 0, lo + i))
    span = 3 * rows
    return pl.pallas_call(
        functools.partial(attend_kernel, rows, per_block),
        grid=(heads // per_block,),
        in_specs=[
            pl.BlockSpec((EXTRA, HD), lambda i: (lists.shape[0] // EXTRA - 1, 0)),
            pl.BlockSpec((rows, width), lambda i: (0, q_lo + i)),
            here,
            key_spec,
            key_spec,
            here,
            value_spec,
            value_spec,
        ],
        out_specs=pl.BlockSpec((rows + EXTRA, width), lambda i: (0, i)),
        out_shape=jax.ShapeDtypeStruct((rows + EXTRA, heads * HD), kind),
        compiler_params=pltpu.CompilerParams(vmem_limit_bytes=VMEM_BYTES),
        cost_estimate=pl.CostEstimate(
            flops=cost, bytes_accessed=0, transcendentals=0
        ),
    )(lists, q, keys, kv_up, kv_down, values, kv_up, kv_down)


def merge_kernel(rows, count, partner_ref, *refs):
    parts, refs = refs[:count], refs[count:]
    attention = refs[-1]
    first = 0
    if len(refs) > 1:
        first = refs[0].shape[1]
        attention[:, :first] = refs[0][...]
    per_block = rows // HD
    width = per_block * HD
    for block in range((attention.shape[1] - first) // width):
        tiles = []
        for part in parts:
            tiles.append(part[:, block * width : (block + 1) * width].astype(jnp.float32))
        shares = []
        for head in range(per_block):
            lses = []
            for number, t in enumerate(tiles):
                row = rows + PIECES * head
                lse = functools.reduce(
                    jnp.add, [t[row + i : row + i + 1, :] for i in range(PIECES)]
                )
                if number:
                    lse = jnp.where(partner_ref[number - 1] == 1, lse, -jnp.inf)
                lses.append(lse)
            top = functools.reduce(jnp.maximum, lses)
            raw = [jnp.exp2(lse - top) for lse in lses]
            total = functools.reduce(jnp.add, raw)
            shares.extend(r / total for r in raw)
        shares.append(jnp.zeros((HD - len(shares), rows), jnp.float32))
        turned = jnp.transpose(jnp.concatenate(shares, axis=0))
        for head in range(per_block):
            inner = slice(head * HD, (head + 1) * HD)
            mixed = functools.reduce(
                jnp.add,
                [
                    t[:rows, inner] * turned[:, head * len(tiles) + n : head * len(tiles) + n + 1]
                    for n, t in enumerate(tiles)
                ],
            )
            start = first + block * width + head * HD
            attention[:, start : start + HD] = mixed.astype(jnp.bfloat16)


def merge(partner, parts, width, merged=None):
    rows = parts[0].shape[0] - EXTRA
    vmem = pl.BlockSpec(memory_space=pltpu.VMEM)
    before = [] if merged is None else [merged]
    total = width + sum(array.shape[1] for array in before)
    return pl.pallas_call(
        functools.partial(merge_kernel, rows, len(parts)),
        in_specs=[pl.BlockSpec(memory_space=pltpu.SMEM)] + [vmem] * (len(parts) + len(before)),
        out_specs=vmem,
        out_shape=jax.ShapeDtypeStruct((rows, total), jnp.bfloat16),
        compiler_params=pltpu.CompilerParams(vmem_limit_bytes=VMEM_BYTES),
        cost_estimate=pl.CostEstimate(flops=WEIGHTY, bytes_accessed=0, transcendentals=0),
    )(partner, *parts, *before)


def project_kernel(plan, steps, *refs):
    weights = refs[: len(plan)]
    attention, out_ref, held, total, sems = refs[len(plan) :]
    moves = [(source, move) for source, moves in zip(weights, plan) for move in moves]
    copies = []
    for step in range(len(steps)):
        for source, (from_row, count, place, wanted) in moves:
            if wanted == step:
                into = pl.multiple_of(place(), 16)
                copy = pltpu.make_async_copy(
                    source.at[pl.ds(from_row, count), :],
                    held.at[pl.ds(into, count), :],
                    sems.at[len(copies)],
                )
                copy.start()
                copies.append((step, copy))
    columns = out_ref.shape[1]
    width = math.gcd(columns, 512)
    depth = attention.shape[1] // len(steps)
    for step, place in enumerate(steps):
        for wanted, copy in copies:
            if wanted == step:
                copy.wait()
        base = pl.multiple_of(place(), HD)
        features = attention[:, pl.ds(base, depth)]

        @pl.loop(0, columns // width)
        def _(i):
            there = pl.ds(pl.multiple_of(i * width, width), width)
            sums = jnp.dot(
                features, held[pl.ds(base, depth), there], preferred_element_type=jnp.float32
            )
            if step:
                sums += total[:, there]
            if step + 1 < len(steps):
                total[:, there] = sums
            else:
                out_ref[:, there] = sums.astype(out_ref.dtype)


def project(pieces, steps, attention):
    arrays = [array for array, _ in pieces]
    plan = [moves for _, moves in pieces]
    rows, features = attention.shape
    columns = arrays[0].shape[1]
    vmem = pl.BlockSpec(memory_space=pltpu.VMEM)
    return pl.pallas_call(
        functools.partial(project_kernel, plan, steps),
        in_specs=[pl.BlockSpec(memory_space=pl.ANY)] * len(arrays) + [vmem],
        out_specs=vmem,
        out_shape=jax.ShapeDtypeStruct((rows, columns), jnp.bfloat16),
        scratch_shapes=[
            pltpu.VMEM((features, columns), jnp.bfloat16),
            pltpu.VMEM((rows, columns), jnp.float32),
            pltpu.SemaphoreType.DMA((sum(len(m) for m in plan),)),
        ],
        compiler_params=pltpu.CompilerParams(vmem_limit_bytes=VMEM_BYTES),
    )(*arrays, attention)


def after(value, *done):
    return lax.optimization_barrier((value, *done))[0]


class Cube:
    def __init__(self, out_weight):
        self.shard = out_weight.shape[0]
        self.half = self.shard // 2
        self.list = []

    def add(self, array, *places):
        moves, row = [], 0
        for bit, turn in places:
            count = self.shard if turn is None else self.half

            def place(bit=bit, turn=turn):
                base = (lax.axis_index("seq") ^ bit) * self.shard
                if turn is None:
                    return base
                return base + (lax.axis_index("group") ^ turn) * self.half

            moves.append((row, count, place, bit // 8))
            row += count
        self.list.append((array, moves))

    def steps(self):
        depth = 8 * self.shard
        return [lambda r=r: (lax.axis_index("seq") // 8 ^ r) * depth for r in range(2)]


def body(groups, query_rows, key_rows, value_rows, block_list, out_weight):
    rows, features = query_rows.shape
    heads = features // HD
    devices = lax.axis_size("seq")
    grid_rows = devices // GRID_COLS
    row = lax.axis_index("seq") // GRID_COLS
    chunk_heads = heads // 2
    chunk = chunk_heads * HD
    phases = [parity for parity in range(2) if parity + 1 < grid_rows]
    cube = None
    if devices == 16 and groups == 2 and out_weight.shape[0] % 32 == 0:
        cube = Cube(out_weight)
        first = lax.axis_index("group") * cube.half
        mine = lax.dynamic_slice_in_dim(out_weight, first, cube.half, 0)
        mz = swap_bit(mine, 4)
        c0 = swap_bit(mine, 8)
    lists = jnp.pad(
        block_list.astype(jnp.bfloat16),
        ((0, EXTRA - FRAMES), (0, HD - block_list.shape[1])),
        constant_values=-1,
    )
    asking = jnp.concatenate([query_rows[:, :chunk], jnp.tile(lists, (1, chunk_heads))], axis=0)
    ahead = [asking] + ([mine] if cube else [])
    kv = join(after(key_rows, *ahead), value_rows, cost=WEIGHTY).reshape(2, rows, features)
    kv_up = column_shift(kv, 1)
    kv_down = column_shift(kv, -1)
    if cube:
        mz = fence(after(mz, kv))
    sent = []
    for parity in phases:
        pairs = row_pairs(parity)
        first = lax.ppermute(asking, "seq", pairs)
        second = query_rows[:, chunk:]
        if cube:
            second = after(second, first)
            c0 = after(c0, mz)
            cz = swap_bit(c0, 4)
            first = after(first, c0)
            x0 = swap_group(mz, groups)
            near = join(out_weight, mz, x0)
            wy = swap_bit(near, 2)
        sent.append([first, lax.ppermute(second, "seq", pairs)])
    common = (key_rows, value_rows, kv_up, kv_down)
    others = []
    for parity, asked in zip(phases, sent):
        back = []
        for number, q in enumerate(asked):
            if number:
                q = after(q, part, far) if cube else after(q, part)
            part = attend(asked[0], q, 0, chunk_heads, *common, number * chunk_heads, jnp.bfloat16)
            if cube and not number:
                far = join(c0, after(cz, part))
                cy = swap_bit(far, 2)
                x1 = swap_group(far, groups)
            back.append(lax.ppermute(part, "seq", row_pairs(parity)))
            last = part
        others.append(back)
    if cube:
        cy = after(cy, last)
        x2 = swap_group(cy, groups)
    own = []
    for number in range(2):
        q, begin = query_rows, number * chunk_heads
        if phases:
            q = after(q, last, *own, *([cy] if cube and number else []))
        own.append(attend(lists, q, begin, chunk_heads, *common, begin, jnp.float32, 0))
    partner = jnp.stack(
        [
            jnp.where(row % 2 == parity, row + 1 < grid_rows, row > 0).astype(jnp.int32)
            for parity in phases
        ]
        or [jnp.int32(0)]
    )
    attention = merge(partner, [own[0]] + [b[0] for b in others], chunk)
    attention = merge(partner, [own[1]] + [b[1] for b in others], features - chunk, attention)
    if cube:
        spread = [
            (near, [(0, None), (4, 0), (4, 1)]),
            (far, [(8, 0), (12, 0)]),
            (wy, [(2, None), (6, 0), (6, 1)]),
            (x1, [(8, 1), (12, 1)]),
            (cy, [(10, 0), (14, 0)]),
            (x2, [(10, 1), (14, 1)]),
        ]
        landed = []
        for number, (array, _) in enumerate(spread):
            ready = after(array, own[1], *(landed[:2] if number in (2, 5) else []))
            landed.append(swap_bit(ready, 1))
        landed = [after(array, attention) for array in landed]
        for (array, places), turned in zip(spread, landed):
            cube.add(array, *places)
            cube.add(turned, *[(bit ^ 1, turn) for bit, turn in places])
        pieces, steps = cube.list, cube.steps()
    else:
        gathered = lax.all_gather(out_weight, "seq", axis=0, tiled=True)
        pieces, steps = [(gathered, [(0, gathered.shape[0], lambda: 0, 0)])], [lambda: 0]
    return project(pieces, steps, attention)


def solution(mesh):
    placed = (
        P(("group", "seq"), None),
        P(("group", "seq"), None),
        P(("group", "seq"), None),
        P(("group", "seq"), None),
        P("seq", None),
    )
    return jax.shard_map(
        functools.partial(body, mesh.shape["group"]),
        mesh=mesh,
        in_specs=placed,
        out_specs=P(("group", "seq"), None),
        check_vma=False,
    )
```

```python
import functools
import math

import jax
import jax.numpy as jnp
from jax import lax
from jax.experimental import pallas as pl
from jax.experimental.pallas import tpu as pltpu
from jax.sharding import PartitionSpec as P

HD = 128
FRAMES = 2
GRID_COLS = 8
EXTRA = 16
PIECES = 3
LOG2E = math.log2(math.e)
MIB = 1024 * 1024
VMEM_BYTES = 48 * MIB
WEIGHTY = 10**12


def swap_bit(value, bit):
    count = lax.axis_size("seq")
    return lax.ppermute(value, "seq", [(s, s ^ bit) for s in range(count)])


def swap_group(value, groups):
    return lax.ppermute(value, "group", [(s, s ^ 1) for s in range(groups)])


def column_shift(value, steps):
    count = lax.axis_size("seq")
    pairs = [(s, s + steps) for s in range(count) if 0 <= s % GRID_COLS + steps < GRID_COLS]
    return lax.ppermute(value, "seq", pairs)


def row_pairs(parity):
    count = lax.axis_size("seq")
    rows = count // GRID_COLS
    pairs = []
    for s in range(count):
        row = s // GRID_COLS
        other = row + 1 if row % 2 == parity else row - 1
        if 0 <= other < rows:
            pairs.append((s, s + (other - row) * GRID_COLS))
    return pairs


def join_kernel(count, *refs):
    sources, (out_ref, sems) = refs[:count], refs[count:]
    copies, first = [], 0
    for i, source in enumerate(sources):
        size = source.shape[0]
        copy = pltpu.make_async_copy(source, out_ref.at[pl.ds(first, size), :], sems.at[i])
        copy.start()
        copies.append(copy)
        first += size
    for copy in copies:
        copy.wait()


def join(*arrays, cost=0):
    rows = sum(array.shape[0] for array in arrays)
    return pl.pallas_call(
        functools.partial(join_kernel, len(arrays)),
        in_specs=[pl.BlockSpec(memory_space=pl.ANY)] * len(arrays),
        out_specs=pl.BlockSpec(memory_space=pltpu.VMEM),
        out_shape=jax.ShapeDtypeStruct((rows, arrays[0].shape[1]), arrays[0].dtype),
        scratch_shapes=[pltpu.SemaphoreType.DMA((len(arrays),))],
        compiler_params=pltpu.CompilerParams(vmem_limit_bytes=8 * MIB),
        cost_estimate=pl.CostEstimate(flops=cost, bytes_accessed=0, transcendentals=0),
    )(*arrays)


def fence_kernel(in_ref, out_ref):
    out_ref[...] = in_ref[...]


def fence(value):
    vmem = pl.BlockSpec(memory_space=pltpu.VMEM)
    return pl.pallas_call(
        fence_kernel,
        in_specs=[vmem],
        out_specs=vmem,
        out_shape=jax.ShapeDtypeStruct(value.shape, value.dtype),
        cost_estimate=pl.CostEstimate(flops=WEIGHTY, bytes_accessed=0, transcendentals=0),
    )(value)


def attend_kernel(rows, per_block, list_ref, q_ref, k0, ka, kb, v0, va, vb, out_ref):
    factor = HD ** (-0.5) * LOG2E
    tile = rows // FRAMES
    position = lax.axis_index("seq")
    lists = list_ref[...].astype(jnp.float32)
    masks = []
    for step in (0, -1, 1):
        bits = []
        for frame in range(FRAMES):
            tile_id = (position + step) * FRAMES + frame
            tile_id = jnp.where(tile_id >= 0, tile_id, -2).astype(jnp.float32)
            hit = jnp.max(jnp.where(lists == tile_id, 0.0, -jnp.inf), axis=1, keepdims=True)
            bits.append(jnp.broadcast_to(hit, (hit.shape[0], tile)))
        masks.append(jnp.concatenate(bits, axis=1))
    nt = (((1,), (1,)), ((), ()))
    lse = jnp.zeros((rows, HD), jnp.float32)
    lane = lax.broadcasted_iota(jnp.int32, (rows, HD), 1)
    for head in range(per_block):
        cols = slice(head * HD, (head + 1) * HD)
        keys = [k0[:, cols], ka[0, :, cols], kb[0, :, cols]]
        values = [v0[:, cols], va[0, :, cols], vb[0, :, cols]]
        parts = []
        for frame in range(FRAMES):
            here = slice(frame * tile, (frame + 1) * tile)
            q = q_ref[here, cols]
            scores = [
                lax.dot_general(q, key, nt, preferred_element_type=jnp.float32)
                + mask[frame : frame + 1, :]
                for key, mask in zip(keys, masks)
            ]
            peak = functools.reduce(jnp.maximum, scores)
            peak = jnp.max(peak, axis=1, keepdims=True)
            weights = [jnp.exp2((s - peak) * factor) for s in scores]
            total = jnp.sum(functools.reduce(jnp.add, weights), axis=1, keepdims=True)
            mixed = functools.reduce(
                jnp.add,
                [
                    jnp.dot(w.astype(jnp.bfloat16), v, preferred_element_type=jnp.float32)
                    for w, v in zip(weights, values)
                ],
            )
            out_ref[here, cols] = (mixed / total).astype(out_ref.dtype)
            parts.append(peak * factor + jnp.log2(total))
        lse = jnp.where(lane == head, jnp.concatenate(parts, axis=0), lse)
    turned = jnp.transpose(lse)
    stats = []
    for head in range(per_block):
        rest = turned[head : head + 1, :]
        for _ in range(PIECES):
            piece = rest.astype(out_ref.dtype)
            stats.append(piece.astype(jnp.float32))
            rest = rest - stats[-1]
    stats.append(jnp.zeros((EXTRA - len(stats), rows), jnp.float32))
    out_ref[rows:, :] = jnp.concatenate(stats, axis=0).astype(out_ref.dtype)


def attend(lists, q, q_first, heads, keys, values, kv_up, kv_down, first, kind, cost=WEIGHTY):
    rows = keys.shape[0]
    per_block = rows // HD
    width = per_block * HD
    lo, q_lo = first * HD // width, q_first * HD // width
    here = pl.BlockSpec((rows, width), lambda i: (0, lo + i))
    key_spec = pl.BlockSpec((1, rows, width), lambda i: (0, 0, lo + i))
    value_spec = pl.BlockSpec((1, rows, width), lambda i: (1, 0, lo + i))
    span = 3 * rows
    return pl.pallas_call(
        functools.partial(attend_kernel, rows, per_block),
        grid=(heads // per_block,),
        in_specs=[
            pl.BlockSpec((EXTRA, HD), lambda i: (lists.shape[0] // EXTRA - 1, 0)),
            pl.BlockSpec((rows, width), lambda i: (0, q_lo + i)),
            here,
            key_spec,
            key_spec,
            here,
            value_spec,
            value_spec,
        ],
        out_specs=pl.BlockSpec((rows + EXTRA, width), lambda i: (0, i)),
        out_shape=jax.ShapeDtypeStruct((rows + EXTRA, heads * HD), kind),
        compiler_params=pltpu.CompilerParams(vmem_limit_bytes=12 * MIB),
        cost_estimate=pl.CostEstimate(
            flops=cost, bytes_accessed=0, transcendentals=0
        ),
    )(lists, q, keys, kv_up, kv_down, values, kv_up, kv_down)


def merge_parts(rows, parts, partner_ref, attention):
    per_block = rows // HD
    width = per_block * HD
    for block in range(attention.shape[1] // width):
        tiles = []
        for part in parts:
            tiles.append(part[:, block * width : (block + 1) * width].astype(jnp.float32))
        shares = []
        for head in range(per_block):
            lses = []
            for number, t in enumerate(tiles):
                row = rows + PIECES * head
                lse = functools.reduce(
                    jnp.add, [t[row + i : row + i + 1, :] for i in range(PIECES)]
                )
                if number:
                    lse = jnp.where(partner_ref[number - 1] == 1, lse, -jnp.inf)
                lses.append(lse)
            top = functools.reduce(jnp.maximum, lses)
            raw = [jnp.exp2(lse - top) for lse in lses]
            total = functools.reduce(jnp.add, raw)
            shares.extend(r / total for r in raw)
        shares.append(jnp.zeros((HD - len(shares), rows), jnp.float32))
        turned = jnp.transpose(jnp.concatenate(shares, axis=0))
        for head in range(per_block):
            inner = slice(head * HD, (head + 1) * HD)
            mixed = functools.reduce(
                jnp.add,
                [
                    t[:rows, inner] * turned[:, head * len(tiles) + n : head * len(tiles) + n + 1]
                    for n, t in enumerate(tiles)
                ],
            )
            start = block * width + head * HD
            attention[:, start : start + HD] = mixed.astype(jnp.bfloat16)


def merge_kernel(rows, partner_ref, *refs):
    merge_parts(rows, refs[:-1], partner_ref, refs[-1])


def merge(partner, parts):
    rows, columns = parts[0].shape[0] - EXTRA, parts[0].shape[1]
    vmem = pl.BlockSpec(memory_space=pltpu.VMEM)
    return pl.pallas_call(
        functools.partial(merge_kernel, rows),
        in_specs=[pl.BlockSpec(memory_space=pltpu.SMEM)] + [vmem] * len(parts),
        out_specs=vmem,
        out_shape=jax.ShapeDtypeStruct((rows, columns), jnp.bfloat16),
        compiler_params=pltpu.CompilerParams(vmem_limit_bytes=8 * MIB),
        cost_estimate=pl.CostEstimate(flops=WEIGHTY, bytes_accessed=0, transcendentals=0),
    )(partner, *parts)


def bring(plan, sources, held, sems):
    copies = []
    for source, moves in zip(sources, plan):
        for from_row, size, place, _ in moves:
            copy = pltpu.make_async_copy(
                source.at[pl.ds(from_row, size), :],
                held.at[pl.ds(pl.multiple_of(place(), 16), size), :],
                sems.at[len(copies)],
            )
            copy.start()
            copies.append(copy)
    return copies


def load_kernel(plan, *refs):
    sources, (_, held, sems) = refs[: len(plan)], refs[len(plan) :]
    copies = bring(plan, sources, held, sems)
    for copy in copies:
        copy.wait()


def load(pieces, features, merged):
    arrays, plan = zip(*pieces)
    vmem = pl.BlockSpec(memory_space=pltpu.VMEM)
    return pl.pallas_call(
        functools.partial(load_kernel, plan),
        in_specs=[pl.BlockSpec(memory_space=pl.ANY)] * (len(arrays) + 1),
        out_specs=vmem,
        out_shape=jax.ShapeDtypeStruct((features, arrays[0].shape[1]), arrays[0].dtype),
        scratch_shapes=[pltpu.SemaphoreType.DMA((sum(len(m) for m in plan),))],
        compiler_params=pltpu.CompilerParams(vmem_limit_bytes=16 * MIB),
        cost_estimate=pl.CostEstimate(flops=WEIGHTY, bytes_accessed=0, transcendentals=0),
    )(*arrays, merged)


def project_kernel(plan, count, partner_ref, *refs):
    sources, refs = refs[: len(plan)], refs[len(plan) :]
    parts, (merged, _, out_ref, held, attention, sems) = refs[:count], refs[count:]
    copies = bring(plan, sources, held, sems)
    first = merged.shape[1]
    attention[:, :first] = merged[...]
    merge_parts(attention.shape[0], parts, partner_ref, attention.at[:, first:])
    for copy in copies:
        copy.wait()
    columns = out_ref.shape[1]
    width = math.gcd(columns, 1024)

    @pl.loop(0, columns // width)
    def _(i):
        there = pl.ds(pl.multiple_of(i * width, width), width)
        out_ref[:, there] = jnp.dot(
            attention[...], held[:, there], preferred_element_type=jnp.float32
        ).astype(out_ref.dtype)


def project(pieces, held, partner, parts, merged):
    arrays, plan = zip(*pieces) if pieces else ((), ())
    rows, (features, columns) = merged.shape[0], held.shape
    vmem = pl.BlockSpec(memory_space=pltpu.VMEM)
    given = len(arrays) + len(parts)
    return pl.pallas_call(
        functools.partial(project_kernel, plan, len(parts)),
        in_specs=[pl.BlockSpec(memory_space=pltpu.SMEM)]
        + [pl.BlockSpec(memory_space=pl.ANY)] * len(arrays)
        + [vmem] * (len(parts) + 2),
        out_specs=(vmem, vmem),
        out_shape=(
            jax.ShapeDtypeStruct((rows, columns), jnp.bfloat16),
            jax.ShapeDtypeStruct(held.shape, held.dtype),
        ),
        input_output_aliases={given + 2: 1},
        scratch_shapes=[
            pltpu.VMEM((rows, features), jnp.bfloat16),
            pltpu.SemaphoreType.DMA((max(1, sum(len(m) for m in plan)),)),
        ],
        compiler_params=pltpu.CompilerParams(vmem_limit_bytes=28 * MIB),
    )(partner, *arrays, *parts, merged, held)[0]


def after(value, *done):
    return lax.optimization_barrier((value, *done))[0]


class Cube:
    def __init__(self, out_weight):
        self.shard = out_weight.shape[0]
        self.half = self.shard // 2
        self.list = []

    def add(self, array, *places):
        moves, row = [], 0
        for bit, turn in places:
            count = self.shard if turn is None else self.half

            def place(bit=bit, turn=turn):
                base = (lax.axis_index("seq") ^ bit) * self.shard
                if turn is None:
                    return base
                return base + (lax.axis_index("group") ^ turn) * self.half

            moves.append((row, count, place, bit // 8))
            row += count
        self.list.append((array, moves))

    def steps(self):
        depth = 8 * self.shard
        return [lambda r=r: (lax.axis_index("seq") // 8 ^ r) * depth for r in range(2)]


def body(groups, query_rows, key_rows, value_rows, block_list, out_weight):
    rows, features = query_rows.shape
    heads = features // HD
    devices = lax.axis_size("seq")
    grid_rows = devices // GRID_COLS
    row = lax.axis_index("seq") // GRID_COLS
    chunk_heads = heads // 2
    chunk = chunk_heads * HD
    phases = [parity for parity in range(2) if parity + 1 < grid_rows]
    cube = None
    if devices == 16 and groups == 2 and out_weight.shape[0] % 32 == 0:
        cube = Cube(out_weight)
        first = lax.axis_index("group") * cube.half
        mine = lax.dynamic_slice_in_dim(out_weight, first, cube.half, 0)
        mz = swap_bit(mine, 4)
        my = swap_bit(mine, 2)
        c0 = swap_bit(mine, 8)
    lists = jnp.pad(
        block_list.astype(jnp.bfloat16),
        ((0, EXTRA - FRAMES), (0, HD - block_list.shape[1])),
        constant_values=-1,
    )
    ahead = [mine] if cube else []
    kv = join(after(key_rows, *ahead), value_rows, cost=WEIGHTY).reshape(2, rows, features)
    kv_up = column_shift(kv, 1)
    kv_down = column_shift(kv, -1)
    if cube:
        mz = fence(after(mz, kv, my))
    asking = after(query_rows, kv, *([mz, my] if cube else []))[:, :chunk]
    asking = jnp.concatenate([asking, jnp.tile(lists, (1, chunk_heads))], axis=0)
    sent = []
    for parity in phases:
        pairs = row_pairs(parity)
        first = lax.ppermute(asking, "seq", pairs)
        second = query_rows[:, chunk:]
        if cube:
            second = after(second, first)
            c0 = after(c0, mz)
            cz = swap_bit(c0, 4)
            first = after(first, c0)
            near = join(mz, my, c0, cost=WEIGHTY)
            x0 = swap_group(near, groups)
            second = after(second, near)
            pair = join(mz, after(c0, first))
            y1 = swap_bit(pair, 2)
        sent.append([first, lax.ppermute(second, "seq", pairs)])
    common = (key_rows, value_rows, kv_up, kv_down)
    others = []
    for parity, asked in zip(phases, sent):
        back = []
        for number, q in enumerate(asked):
            if number:
                q = after(q, part, cz) if cube else after(q, part)
            part = attend(asked[0], q, 0, chunk_heads, *common, number * chunk_heads, jnp.bfloat16)
            if cube and not number:
                cz = after(cz, part)
                cy = swap_bit(cz, 2)
                x1 = swap_group(cz, groups)
            back.append(lax.ppermute(part, "seq", row_pairs(parity)))
            last = part
        others.append(back)
    if cube:
        y1, cy = after(y1, last), after(cy, last)
        x2 = swap_group(y1, groups)
        x3 = swap_group(cy, groups)
        base = join(out_weight, near, after(x0, last), cz, after(x1, last))
    own = []
    for number in range(2):
        q, begin = query_rows, number * chunk_heads
        if phases:
            q = after(q, last, *own, *([cy] if cube and number else []))
        own.append(attend(lists, q, begin, chunk_heads, *common, begin, jnp.float32, 0))
    partner = jnp.stack(
        [
            jnp.where(row % 2 == parity, row + 1 < grid_rows, row > 0).astype(jnp.int32)
            for parity in phases
        ]
        or [jnp.int32(0)]
    )
    runs = [[own[n]] + [back[n] for back in others] for n in range(2)]
    merged = merge(partner, runs[0])
    if cube:
        tail = join(y1, after(x2, own[1]), cy, x3)
        at_base = [(0, None), (4, 0), (2, 0), (8, 0), (4, 1), (2, 1), (8, 1), (12, 0), (12, 1)]
        at_tail = [(6, 0), (10, 0), (6, 1), (10, 1), (14, 0), (14, 1)]
        for array, places in ((base, at_base), (tail, at_tail)):
            cube.add(array, *places)
            cube.add(swap_bit(array, 1), *[(bit ^ 1, turn) for bit, turn in places])
        pieces = cube.list
    else:
        gathered = lax.all_gather(out_weight, "seq", axis=0, tiled=True)
        pieces = [(gathered, [(0, gathered.shape[0], lambda: 0, 0)])]
    held = load(pieces[:2], features, merged)
    return project(pieces[2:], held, partner, runs[1], merged)


def solution(mesh):
    placed = (
        P(("group", "seq"), None),
        P(("group", "seq"), None),
        P(("group", "seq"), None),
        P(("group", "seq"), None),
        P("seq", None),
    )
    return jax.shard_map(
        functools.partial(body, mesh.shape["group"]),
        mesh=mesh,
        in_specs=placed,
        out_specs=P(("group", "seq"), None),
        check_vma=False,
    )
```

```python
import functools
import math

import jax
import jax.numpy as jnp
from jax import lax
from jax.experimental import pallas as pl
from jax.experimental.pallas import tpu as pltpu
from jax.sharding import PartitionSpec as P

HD = 128
FRAMES = 2
GRID_COLS = 8
EXTRA = 16
PIECES = 3
LOG2E = math.log2(math.e)
MIB = 1024 * 1024
VMEM_BYTES = 48 * MIB
WEIGHTY = 10**12


def swap_bit(value, bit):
    count = lax.axis_size("seq")
    return lax.ppermute(value, "seq", [(s, s ^ bit) for s in range(count)])


def swap_group(value, groups):
    return lax.ppermute(value, "group", [(s, s ^ 1) for s in range(groups)])


def column_shift(value, steps):
    count = lax.axis_size("seq")
    pairs = [(s, s + steps) for s in range(count) if 0 <= s % GRID_COLS + steps < GRID_COLS]
    return lax.ppermute(value, "seq", pairs)


def row_pairs(parity):
    count = lax.axis_size("seq")
    rows = count // GRID_COLS
    pairs = []
    for s in range(count):
        row = s // GRID_COLS
        other = row + 1 if row % 2 == parity else row - 1
        if 0 <= other < rows:
            pairs.append((s, s + (other - row) * GRID_COLS))
    return pairs


def join_kernel(count, *refs):
    sources, (out_ref, sems) = refs[:count], refs[count:]
    copies, first = [], 0
    for i, source in enumerate(sources):
        size = source.shape[0]
        copy = pltpu.make_async_copy(source, out_ref.at[pl.ds(first, size), :], sems.at[i])
        copy.start()
        copies.append(copy)
        first += size
    for copy in copies:
        copy.wait()


def join(*arrays, cost=0):
    rows = sum(array.shape[0] for array in arrays)
    return pl.pallas_call(
        functools.partial(join_kernel, len(arrays)),
        in_specs=[pl.BlockSpec(memory_space=pl.ANY)] * len(arrays),
        out_specs=pl.BlockSpec(memory_space=pltpu.VMEM),
        out_shape=jax.ShapeDtypeStruct((rows, arrays[0].shape[1]), arrays[0].dtype),
        scratch_shapes=[pltpu.SemaphoreType.DMA((len(arrays),))],
        compiler_params=pltpu.CompilerParams(vmem_limit_bytes=8 * MIB),
        cost_estimate=pl.CostEstimate(flops=cost, bytes_accessed=0, transcendentals=0),
    )(*arrays)


def fence_kernel(in_ref, out_ref):
    out_ref[...] = in_ref[...]


def fence(value, cost=WEIGHTY):
    vmem = pl.BlockSpec(memory_space=pltpu.VMEM)
    return pl.pallas_call(
        fence_kernel,
        in_specs=[vmem],
        out_specs=vmem,
        out_shape=jax.ShapeDtypeStruct(value.shape, value.dtype),
        cost_estimate=pl.CostEstimate(flops=cost, bytes_accessed=0, transcendentals=0),
    )(value)


def attend_kernel(rows, per_block, list_ref, q_ref, k0, ka, kb, v0, va, vb, out_ref):
    factor = HD ** (-0.5) * LOG2E
    tile = rows // FRAMES
    position = lax.axis_index("seq")
    lists = list_ref[...].astype(jnp.float32)
    masks = []
    for step in (0, -1, 1):
        bits = []
        for frame in range(FRAMES):
            tile_id = (position + step) * FRAMES + frame
            tile_id = jnp.where(tile_id >= 0, tile_id, -2).astype(jnp.float32)
            hit = jnp.max(jnp.where(lists == tile_id, 0.0, -jnp.inf), axis=1, keepdims=True)
            bits.append(jnp.broadcast_to(hit, (hit.shape[0], tile)))
        masks.append(jnp.concatenate(bits, axis=1))
    nt = (((1,), (1,)), ((), ()))
    lse = jnp.zeros((rows, HD), jnp.float32)
    lane = lax.broadcasted_iota(jnp.int32, (rows, HD), 1)
    frames = [slice(frame * tile, (frame + 1) * tile) for frame in range(FRAMES)]
    heads = [slice(head * HD, (head + 1) * HD) for head in range(per_block)]
    for head, cols in enumerate(heads):
        keys = [k0[:, cols], ka[0, :, cols], kb[0, :, cols]]
        product = [
            lax.dot_general(q_ref[:rows, cols], key, nt, preferred_element_type=jnp.float32)
            for key in keys
        ]
        values = [v0[:, cols], va[0, :, cols], vb[0, :, cols]]
        peaks, totals, probs = [], [], []
        for frame, here in enumerate(frames):
            scores = [s[here] + mask[frame : frame + 1, :] for s, mask in zip(product, masks)]
            peak = functools.reduce(jnp.maximum, scores)
            peak = jnp.max(peak, axis=1, keepdims=True)
            weights = [jnp.exp2((s - peak) * factor) for s in scores]
            totals.append(jnp.sum(functools.reduce(jnp.add, weights), axis=1, keepdims=True))
            peaks.append(peak)
            probs.append([w.astype(jnp.bfloat16) for w in weights])
        mixed = functools.reduce(
            jnp.add,
            [
                jnp.dot(jnp.concatenate(p, axis=0), v, preferred_element_type=jnp.float32)
                for p, v in zip(zip(*probs), values)
            ],
        )
        total = jnp.concatenate(totals, axis=0)
        out_ref[:rows, cols] = (mixed * (1.0 / total)).astype(out_ref.dtype)
        peak = jnp.concatenate(peaks, axis=0)
        lse = jnp.where(lane == head, peak * factor + jnp.log2(total), lse)
    turned = jnp.transpose(lse)
    stats = []
    for head in range(per_block):
        rest = turned[head : head + 1, :]
        for _ in range(PIECES):
            piece = rest.astype(out_ref.dtype)
            stats.append(piece.astype(jnp.float32))
            rest = rest - stats[-1]
    stats.append(jnp.zeros((EXTRA - len(stats), rows), jnp.float32))
    out_ref[rows:, :] = jnp.concatenate(stats, axis=0).astype(out_ref.dtype)


def attend(lists, q, q_first, heads, keys, values, kv_up, kv_down, first, kind, cost=WEIGHTY):
    rows = keys.shape[0]
    per_block = rows // HD
    width = per_block * HD
    lo, q_lo = first * HD // width, q_first * HD // width
    here = pl.BlockSpec((rows, width), lambda i: (0, lo + i))
    key_spec = pl.BlockSpec((1, rows, width), lambda i: (0, 0, lo + i))
    value_spec = pl.BlockSpec((1, rows, width), lambda i: (1, 0, lo + i))
    span = 3 * rows
    return pl.pallas_call(
        functools.partial(attend_kernel, rows, per_block),
        grid=(heads // per_block,),
        in_specs=[
            pl.BlockSpec((EXTRA, HD), lambda i: (lists.shape[0] // EXTRA - 1, 0)),
            pl.BlockSpec((rows, width), lambda i: (0, q_lo + i)),
            here,
            key_spec,
            key_spec,
            here,
            value_spec,
            value_spec,
        ],
        out_specs=pl.BlockSpec((rows + EXTRA, width), lambda i: (0, i)),
        out_shape=jax.ShapeDtypeStruct((rows + EXTRA, heads * HD), kind),
        compiler_params=pltpu.CompilerParams(vmem_limit_bytes=12 * MIB),
        cost_estimate=pl.CostEstimate(
            flops=cost, bytes_accessed=0, transcendentals=0
        ),
    )(lists, q, keys, kv_up, kv_down, values, kv_up, kv_down)


def merge_parts(rows, parts, partner_ref, attention):
    per_block = rows // HD
    width = per_block * HD
    for block in range(attention.shape[1] // width):
        tiles = []
        for part in parts:
            tiles.append(part[:, block * width : (block + 1) * width].astype(jnp.float32))
        shares = []
        for head in range(per_block):
            lses = []
            for number, t in enumerate(tiles):
                row = rows + PIECES * head
                lse = functools.reduce(
                    jnp.add, [t[row + i : row + i + 1, :] for i in range(PIECES)]
                )
                if number:
                    lse = jnp.where(partner_ref[number - 1] == 1, lse, -jnp.inf)
                lses.append(lse)
            top = functools.reduce(jnp.maximum, lses)
            raw = [jnp.exp2(lse - top) for lse in lses]
            total = functools.reduce(jnp.add, raw)
            shares.extend(r / total for r in raw)
        shares.append(jnp.zeros((HD - len(shares), rows), jnp.float32))
        turned = jnp.transpose(jnp.concatenate(shares, axis=0))
        for head in range(per_block):
            inner = slice(head * HD, (head + 1) * HD)
            mixed = functools.reduce(
                jnp.add,
                [
                    t[:rows, inner] * turned[:, head * len(tiles) + n : head * len(tiles) + n + 1]
                    for n, t in enumerate(tiles)
                ],
            )
            start = block * width + head * HD
            attention[:, start : start + HD] = mixed.astype(jnp.bfloat16)


def merge_kernel(rows, partner_ref, *refs):
    merge_parts(rows, refs[:-1], partner_ref, refs[-1])


def merge(partner, parts):
    rows, columns = parts[0].shape[0] - EXTRA, parts[0].shape[1]
    vmem = pl.BlockSpec(memory_space=pltpu.VMEM)
    return pl.pallas_call(
        functools.partial(merge_kernel, rows),
        in_specs=[pl.BlockSpec(memory_space=pltpu.SMEM)] + [vmem] * len(parts),
        out_specs=vmem,
        out_shape=jax.ShapeDtypeStruct((rows, columns), jnp.bfloat16),
        compiler_params=pltpu.CompilerParams(vmem_limit_bytes=8 * MIB),
        cost_estimate=pl.CostEstimate(flops=WEIGHTY, bytes_accessed=0, transcendentals=0),
    )(partner, *parts)


def bring(plan, sources, held, sems):
    copies = []
    for source, moves in zip(sources, plan):
        for from_row, size, place, _ in moves:
            copy = pltpu.make_async_copy(
                source.at[pl.ds(from_row, size), :],
                held.at[pl.ds(pl.multiple_of(place(), 16), size), :],
                sems.at[len(copies)],
            )
            copy.start()
            copies.append(copy)
    return copies


def load_kernel(plan, *refs):
    sources, (_, held, sems) = refs[: len(plan)], refs[len(plan) :]
    copies = bring(plan, sources, held, sems)
    for copy in copies:
        copy.wait()


def load(pieces, features, merged):
    arrays, plan = zip(*pieces)
    vmem = pl.BlockSpec(memory_space=pltpu.VMEM)
    return pl.pallas_call(
        functools.partial(load_kernel, plan),
        in_specs=[pl.BlockSpec(memory_space=pl.ANY)] * (len(arrays) + 1),
        out_specs=vmem,
        out_shape=jax.ShapeDtypeStruct((features, arrays[0].shape[1]), arrays[0].dtype),
        scratch_shapes=[pltpu.SemaphoreType.DMA((sum(len(m) for m in plan),))],
        compiler_params=pltpu.CompilerParams(vmem_limit_bytes=16 * MIB),
        cost_estimate=pl.CostEstimate(flops=WEIGHTY, bytes_accessed=0, transcendentals=0),
    )(*arrays, merged)


def project_kernel(plan, count, partner_ref, *refs):
    sources, refs = refs[: len(plan)], refs[len(plan) :]
    parts, (merged, _, out_ref, held, attention, sems) = refs[:count], refs[count:]
    copies = bring(plan, sources, held, sems)
    first = merged.shape[1]
    attention[:, :first] = merged[...]
    merge_parts(attention.shape[0], parts, partner_ref, attention.at[:, first:])
    for copy in copies:
        copy.wait()
    columns = out_ref.shape[1]
    width = math.gcd(columns, 1536)

    @pl.loop(0, columns // width)
    def _(i):
        there = pl.ds(pl.multiple_of(i * width, width), width)
        out_ref[:, there] = jnp.dot(
            attention[...], held[:, there], preferred_element_type=jnp.float32
        ).astype(out_ref.dtype)


def project(pieces, held, partner, parts, merged):
    arrays, plan = zip(*pieces) if pieces else ((), ())
    rows, (features, columns) = merged.shape[0], held.shape
    vmem = pl.BlockSpec(memory_space=pltpu.VMEM)
    given = len(arrays) + len(parts)
    return pl.pallas_call(
        functools.partial(project_kernel, plan, len(parts)),
        in_specs=[pl.BlockSpec(memory_space=pltpu.SMEM)]
        + [pl.BlockSpec(memory_space=pl.ANY)] * len(arrays)
        + [vmem] * (len(parts) + 2),
        out_specs=(vmem, vmem),
        out_shape=(
            jax.ShapeDtypeStruct((rows, columns), jnp.bfloat16),
            jax.ShapeDtypeStruct(held.shape, held.dtype),
        ),
        input_output_aliases={given + 2: 1},
        scratch_shapes=[
            pltpu.VMEM((rows, features), jnp.bfloat16),
            pltpu.SemaphoreType.DMA((max(1, sum(len(m) for m in plan)),)),
        ],
        compiler_params=pltpu.CompilerParams(vmem_limit_bytes=28 * MIB),
    )(partner, *arrays, *parts, merged, held)[0]


def after(value, *done):
    return lax.optimization_barrier((value, *done))[0]


class Cube:
    def __init__(self, out_weight):
        self.shard = out_weight.shape[0]
        self.half = self.shard // 2
        self.list = []

    def add(self, array, *places):
        moves, row = [], 0
        for bit, turn in places:
            count = self.shard if turn is None else self.half

            def place(bit=bit, turn=turn):
                base = (lax.axis_index("seq") ^ bit) * self.shard
                if turn is None:
                    return base
                return base + (lax.axis_index("group") ^ turn) * self.half

            moves.append((row, count, place, bit // 8))
            row += count
        self.list.append((array, moves))

    def steps(self):
        depth = 8 * self.shard
        return [lambda r=r: (lax.axis_index("seq") // 8 ^ r) * depth for r in range(2)]


def body(groups, query_rows, key_rows, value_rows, block_list, out_weight):
    rows, features = query_rows.shape
    heads = features // HD
    devices = lax.axis_size("seq")
    grid_rows = devices // GRID_COLS
    row = lax.axis_index("seq") // GRID_COLS
    chunk_heads = heads // 2
    chunk = chunk_heads * HD
    phases = [parity for parity in range(2) if parity + 1 < grid_rows]
    cube = None
    if devices == 16 and groups == 2 and out_weight.shape[0] % 32 == 0:
        cube = Cube(out_weight)
        first = lax.axis_index("group") * cube.half
        mine = lax.dynamic_slice_in_dim(out_weight, first, cube.half, 0)
        mz = swap_bit(mine, 4)
        my = swap_bit(mine, 2)
        c0 = swap_bit(mine, 8)
    lists = jnp.pad(
        block_list.astype(jnp.bfloat16),
        ((0, EXTRA - FRAMES), (0, HD - block_list.shape[1])),
        constant_values=-1,
    )
    ahead = [mine] if cube else []
    kv = join(after(key_rows, *ahead), value_rows, cost=WEIGHTY).reshape(2, rows, features)
    kv_up = column_shift(kv, 1)
    kv_down = column_shift(kv, -1)
    asking = jnp.concatenate(
        [after(query_rows, kv)[:, :chunk], jnp.tile(lists, (1, chunk_heads))], axis=0
    )
    if cube:
        lists = fence(after(lists, asking, mz, my))
    sent = []
    for parity in phases:
        pairs = row_pairs(parity)
        first = lax.ppermute(asking, "seq", pairs)
        second = query_rows[:, chunk:]
        if cube:
            second = after(second, first)
            c0 = after(c0, lists)
            cz = swap_bit(after(c0, first), 4)
            first = after(first, c0)
            near = join(mz, my, c0, cost=WEIGHTY)
            x0 = swap_group(near, groups)
            second = after(second, near)
            pair = join(mz, after(c0, first))
            y1 = swap_bit(pair, 2)
        sent.append([first, lax.ppermute(second, "seq", pairs)])
    common = (key_rows, value_rows, kv_up, kv_down)
    others = []
    for parity, asked in zip(phases, sent):
        back = []
        for number, q in enumerate(asked):
            if number:
                q = after(q, part, cz) if cube else after(q, part)
            part = attend(asked[0], q, 0, chunk_heads, *common, number * chunk_heads, jnp.bfloat16)
            if cube and not number:
                cz = after(cz, part)
                cy = swap_bit(cz, 2)
                x1 = swap_group(cz, groups)
            sending = part if number else fence(after(part, asked[1]), 0)
            back.append(lax.ppermute(sending, "seq", row_pairs(parity)))
            last = part
        others.append(back)
    if cube:
        y1, cy = after(y1, last), after(cy, last)
        x2 = swap_group(y1, groups)
        x3 = swap_group(cy, groups)
        base = join(out_weight, near, after(x0, last), cz, after(x1, last))
    own = []
    for number in range(2):
        q, begin = query_rows, number * chunk_heads
        if phases:
            q = after(q, last, *own, *([cy] if cube and number else []))
        own.append(attend(lists, q, begin, chunk_heads, *common, begin, jnp.float32, 0))
    partner = jnp.stack(
        [
            jnp.where(row % 2 == parity, row + 1 < grid_rows, row > 0).astype(jnp.int32)
            for parity in phases
        ]
        or [jnp.int32(0)]
    )
    runs = [[own[n]] + [back[n] for back in others] for n in range(2)]
    merged = merge(partner, runs[0])
    if cube:
        tail = join(y1, after(x2, own[1]), cy, x3)
        at_base = [(0, None), (4, 0), (2, 0), (8, 0), (4, 1), (2, 1), (8, 1), (12, 0), (12, 1)]
        at_tail = [(6, 0), (10, 0), (6, 1), (10, 1), (14, 0), (14, 1)]
        for array, places in ((base, at_base), (tail, at_tail)):
            cube.add(array, *places)
            cube.add(swap_bit(array, 1), *[(bit ^ 1, turn) for bit, turn in places])
        pieces = cube.list
    else:
        gathered = lax.all_gather(out_weight, "seq", axis=0, tiled=True)
        pieces = [(gathered, [(0, gathered.shape[0], lambda: 0, 0)])]
    held = load(pieces[:2], features, merged)
    return project(pieces[2:], held, partner, runs[1], merged)


def solution(mesh):
    placed = (
        P(("group", "seq"), None),
        P(("group", "seq"), None),
        P(("group", "seq"), None),
        P(("group", "seq"), None),
        P("seq", None),
    )
    return jax.shard_map(
        functools.partial(body, mesh.shape["group"]),
        mesh=mesh,
        in_specs=placed,
        out_specs=P(("group", "seq"), None),
        check_vma=False,
    )
```

```python
import functools
import math

import jax
import jax.numpy as jnp
from jax import lax
from jax.experimental import pallas as pl
from jax.experimental.pallas import tpu as pltpu
from jax.sharding import PartitionSpec as P

HD = 128
FRAMES = 2
GRID_COLS = 8
EXTRA = 16
STATS = 8
PIECES = 3
LOG2E = math.log2(math.e)
MIB = 1024 * 1024
VMEM_BYTES = 48 * MIB
WEIGHTY = 10**12


def swap_bit(value, bit):
    count = lax.axis_size("seq")
    return lax.ppermute(value, "seq", [(s, s ^ bit) for s in range(count)])


def swap_group(value, groups):
    return lax.ppermute(value, "group", [(s, s ^ 1) for s in range(groups)])


def column_shift(value, steps):
    count = lax.axis_size("seq")
    pairs = [(s, s + steps) for s in range(count) if 0 <= s % GRID_COLS + steps < GRID_COLS]
    return lax.ppermute(value, "seq", pairs)


def row_pairs(parity):
    count = lax.axis_size("seq")
    rows = count // GRID_COLS
    pairs = []
    for s in range(count):
        row = s // GRID_COLS
        other = row + 1 if row % 2 == parity else row - 1
        if 0 <= other < rows:
            pairs.append((s, s + (other - row) * GRID_COLS))
    return pairs


def join_kernel(count, *refs):
    sources, (out_ref, sems) = refs[:count], refs[count:]
    copies, first = [], 0
    for i, source in enumerate(sources):
        size = source.shape[0]
        copy = pltpu.make_async_copy(source, out_ref.at[pl.ds(first, size), :], sems.at[i])
        copy.start()
        copies.append(copy)
        first += size
    for copy in copies:
        copy.wait()


def join(*arrays, cost=0):
    rows = sum(array.shape[0] for array in arrays)
    return pl.pallas_call(
        functools.partial(join_kernel, len(arrays)),
        in_specs=[pl.BlockSpec(memory_space=pl.ANY)] * len(arrays),
        out_specs=pl.BlockSpec(memory_space=pltpu.VMEM),
        out_shape=jax.ShapeDtypeStruct((rows, arrays[0].shape[1]), arrays[0].dtype),
        scratch_shapes=[pltpu.SemaphoreType.DMA((len(arrays),))],
        compiler_params=pltpu.CompilerParams(vmem_limit_bytes=8 * MIB),
        cost_estimate=pl.CostEstimate(flops=cost, bytes_accessed=0, transcendentals=0),
    )(*arrays)


def fence_kernel(in_ref, out_ref):
    out_ref[...] = in_ref[...]


def fence(value, cost=WEIGHTY):
    vmem = pl.BlockSpec(memory_space=pltpu.VMEM)
    return pl.pallas_call(
        fence_kernel,
        in_specs=[vmem],
        out_specs=vmem,
        out_shape=jax.ShapeDtypeStruct(value.shape, value.dtype),
        cost_estimate=pl.CostEstimate(flops=cost, bytes_accessed=0, transcendentals=0),
    )(value)


def attend_kernel(rows, per_block, list_ref, q_ref, k0, ka, kb, v0, va, vb, out_ref):
    factor = HD ** (-0.5) * LOG2E
    tile = rows // FRAMES
    position = lax.axis_index("seq")
    lists = list_ref[...].astype(jnp.float32)
    masks = []
    for step in (0, -1, 1):
        bits = []
        for frame in range(FRAMES):
            tile_id = (position + step) * FRAMES + frame
            tile_id = jnp.where(tile_id >= 0, tile_id, -2).astype(jnp.float32)
            hit = jnp.max(jnp.where(lists == tile_id, 0.0, -jnp.inf), axis=1, keepdims=True)
            bits.append(jnp.broadcast_to(hit, (hit.shape[0], tile)))
        masks.append(jnp.concatenate(bits, axis=1))
    nt = (((1,), (1,)), ((), ()))
    lse = jnp.zeros((rows, HD), jnp.float32)
    lane = lax.broadcasted_iota(jnp.int32, (rows, HD), 1)
    frames = [slice(frame * tile, (frame + 1) * tile) for frame in range(FRAMES)]
    heads = [slice(head * HD, (head + 1) * HD) for head in range(per_block)]
    for head, cols in enumerate(heads):
        keys = [k0[:, cols], ka[0, :, cols], kb[0, :, cols]]
        product = [
            lax.dot_general(q_ref[:rows, cols], key, nt, preferred_element_type=jnp.float32)
            for key in keys
        ]
        values = [v0[:, cols], va[0, :, cols], vb[0, :, cols]]
        peaks, totals, probs = [], [], []
        for frame, here in enumerate(frames):
            scores = [s[here] + mask[frame : frame + 1, :] for s, mask in zip(product, masks)]
            peak = functools.reduce(jnp.maximum, scores)
            peak = jnp.max(peak, axis=1, keepdims=True)
            weights = [jnp.exp2((s - peak) * factor) for s in scores]
            totals.append(jnp.sum(functools.reduce(jnp.add, weights), axis=1, keepdims=True))
            peaks.append(peak)
            probs.append([w.astype(jnp.bfloat16) for w in weights])
        mixed = functools.reduce(
            jnp.add,
            [
                jnp.dot(jnp.concatenate(p, axis=0), v, preferred_element_type=jnp.float32)
                for p, v in zip(zip(*probs), values)
            ],
        )
        total = jnp.concatenate(totals, axis=0)
        out_ref[:rows, cols] = (mixed * (1.0 / total)).astype(out_ref.dtype)
        peak = jnp.concatenate(peaks, axis=0)
        lse = jnp.where(lane == head, peak * factor + jnp.log2(total), lse)
    turned = jnp.transpose(lse)
    stats = []
    for head in range(per_block):
        rest = turned[head : head + 1, :]
        for _ in range(PIECES):
            piece = rest.astype(out_ref.dtype)
            stats.append(piece.astype(jnp.float32))
            rest = rest - stats[-1]
    stats.append(jnp.zeros((STATS - len(stats), rows), jnp.float32))
    out_ref[rows:, :] = jnp.concatenate(stats, axis=0).astype(out_ref.dtype)


def attend(lists, q, q_first, heads, keys, values, kv_up, kv_down, first, kind, cost=WEIGHTY):
    rows = keys.shape[0]
    per_block = rows // HD
    width = per_block * HD
    lo, q_lo = first * HD // width, q_first * HD // width
    here = pl.BlockSpec((rows, width), lambda i: (0, lo + i))
    key_spec = pl.BlockSpec((1, rows, width), lambda i: (0, 0, lo + i))
    value_spec = pl.BlockSpec((1, rows, width), lambda i: (1, 0, lo + i))
    span = 3 * rows
    return pl.pallas_call(
        functools.partial(attend_kernel, rows, per_block),
        grid=(heads // per_block,),
        in_specs=[
            pl.BlockSpec((EXTRA, HD), lambda i: (lists.shape[0] // EXTRA - 1, 0)),
            pl.BlockSpec((rows, width), lambda i: (0, q_lo + i)),
            here,
            key_spec,
            key_spec,
            here,
            value_spec,
            value_spec,
        ],
        out_specs=pl.BlockSpec((rows + STATS, width), lambda i: (0, i)),
        out_shape=jax.ShapeDtypeStruct((rows + STATS, heads * HD), kind),
        compiler_params=pltpu.CompilerParams(vmem_limit_bytes=12 * MIB),
        cost_estimate=pl.CostEstimate(
            flops=cost, bytes_accessed=0, transcendentals=0
        ),
    )(lists, q, keys, kv_up, kv_down, values, kv_up, kv_down)


def merge_parts(rows, parts, partner_ref, attention):
    per_block = rows // HD
    width = per_block * HD
    for block in range(attention.shape[1] // width):
        tiles = []
        for part in parts:
            tiles.append(part[:, block * width : (block + 1) * width].astype(jnp.float32))
        shares = []
        for head in range(per_block):
            lses = []
            for number, t in enumerate(tiles):
                row = rows + PIECES * head
                lse = functools.reduce(
                    jnp.add, [t[row + i : row + i + 1, :] for i in range(PIECES)]
                )
                if number:
                    lse = jnp.where(partner_ref[number - 1] == 1, lse, -jnp.inf)
                lses.append(lse)
            top = functools.reduce(jnp.maximum, lses)
            raw = [jnp.exp2(lse - top) for lse in lses]
            total = functools.reduce(jnp.add, raw)
            shares.extend(r / total for r in raw)
        shares.append(jnp.zeros((HD - len(shares), rows), jnp.float32))
        turned = jnp.transpose(jnp.concatenate(shares, axis=0))
        for head in range(per_block):
            inner = slice(head * HD, (head + 1) * HD)
            mixed = functools.reduce(
                jnp.add,
                [
                    t[:rows, inner] * turned[:, head * len(tiles) + n : head * len(tiles) + n + 1]
                    for n, t in enumerate(tiles)
                ],
            )
            start = block * width + head * HD
            attention[:, start : start + HD] = mixed.astype(jnp.bfloat16)


def merge_kernel(rows, partner_ref, *refs):
    merge_parts(rows, refs[:-1], partner_ref, refs[-1])


def merge(partner, parts):
    rows, columns = parts[0].shape[0] - STATS, parts[0].shape[1]
    vmem = pl.BlockSpec(memory_space=pltpu.VMEM)
    return pl.pallas_call(
        functools.partial(merge_kernel, rows),
        in_specs=[pl.BlockSpec(memory_space=pltpu.SMEM)] + [vmem] * len(parts),
        out_specs=vmem,
        out_shape=jax.ShapeDtypeStruct((rows, columns), jnp.bfloat16),
        compiler_params=pltpu.CompilerParams(vmem_limit_bytes=8 * MIB),
        cost_estimate=pl.CostEstimate(flops=WEIGHTY, bytes_accessed=0, transcendentals=0),
    )(partner, *parts)


def bring(plan, sources, held, sems):
    copies = []
    for source, moves in zip(sources, plan):
        for from_row, size, place, _ in moves:
            copy = pltpu.make_async_copy(
                source.at[pl.ds(from_row, size), :],
                held.at[pl.ds(pl.multiple_of(place(), 16), size), :],
                sems.at[len(copies)],
            )
            copy.start()
            copies.append(copy)
    return copies


def load_kernel(plan, *refs):
    sources, (_, held, sems) = refs[: len(plan)], refs[len(plan) :]
    copies = bring(plan, sources, held, sems)
    for copy in copies:
        copy.wait()


def load(pieces, features, merged):
    arrays, plan = zip(*pieces)
    vmem = pl.BlockSpec(memory_space=pltpu.VMEM)
    return pl.pallas_call(
        functools.partial(load_kernel, plan),
        in_specs=[pl.BlockSpec(memory_space=pl.ANY)] * (len(arrays) + 1),
        out_specs=vmem,
        out_shape=jax.ShapeDtypeStruct((features, arrays[0].shape[1]), arrays[0].dtype),
        scratch_shapes=[pltpu.SemaphoreType.DMA((sum(len(m) for m in plan),))],
        compiler_params=pltpu.CompilerParams(vmem_limit_bytes=16 * MIB),
        cost_estimate=pl.CostEstimate(flops=WEIGHTY, bytes_accessed=0, transcendentals=0),
    )(*arrays, merged)


def project_kernel(plan, count, partner_ref, *refs):
    sources, refs = refs[: len(plan)], refs[len(plan) :]
    parts, refs = refs[:count], refs[count:]
    merged, _, out_ref, held, attention, staged, sems, out_sems = refs
    copies = bring(plan, sources, held, sems)
    first = merged.shape[1]
    attention[:, :first] = merged[...]
    merge_parts(attention.shape[0], parts, partner_ref, attention.at[:, first:])
    for copy in copies:
        copy.wait()
    columns = out_ref.shape[1]
    width = staged.shape[2]

    written = []
    for i in range(columns // width):
        there = pl.ds(i * width, width)
        staged[i] = jnp.dot(
            attention[...], held[:, there], preferred_element_type=jnp.float32
        ).astype(out_ref.dtype)
        copy = pltpu.make_async_copy(staged.at[i], out_ref.at[:, there], out_sems.at[i])
        copy.start()
        written.append(copy)
    for copy in written:
        copy.wait()


def project(pieces, held, partner, parts, merged):
    arrays, plan = zip(*pieces) if pieces else ((), ())
    rows, (features, columns) = merged.shape[0], held.shape
    vmem = pl.BlockSpec(memory_space=pltpu.VMEM)
    given = len(arrays) + len(parts)
    width = math.gcd(columns, 768)
    return pl.pallas_call(
        functools.partial(project_kernel, plan, len(parts)),
        in_specs=[pl.BlockSpec(memory_space=pltpu.SMEM)]
        + [pl.BlockSpec(memory_space=pl.ANY)] * len(arrays)
        + [vmem] * (len(parts) + 2),
        out_specs=(pl.BlockSpec(memory_space=pl.ANY), vmem),
        out_shape=(
            jax.ShapeDtypeStruct((rows, columns), jnp.bfloat16),
            jax.ShapeDtypeStruct(held.shape, held.dtype),
        ),
        input_output_aliases={given + 2: 1},
        scratch_shapes=[
            pltpu.VMEM((rows, features), jnp.bfloat16),
            pltpu.VMEM((columns // width, rows, width), jnp.bfloat16),
            pltpu.SemaphoreType.DMA((max(1, sum(len(m) for m in plan)),)),
            pltpu.SemaphoreType.DMA((columns // width,)),
        ],
        compiler_params=pltpu.CompilerParams(vmem_limit_bytes=28 * MIB),
    )(partner, *arrays, *parts, merged, held)[0]


def after(value, *done):
    return lax.optimization_barrier((value, *done))[0]


class Cube:
    def __init__(self, out_weight):
        self.shard = out_weight.shape[0]
        self.half = self.shard // 2
        self.list = []

    def add(self, array, *places):
        moves, row = [], 0
        for bit, turn in places:
            count = self.shard if turn is None else self.half

            def place(bit=bit, turn=turn):
                base = (lax.axis_index("seq") ^ bit) * self.shard
                if turn is None:
                    return base
                return base + (lax.axis_index("group") ^ turn) * self.half

            moves.append((row, count, place, bit // 8))
            row += count
        self.list.append((array, moves))

    def steps(self):
        depth = 8 * self.shard
        return [lambda r=r: (lax.axis_index("seq") // 8 ^ r) * depth for r in range(2)]


def body(groups, query_rows, key_rows, value_rows, block_list, out_weight):
    rows, features = query_rows.shape
    heads = features // HD
    devices = lax.axis_size("seq")
    grid_rows = devices // GRID_COLS
    row = lax.axis_index("seq") // GRID_COLS
    chunk_heads = heads // 2
    chunk = chunk_heads * HD
    phases = [parity for parity in range(2) if parity + 1 < grid_rows]
    cube = None
    if devices == 16 and groups == 2 and out_weight.shape[0] % 32 == 0:
        cube = Cube(out_weight)
        first = lax.axis_index("group") * cube.half
        mine = lax.dynamic_slice_in_dim(out_weight, first, cube.half, 0)
        mz = swap_bit(mine, 4)
        my = swap_bit(mine, 2)
        c0 = swap_bit(mine, 8)
    lists = jnp.pad(
        block_list.astype(jnp.bfloat16),
        ((0, EXTRA - FRAMES), (0, HD - block_list.shape[1])),
        constant_values=-1,
    )
    ahead = [mine] if cube else []
    kv = join(after(key_rows, *ahead), value_rows, cost=WEIGHTY).reshape(2, rows, features)
    kv_up = column_shift(kv, 1)
    kv_down = column_shift(kv, -1)
    asking = jnp.concatenate(
        [after(query_rows, kv)[:, :chunk], jnp.tile(lists, (1, chunk_heads))], axis=0
    )
    if cube:
        lists = fence(after(lists, asking, mz, my))
    sent = []
    for parity in phases:
        pairs = row_pairs(parity)
        first = lax.ppermute(asking, "seq", pairs)
        second = query_rows[:, chunk:]
        if cube:
            second = after(second, first)
            c0 = after(c0, lists)
            cz = swap_bit(after(c0, first), 4)
            first = after(first, c0)
            near = join(mz, my, c0, cost=WEIGHTY)
            x0 = swap_group(near, groups)
            second = after(second, near)
            pair = join(mz, after(c0, first))
            y1 = swap_bit(pair, 2)
        sent.append([first, lax.ppermute(second, "seq", pairs)])
    common = (key_rows, value_rows, kv_up, kv_down)
    others = []
    for parity, asked in zip(phases, sent):
        back = []
        for number, q in enumerate(asked):
            if number:
                q = after(q, part, cz) if cube else after(q, part)
            part = attend(asked[0], q, 0, chunk_heads, *common, number * chunk_heads, jnp.bfloat16)
            if cube and not number:
                cz = after(cz, part)
                cy = swap_bit(cz, 2)
                x1 = swap_group(cz, groups)
            sending = part if number else fence(after(part, asked[1]), 0)
            back.append(lax.ppermute(sending, "seq", row_pairs(parity)))
            last = part
        others.append(back)
    if cube:
        y1, cy = after(y1, last), after(cy, last)
        x2 = swap_group(y1, groups)
        x3 = swap_group(cy, groups)
        base = join(out_weight, near, after(x0, last), cz, after(x1, last))
    own = []
    for number in range(2):
        q, begin = query_rows, number * chunk_heads
        if phases:
            q = after(q, last, *own, *([cy] if cube and number else []))
        own.append(attend(lists, q, begin, chunk_heads, *common, begin, jnp.float32, 0))
    partner = jnp.stack(
        [
            jnp.where(row % 2 == parity, row + 1 < grid_rows, row > 0).astype(jnp.int32)
            for parity in phases
        ]
        or [jnp.int32(0)]
    )
    runs = [[own[n]] + [back[n] for back in others] for n in range(2)]
    merged = merge(partner, runs[0])
    if cube:
        tail = join(y1, after(x2, own[1]), cy, x3)
        at_base = [(0, None), (4, 0), (2, 0), (8, 0), (4, 1), (2, 1), (8, 1), (12, 0), (12, 1)]
        at_tail = [(6, 0), (10, 0), (6, 1), (10, 1), (14, 0), (14, 1)]
        for array, places in ((base, at_base), (tail, at_tail)):
            cube.add(array, *places)
            cube.add(swap_bit(array, 1), *[(bit ^ 1, turn) for bit, turn in places])
        pieces = cube.list
    else:
        gathered = lax.all_gather(out_weight, "seq", axis=0, tiled=True)
        pieces = [(gathered, [(0, gathered.shape[0], lambda: 0, 0)])]
    held = load(pieces[:2], features, merged)
    return project(pieces[2:], held, partner, runs[1], merged)


def solution(mesh):
    placed = (
        P(("group", "seq"), None),
        P(("group", "seq"), None),
        P(("group", "seq"), None),
        P(("group", "seq"), None),
        P("seq", None),
    )
    return jax.shard_map(
        functools.partial(body, mesh.shape["group"]),
        mesh=mesh,
        in_specs=placed,
        out_specs=P(("group", "seq"), None),
        check_vma=False,
    )
```

```python
import functools
import math

import jax
import jax.numpy as jnp
from jax import lax
from jax.experimental import pallas as pl
from jax.experimental.pallas import tpu as pltpu
from jax.sharding import PartitionSpec as P

HD = 128
FRAMES = 2
GRID_COLS = 8
EXTRA = 16
STATS = 8
PIECES = 3
LOG2E = math.log2(math.e)
MIB = 1024 * 1024
VMEM_BYTES = 48 * MIB
WEIGHTY = 10**12


def swap_bit(value, bit):
    count = lax.axis_size("seq")
    return lax.ppermute(value, "seq", [(s, s ^ bit) for s in range(count)])


def swap_group(value, groups):
    return lax.ppermute(value, "group", [(s, s ^ 1) for s in range(groups)])


def column_shift(value, steps):
    count = lax.axis_size("seq")
    pairs = [(s, s + steps) for s in range(count) if 0 <= s % GRID_COLS + steps < GRID_COLS]
    return lax.ppermute(value, "seq", pairs)


def row_pairs(parity):
    count = lax.axis_size("seq")
    rows = count // GRID_COLS
    pairs = []
    for s in range(count):
        row = s // GRID_COLS
        other = row + 1 if row % 2 == parity else row - 1
        if 0 <= other < rows:
            pairs.append((s, s + (other - row) * GRID_COLS))
    return pairs


def join_kernel(count, *refs):
    sources, (out_ref, sems) = refs[:count], refs[count:]
    copies, first = [], 0
    for i, source in enumerate(sources):
        size = source.shape[0]
        copy = pltpu.make_async_copy(source, out_ref.at[pl.ds(first, size), :], sems.at[i])
        copy.start()
        copies.append(copy)
        first += size
    for copy in copies:
        copy.wait()


def join(*arrays, cost=0):
    rows = sum(array.shape[0] for array in arrays)
    return pl.pallas_call(
        functools.partial(join_kernel, len(arrays)),
        in_specs=[pl.BlockSpec(memory_space=pl.ANY)] * len(arrays),
        out_specs=pl.BlockSpec(memory_space=pltpu.VMEM),
        out_shape=jax.ShapeDtypeStruct((rows, arrays[0].shape[1]), arrays[0].dtype),
        scratch_shapes=[pltpu.SemaphoreType.DMA((len(arrays),))],
        compiler_params=pltpu.CompilerParams(vmem_limit_bytes=8 * MIB),
        cost_estimate=pl.CostEstimate(flops=cost, bytes_accessed=0, transcendentals=0),
    )(*arrays)


def fence_kernel(in_ref, out_ref):
    out_ref[...] = in_ref[...]


def fence(value, cost=WEIGHTY):
    vmem = pl.BlockSpec(memory_space=pltpu.VMEM)
    return pl.pallas_call(
        fence_kernel,
        in_specs=[vmem],
        out_specs=vmem,
        out_shape=jax.ShapeDtypeStruct(value.shape, value.dtype),
        cost_estimate=pl.CostEstimate(flops=cost, bytes_accessed=0, transcendentals=0),
    )(value)


def attend_kernel(rows, per_block, list_ref, q_ref, k0, ka, kb, v0, va, vb, out_ref):
    factor = HD ** (-0.5) * LOG2E
    tile = rows // FRAMES
    position = lax.axis_index("seq")
    lists = list_ref[...].astype(jnp.float32)
    masks = []
    for step in (0, -1, 1):
        bits = []
        for frame in range(FRAMES):
            tile_id = (position + step) * FRAMES + frame
            tile_id = jnp.where(tile_id >= 0, tile_id, -2).astype(jnp.float32)
            hit = jnp.max(jnp.where(lists == tile_id, 0.0, -jnp.inf), axis=1, keepdims=True)
            bits.append(jnp.broadcast_to(hit, (hit.shape[0], tile)))
        masks.append(jnp.concatenate(bits, axis=1))
    nt = (((1,), (1,)), ((), ()))
    lse = jnp.zeros((rows, HD), jnp.float32)
    lane = lax.broadcasted_iota(jnp.int32, (rows, HD), 1)
    frames = [slice(frame * tile, (frame + 1) * tile) for frame in range(FRAMES)]
    heads = [slice(head * HD, (head + 1) * HD) for head in range(per_block)]
    for head, cols in enumerate(heads):
        keys = [k0[:, cols], ka[0, :, cols], kb[0, :, cols]]
        product = [
            lax.dot_general(q_ref[:rows, cols], key, nt, preferred_element_type=jnp.float32)
            for key in keys
        ]
        values = [v0[:, cols], va[0, :, cols], vb[0, :, cols]]
        peaks, totals, probs = [], [], []
        for frame, here in enumerate(frames):
            scores = [s[here] + mask[frame : frame + 1, :] for s, mask in zip(product, masks)]
            peak = functools.reduce(jnp.maximum, scores)
            peak = jnp.max(peak, axis=1, keepdims=True)
            weights = [jnp.exp2((s - peak) * factor) for s in scores]
            totals.append(jnp.sum(functools.reduce(jnp.add, weights), axis=1, keepdims=True))
            peaks.append(peak)
            probs.append([w.astype(jnp.bfloat16) for w in weights])
        mixed = functools.reduce(
            jnp.add,
            [
                jnp.dot(jnp.concatenate(p, axis=0), v, preferred_element_type=jnp.float32)
                for p, v in zip(zip(*probs), values)
            ],
        )
        total = jnp.concatenate(totals, axis=0)
        out_ref[:rows, cols] = (mixed * (1.0 / total)).astype(out_ref.dtype)
        peak = jnp.concatenate(peaks, axis=0)
        lse = jnp.where(lane == head, peak * factor + jnp.log2(total), lse)
    turned = jnp.transpose(lse)
    stats = []
    for head in range(per_block):
        rest = turned[head : head + 1, :]
        for _ in range(PIECES):
            piece = rest.astype(out_ref.dtype)
            stats.append(piece.astype(jnp.float32))
            rest = rest - stats[-1]
    stats.append(jnp.zeros((STATS - len(stats), rows), jnp.float32))
    out_ref[rows:, :] = jnp.concatenate(stats, axis=0).astype(out_ref.dtype)


def attend(lists, q, q_first, heads, keys, values, kv_up, kv_down, first, kind, cost=WEIGHTY):
    rows = keys.shape[0]
    per_block = rows // HD
    width = per_block * HD
    lo, q_lo = first * HD // width, q_first * HD // width
    here = pl.BlockSpec((rows, width), lambda i: (0, lo + i))
    key_spec = pl.BlockSpec((1, rows, width), lambda i: (0, 0, lo + i))
    value_spec = pl.BlockSpec((1, rows, width), lambda i: (1, 0, lo + i))
    span = 3 * rows
    return pl.pallas_call(
        functools.partial(attend_kernel, rows, per_block),
        grid=(heads // per_block,),
        in_specs=[
            pl.BlockSpec((EXTRA, HD), lambda i: (lists.shape[0] // EXTRA - 1, 0)),
            pl.BlockSpec((rows, width), lambda i: (0, q_lo + i)),
            here,
            key_spec,
            key_spec,
            here,
            value_spec,
            value_spec,
        ],
        out_specs=pl.BlockSpec((rows + STATS, width), lambda i: (0, i)),
        out_shape=jax.ShapeDtypeStruct((rows + STATS, heads * HD), kind),
        compiler_params=pltpu.CompilerParams(vmem_limit_bytes=12 * MIB),
        cost_estimate=pl.CostEstimate(
            flops=cost, bytes_accessed=0, transcendentals=0
        ),
    )(lists, q, keys, kv_up, kv_down, values, kv_up, kv_down)


def merge_parts(rows, parts, partner_ref, attention):
    per_block = rows // HD
    width = per_block * HD
    for block in range(attention.shape[1] // width):
        tiles = []
        for part in parts:
            tiles.append(part[:, block * width : (block + 1) * width].astype(jnp.float32))
        shares = []
        for head in range(per_block):
            lses = []
            for number, t in enumerate(tiles):
                row = rows + PIECES * head
                lse = functools.reduce(
                    jnp.add, [t[row + i : row + i + 1, :] for i in range(PIECES)]
                )
                if number:
                    lse = jnp.where(partner_ref[number - 1] == 1, lse, -jnp.inf)
                lses.append(lse)
            top = functools.reduce(jnp.maximum, lses)
            raw = [jnp.exp2(lse - top) for lse in lses]
            total = functools.reduce(jnp.add, raw)
            shares.extend(r / total for r in raw)
        shares.append(jnp.zeros((HD - len(shares), rows), jnp.float32))
        turned = jnp.transpose(jnp.concatenate(shares, axis=0))
        for head in range(per_block):
            inner = slice(head * HD, (head + 1) * HD)
            mixed = functools.reduce(
                jnp.add,
                [
                    t[:rows, inner] * turned[:, head * len(tiles) + n : head * len(tiles) + n + 1]
                    for n, t in enumerate(tiles)
                ],
            )
            start = block * width + head * HD
            attention[:, start : start + HD] = mixed.astype(jnp.bfloat16)


def merge_kernel(rows, partner_ref, *refs):
    merge_parts(rows, refs[:-1], partner_ref, refs[-1])


def merge(partner, parts):
    rows, columns = parts[0].shape[0] - STATS, parts[0].shape[1]
    vmem = pl.BlockSpec(memory_space=pltpu.VMEM)
    return pl.pallas_call(
        functools.partial(merge_kernel, rows),
        in_specs=[pl.BlockSpec(memory_space=pltpu.SMEM)] + [vmem] * len(parts),
        out_specs=vmem,
        out_shape=jax.ShapeDtypeStruct((rows, columns), jnp.bfloat16),
        compiler_params=pltpu.CompilerParams(vmem_limit_bytes=8 * MIB),
        cost_estimate=pl.CostEstimate(flops=WEIGHTY, bytes_accessed=0, transcendentals=0),
    )(partner, *parts)


def bring(plan, sources, held, sems):
    copies = []
    for source, moves in zip(sources, plan):
        for from_row, size, place, _ in moves:
            copy = pltpu.make_async_copy(
                source.at[pl.ds(from_row, size), :],
                held.at[pl.ds(pl.multiple_of(place(), 16), size), :],
                sems.at[len(copies)],
            )
            copy.start()
            copies.append(copy)
    return copies


def load_kernel(plan, *refs):
    sources, (_, held, sems) = refs[: len(plan)], refs[len(plan) :]
    copies = bring(plan, sources, held, sems)
    for copy in copies:
        copy.wait()


def load(pieces, features, merged):
    arrays, plan = zip(*pieces)
    vmem = pl.BlockSpec(memory_space=pltpu.VMEM)
    return pl.pallas_call(
        functools.partial(load_kernel, plan),
        in_specs=[pl.BlockSpec(memory_space=pl.ANY)] * (len(arrays) + 1),
        out_specs=vmem,
        out_shape=jax.ShapeDtypeStruct((features, arrays[0].shape[1]), arrays[0].dtype),
        scratch_shapes=[pltpu.SemaphoreType.DMA((sum(len(m) for m in plan),))],
        compiler_params=pltpu.CompilerParams(vmem_limit_bytes=16 * MIB),
        cost_estimate=pl.CostEstimate(flops=WEIGHTY, bytes_accessed=0, transcendentals=0),
    )(*arrays, merged)


def project_kernel(plan, count, partner_ref, *refs):
    sources, refs = refs[: len(plan)], refs[len(plan) :]
    parts, refs = refs[:count], refs[count:]
    merged, held, out_ref, _, attention, staged, sems, out_sems = refs
    copies = bring(plan, sources, held, sems)
    first = merged.shape[1]
    attention[:, :first] = merged[...]
    merge_parts(attention.shape[0], parts, partner_ref, attention.at[:, first:])
    for copy in copies:
        copy.wait()
    columns = out_ref.shape[1]
    width = staged.shape[2]

    written = []
    for i in range(columns // width):
        there = pl.ds(i * width, width)
        staged[i] = jnp.dot(
            attention[...], held[:, there], preferred_element_type=jnp.float32
        ).astype(out_ref.dtype)
        copy = pltpu.make_async_copy(staged.at[i], out_ref.at[:, there], out_sems.at[i])
        copy.start()
        written.append(copy)
    for copy in written:
        copy.wait()


def project(pieces, held, partner, parts, merged):
    arrays, plan = zip(*pieces) if pieces else ((), ())
    rows, (features, columns) = merged.shape[0], held.shape
    vmem = pl.BlockSpec(memory_space=pltpu.VMEM)
    given = len(arrays) + len(parts)
    width = math.gcd(columns, 768)
    return pl.pallas_call(
        functools.partial(project_kernel, plan, len(parts)),
        in_specs=[pl.BlockSpec(memory_space=pltpu.SMEM)]
        + [pl.BlockSpec(memory_space=pl.ANY)] * len(arrays)
        + [vmem] * (len(parts) + 2),
        out_specs=(pl.BlockSpec(memory_space=pl.ANY), vmem),
        out_shape=(
            jax.ShapeDtypeStruct((rows, columns), jnp.bfloat16),
            jax.ShapeDtypeStruct(held.shape, held.dtype),
        ),
        input_output_aliases={given + 2: 1},
        scratch_shapes=[
            pltpu.VMEM((rows, features), jnp.bfloat16),
            pltpu.VMEM((columns // width, rows, width), jnp.bfloat16),
            pltpu.SemaphoreType.DMA((max(1, sum(len(m) for m in plan)),)),
            pltpu.SemaphoreType.DMA((columns // width,)),
        ],
        compiler_params=pltpu.CompilerParams(vmem_limit_bytes=28 * MIB),
    )(partner, *arrays, *parts, merged, held)[0]


def after(value, *done):
    return lax.optimization_barrier((value, *done))[0]


class Cube:
    def __init__(self, out_weight):
        self.shard = out_weight.shape[0]
        self.half = self.shard // 2
        self.list = []

    def add(self, array, *places):
        moves, row = [], 0
        for bit, turn in places:
            count = self.shard if turn is None else self.half

            def place(bit=bit, turn=turn):
                base = (lax.axis_index("seq") ^ bit) * self.shard
                if turn is None:
                    return base
                return base + (lax.axis_index("group") ^ turn) * self.half

            moves.append((row, count, place, bit // 8))
            row += count
        self.list.append((array, moves))

    def steps(self):
        depth = 8 * self.shard
        return [lambda r=r: (lax.axis_index("seq") // 8 ^ r) * depth for r in range(2)]


def body(groups, query_rows, key_rows, value_rows, block_list, out_weight):
    rows, features = query_rows.shape
    heads = features // HD
    devices = lax.axis_size("seq")
    grid_rows = devices // GRID_COLS
    row = lax.axis_index("seq") // GRID_COLS
    chunk_heads = heads // 2
    chunk = chunk_heads * HD
    phases = [parity for parity in range(2) if parity + 1 < grid_rows]
    cube = None
    if devices == 16 and groups == 2 and out_weight.shape[0] % 32 == 0:
        cube = Cube(out_weight)
        first = lax.axis_index("group") * cube.half
        mine = lax.dynamic_slice_in_dim(out_weight, first, cube.half, 0)
        mz = swap_bit(mine, 4)
        my = swap_bit(mine, 2)
        c0 = swap_bit(mine, 8)
    lists = jnp.pad(
        block_list.astype(jnp.bfloat16),
        ((0, EXTRA - FRAMES), (0, HD - block_list.shape[1])),
        constant_values=-1,
    )
    ahead = [mine] if cube else []
    kv = join(after(key_rows, *ahead), value_rows, cost=WEIGHTY).reshape(2, rows, features)
    kv_up = column_shift(kv, 1)
    kv_down = column_shift(kv, -1)
    asking = jnp.concatenate(
        [after(query_rows, kv)[:, :chunk], jnp.tile(lists, (1, chunk_heads))], axis=0
    )
    if cube:
        lists = fence(after(lists, asking, mz, my))
    sent = []
    for parity in phases:
        pairs = row_pairs(parity)
        first = lax.ppermute(asking, "seq", pairs)
        second = query_rows[:, chunk:]
        if cube:
            second = after(second, first)
            c0 = after(c0, lists)
            cz = swap_bit(after(c0, first), 4)
            first = after(first, c0)
            near = join(mz, my, c0, cost=WEIGHTY)
            x0 = swap_group(near, groups)
            second = after(second, near)
            pair = join(mz, after(c0, first))
            y1 = swap_bit(pair, 2)
        sent.append([first, lax.ppermute(second, "seq", pairs)])
    common = (key_rows, value_rows, kv_up, kv_down)
    others = []
    for parity, asked in zip(phases, sent):
        back = []
        for number, q in enumerate(asked):
            if number:
                q = after(q, part, cz) if cube else after(q, part)
            part = attend(asked[0], q, 0, chunk_heads, *common, number * chunk_heads, jnp.bfloat16)
            if cube and not number:
                cz = after(cz, part)
                cy = swap_bit(cz, 2)
                x1 = swap_group(cz, groups)
            sending = part if number else fence(after(part, asked[1]), 0)
            back.append(lax.ppermute(sending, "seq", row_pairs(parity)))
            last = part
        others.append(back)
    if cube:
        y1, cy = after(y1, last), after(cy, last)
        x2 = swap_group(y1, groups)
        x3 = swap_group(cy, groups)
        base = join(out_weight, near, after(x0, last), cz, after(x1, last))
    own = []
    for number in range(2):
        q, begin = query_rows, number * chunk_heads
        if phases:
            q = after(q, last, *own, *([cy] if cube and number else []))
        own.append(attend(lists, q, begin, chunk_heads, *common, begin, jnp.float32, 0))
    partner = jnp.stack(
        [
            jnp.where(row % 2 == parity, row + 1 < grid_rows, row > 0).astype(jnp.int32)
            for parity in phases
        ]
        or [jnp.int32(0)]
    )
    runs = [[own[n]] + [back[n] for back in others] for n in range(2)]
    merged = merge(partner, runs[0])
    if cube:
        tail = join(y1, after(x2, own[1]), cy, x3)
        at_base = [(0, None), (4, 0), (2, 0), (8, 0), (4, 1), (2, 1), (8, 1), (12, 0), (12, 1)]
        at_tail = [(6, 0), (10, 0), (6, 1), (10, 1), (14, 0), (14, 1)]
        for array, places in ((base, at_base), (tail, at_tail)):
            cube.add(array, *places)
            cube.add(swap_bit(array, 1), *[(bit ^ 1, turn) for bit, turn in places])
        pieces = cube.list
    else:
        gathered = lax.all_gather(out_weight, "seq", axis=0, tiled=True)
        pieces = [(gathered, [(0, gathered.shape[0], lambda: 0, 0)])]
    held = load(pieces[:2], features, merged)
    return project(pieces[2:], held, partner, runs[1], merged)


def solution(mesh):
    placed = (
        P(("group", "seq"), None),
        P(("group", "seq"), None),
        P(("group", "seq"), None),
        P(("group", "seq"), None),
        P("seq", None),
    )
    return jax.shard_map(
        functools.partial(body, mesh.shape["group"]),
        mesh=mesh,
        in_specs=placed,
        out_specs=P(("group", "seq"), None),
        check_vma=False,
    )
```

```python
import functools
import math

import jax
import jax.numpy as jnp
from jax import lax
from jax.experimental import pallas as pl
from jax.experimental.pallas import tpu as pltpu
from jax.sharding import PartitionSpec as P

HD = 128
FRAMES = 2
GRID_COLS = 8
EXTRA = 8
STATS = 8
PIECES = 3
LOG2E = math.log2(math.e)
MIB = 1024 * 1024
VMEM_BYTES = 48 * MIB
WEIGHTY = 10**12


def swap_bit(value, bit):
    count = lax.axis_size("seq")
    return lax.ppermute(value, "seq", [(s, s ^ bit) for s in range(count)])


def swap_group(value, groups):
    return lax.ppermute(value, "group", [(s, s ^ 1) for s in range(groups)])


def column_shift(value, steps):
    count = lax.axis_size("seq")
    pairs = [(s, s + steps) for s in range(count) if 0 <= s % GRID_COLS + steps < GRID_COLS]
    return lax.ppermute(value, "seq", pairs)


def row_pairs(parity):
    count = lax.axis_size("seq")
    rows = count // GRID_COLS
    pairs = []
    for s in range(count):
        row = s // GRID_COLS
        other = row + 1 if row % 2 == parity else row - 1
        if 0 <= other < rows:
            pairs.append((s, s + (other - row) * GRID_COLS))
    return pairs


def join_kernel(count, *refs):
    sources, (out_ref, sems) = refs[:count], refs[count:]
    copies, first = [], 0
    for i, source in enumerate(sources):
        size = source.shape[0]
        copy = pltpu.make_async_copy(source, out_ref.at[pl.ds(first, size), :], sems.at[i])
        copy.start()
        copies.append(copy)
        first += size
    for copy in copies:
        copy.wait()


def join(*arrays, cost=0):
    rows = sum(array.shape[0] for array in arrays)
    return pl.pallas_call(
        functools.partial(join_kernel, len(arrays)),
        in_specs=[pl.BlockSpec(memory_space=pl.ANY)] * len(arrays),
        out_specs=pl.BlockSpec(memory_space=pltpu.VMEM),
        out_shape=jax.ShapeDtypeStruct((rows, arrays[0].shape[1]), arrays[0].dtype),
        scratch_shapes=[pltpu.SemaphoreType.DMA((len(arrays),))],
        compiler_params=pltpu.CompilerParams(vmem_limit_bytes=8 * MIB),
        cost_estimate=pl.CostEstimate(flops=cost, bytes_accessed=0, transcendentals=0),
    )(*arrays)


def fence_kernel(in_ref, out_ref):
    out_ref[...] = in_ref[...]


def fence(value, cost=WEIGHTY):
    vmem = pl.BlockSpec(memory_space=pltpu.VMEM)
    return pl.pallas_call(
        fence_kernel,
        in_specs=[vmem],
        out_specs=vmem,
        out_shape=jax.ShapeDtypeStruct(value.shape, value.dtype),
        cost_estimate=pl.CostEstimate(flops=cost, bytes_accessed=0, transcendentals=0),
    )(value)


def attend_kernel(rows, per_block, list_ref, q_ref, k0, ka, kb, v0, va, vb, out_ref):
    factor = HD ** (-0.5) * LOG2E
    tile = rows // FRAMES
    position = lax.axis_index("seq")
    lists = list_ref[...].astype(jnp.float32)
    masks = []
    for step in (0, -1, 1):
        bits = []
        for frame in range(FRAMES):
            tile_id = (position + step) * FRAMES + frame
            tile_id = jnp.where(tile_id >= 0, tile_id, -2).astype(jnp.float32)
            hit = jnp.max(jnp.where(lists == tile_id, 0.0, -jnp.inf), axis=1, keepdims=True)
            bits.append(jnp.broadcast_to(hit, (hit.shape[0], tile)))
        masks.append(jnp.concatenate(bits, axis=1))
    nt = (((1,), (1,)), ((), ()))
    lse = jnp.zeros((rows, HD), jnp.float32)
    lane = lax.broadcasted_iota(jnp.int32, (rows, HD), 1)
    frames = [slice(frame * tile, (frame + 1) * tile) for frame in range(FRAMES)]
    heads = [slice(head * HD, (head + 1) * HD) for head in range(per_block)]
    for head, cols in enumerate(heads):
        keys = [k0[:, cols], ka[0, :, cols], kb[0, :, cols]]
        product = [
            lax.dot_general(q_ref[:rows, cols], key, nt, preferred_element_type=jnp.float32)
            for key in keys
        ]
        values = [v0[:, cols], va[0, :, cols], vb[0, :, cols]]
        peaks, totals, probs = [], [], []
        for frame, here in enumerate(frames):
            scores = [s[here] + mask[frame : frame + 1, :] for s, mask in zip(product, masks)]
            peak = functools.reduce(jnp.maximum, scores)
            peak = jnp.max(peak, axis=1, keepdims=True)
            weights = [jnp.exp2((s - peak) * factor) for s in scores]
            totals.append(jnp.sum(functools.reduce(jnp.add, weights), axis=1, keepdims=True))
            peaks.append(peak)
            probs.append([w.astype(jnp.bfloat16) for w in weights])
        mixed = functools.reduce(
            jnp.add,
            [
                jnp.dot(jnp.concatenate(p, axis=0), v, preferred_element_type=jnp.float32)
                for p, v in zip(zip(*probs), values)
            ],
        )
        total = jnp.concatenate(totals, axis=0)
        out_ref[:rows, cols] = (mixed * (1.0 / total)).astype(out_ref.dtype)
        peak = jnp.concatenate(peaks, axis=0)
        lse = jnp.where(lane == head, peak * factor + jnp.log2(total), lse)
    turned = jnp.transpose(lse)
    stats = []
    for head in range(per_block):
        rest = turned[head : head + 1, :]
        for _ in range(PIECES):
            piece = rest.astype(out_ref.dtype)
            stats.append(piece.astype(jnp.float32))
            rest = rest - stats[-1]
    stats.append(jnp.zeros((STATS - len(stats), rows), jnp.float32))
    out_ref[rows:, :] = jnp.concatenate(stats, axis=0).astype(out_ref.dtype)


def attend(lists, q, q_first, heads, keys, values, kv_up, kv_down, first, kind, cost=WEIGHTY):
    rows = keys.shape[0]
    per_block = rows // HD
    width = per_block * HD
    lo, q_lo = first * HD // width, q_first * HD // width
    here = pl.BlockSpec((rows, width), lambda i: (0, lo + i))
    key_spec = pl.BlockSpec((1, rows, width), lambda i: (0, 0, lo + i))
    value_spec = pl.BlockSpec((1, rows, width), lambda i: (1, 0, lo + i))
    span = 3 * rows
    return pl.pallas_call(
        functools.partial(attend_kernel, rows, per_block),
        grid=(heads // per_block,),
        in_specs=[
            pl.BlockSpec((EXTRA, HD), lambda i: (0, 0)),
            pl.BlockSpec((rows, width), lambda i: (0, q_lo + i)),
            here,
            key_spec,
            key_spec,
            here,
            value_spec,
            value_spec,
        ],
        out_specs=pl.BlockSpec((rows + STATS, width), lambda i: (0, i)),
        out_shape=jax.ShapeDtypeStruct((rows + STATS, heads * HD), kind),
        compiler_params=pltpu.CompilerParams(vmem_limit_bytes=12 * MIB),
        cost_estimate=pl.CostEstimate(
            flops=cost, bytes_accessed=0, transcendentals=0
        ),
    )(lists, q, keys, kv_up, kv_down, values, kv_up, kv_down)


def merge_parts(rows, parts, partner_ref, attention):
    per_block = rows // HD
    width = per_block * HD
    for block in range(attention.shape[1] // width):
        tiles = []
        for part in parts:
            tiles.append(part[:, block * width : (block + 1) * width].astype(jnp.float32))
        shares = []
        for head in range(per_block):
            lses = []
            for number, t in enumerate(tiles):
                row = rows + PIECES * head
                lse = functools.reduce(
                    jnp.add, [t[row + i : row + i + 1, :] for i in range(PIECES)]
                )
                if number:
                    lse = jnp.where(partner_ref[number - 1] == 1, lse, -jnp.inf)
                lses.append(lse)
            top = functools.reduce(jnp.maximum, lses)
            raw = [jnp.exp2(lse - top) for lse in lses]
            total = functools.reduce(jnp.add, raw)
            shares.extend(r / total for r in raw)
        shares.append(jnp.zeros((HD - len(shares), rows), jnp.float32))
        turned = jnp.transpose(jnp.concatenate(shares, axis=0))
        for head in range(per_block):
            inner = slice(head * HD, (head + 1) * HD)
            mixed = functools.reduce(
                jnp.add,
                [
                    t[:rows, inner] * turned[:, head * len(tiles) + n : head * len(tiles) + n + 1]
                    for n, t in enumerate(tiles)
                ],
            )
            start = block * width + head * HD
            attention[:, start : start + HD] = mixed.astype(jnp.bfloat16)


def merge_kernel(rows, partner_ref, *refs):
    merge_parts(rows, refs[:-1], partner_ref, refs[-1])


def merge(partner, parts):
    rows, columns = parts[0].shape[0] - STATS, parts[0].shape[1]
    vmem = pl.BlockSpec(memory_space=pltpu.VMEM)
    return pl.pallas_call(
        functools.partial(merge_kernel, rows),
        in_specs=[pl.BlockSpec(memory_space=pltpu.SMEM)] + [vmem] * len(parts),
        out_specs=vmem,
        out_shape=jax.ShapeDtypeStruct((rows, columns), jnp.bfloat16),
        compiler_params=pltpu.CompilerParams(vmem_limit_bytes=8 * MIB),
        cost_estimate=pl.CostEstimate(flops=WEIGHTY, bytes_accessed=0, transcendentals=0),
    )(partner, *parts)


def bring(plan, sources, held, sems):
    copies = []
    for source, moves in zip(sources, plan):
        for from_row, size, place, _ in moves:
            copy = pltpu.make_async_copy(
                source.at[pl.ds(from_row, size), :],
                held.at[pl.ds(pl.multiple_of(place(), 16), size), :],
                sems.at[len(copies)],
            )
            copy.start()
            copies.append(copy)
    return copies


def load_kernel(plan, *refs):
    sources, (_, held, sems) = refs[: len(plan)], refs[len(plan) :]
    copies = bring(plan, sources, held, sems)
    for copy in copies:
        copy.wait()


def load(pieces, features, merged):
    arrays, plan = zip(*pieces)
    vmem = pl.BlockSpec(memory_space=pltpu.VMEM)
    return pl.pallas_call(
        functools.partial(load_kernel, plan),
        in_specs=[pl.BlockSpec(memory_space=pl.ANY)] * (len(arrays) + 1),
        out_specs=vmem,
        out_shape=jax.ShapeDtypeStruct((features, arrays[0].shape[1]), arrays[0].dtype),
        scratch_shapes=[pltpu.SemaphoreType.DMA((sum(len(m) for m in plan),))],
        compiler_params=pltpu.CompilerParams(vmem_limit_bytes=16 * MIB),
        cost_estimate=pl.CostEstimate(flops=WEIGHTY, bytes_accessed=0, transcendentals=0),
    )(*arrays, merged)


def project_kernel(plan, count, partner_ref, *refs):
    sources, refs = refs[: len(plan)], refs[len(plan) :]
    parts, refs = refs[:count], refs[count:]
    merged, held, out_ref, _, attention, staged, sems, out_sems = refs
    copies = bring(plan, sources, held, sems)
    first = merged.shape[1]
    attention[:, :first] = merged[...]
    merge_parts(attention.shape[0], parts, partner_ref, attention.at[:, first:])
    for copy in copies:
        copy.wait()
    columns = out_ref.shape[1]
    width = staged.shape[2]

    written = []
    for i in range(columns // width):
        there = pl.ds(i * width, width)
        staged[i] = jnp.dot(
            attention[...], held[:, there], preferred_element_type=jnp.float32
        ).astype(out_ref.dtype)
        copy = pltpu.make_async_copy(staged.at[i], out_ref.at[:, there], out_sems.at[i])
        copy.start()
        written.append(copy)
    for copy in written:
        copy.wait()


def project(pieces, held, partner, parts, merged):
    arrays, plan = zip(*pieces) if pieces else ((), ())
    rows, (features, columns) = merged.shape[0], held.shape
    vmem = pl.BlockSpec(memory_space=pltpu.VMEM)
    given = len(arrays) + len(parts)
    width = math.gcd(columns, 768)
    return pl.pallas_call(
        functools.partial(project_kernel, plan, len(parts)),
        in_specs=[pl.BlockSpec(memory_space=pltpu.SMEM)]
        + [pl.BlockSpec(memory_space=pl.ANY)] * len(arrays)
        + [vmem] * (len(parts) + 2),
        out_specs=(pl.BlockSpec(memory_space=pl.ANY), vmem),
        out_shape=(
            jax.ShapeDtypeStruct((rows, columns), jnp.bfloat16),
            jax.ShapeDtypeStruct(held.shape, held.dtype),
        ),
        input_output_aliases={given + 2: 1},
        scratch_shapes=[
            pltpu.VMEM((rows, features), jnp.bfloat16),
            pltpu.VMEM((columns // width, rows, width), jnp.bfloat16),
            pltpu.SemaphoreType.DMA((max(1, sum(len(m) for m in plan)),)),
            pltpu.SemaphoreType.DMA((columns // width,)),
        ],
        compiler_params=pltpu.CompilerParams(vmem_limit_bytes=28 * MIB),
    )(partner, *arrays, *parts, merged, held)[0]


def after(value, *done):
    return lax.optimization_barrier((value, *done))[0]


class Cube:
    def __init__(self, out_weight):
        self.shard = out_weight.shape[0]
        self.half = self.shard // 2
        self.list = []

    def add(self, array, *places):
        moves, row = [], 0
        for bit, turn in places:
            count = self.shard if turn is None else self.half

            def place(bit=bit, turn=turn):
                base = (lax.axis_index("seq") ^ bit) * self.shard
                if turn is None:
                    return base
                return base + (lax.axis_index("group") ^ turn) * self.half

            moves.append((row, count, place, bit // 8))
            row += count
        self.list.append((array, moves))

    def steps(self):
        depth = 8 * self.shard
        return [lambda r=r: (lax.axis_index("seq") // 8 ^ r) * depth for r in range(2)]


def body(groups, query_rows, key_rows, value_rows, block_list, out_weight):
    rows, features = query_rows.shape
    heads = features // HD
    devices = lax.axis_size("seq")
    grid_rows = devices // GRID_COLS
    row = lax.axis_index("seq") // GRID_COLS
    chunk_heads = heads // 2
    chunk = chunk_heads * HD
    phases = [parity for parity in range(2) if parity + 1 < grid_rows]
    cube = None
    if devices == 16 and groups == 2 and out_weight.shape[0] % 32 == 0:
        cube = Cube(out_weight)
        first = lax.axis_index("group") * cube.half
        mine = lax.dynamic_slice_in_dim(out_weight, first, cube.half, 0)
        mz = swap_bit(mine, 4)
        my = swap_bit(mine, 2)
        c0 = swap_bit(mine, 8)
    lists = jnp.pad(
        block_list.astype(jnp.bfloat16),
        ((0, EXTRA - FRAMES), (0, HD - block_list.shape[1])),
        constant_values=-1,
    )
    ahead = [mine] if cube else []
    kv = join(after(key_rows, *ahead), value_rows, cost=WEIGHTY).reshape(2, rows, features)
    kv_up = column_shift(kv, 1)
    kv_down = column_shift(kv, -1)
    asking = jnp.concatenate(
        [after(query_rows, kv)[:, :chunk], jnp.tile(lists, (1, chunk_heads))], axis=0
    )
    if cube:
        lists = fence(after(lists, asking, mz, my))
    sent = []
    for parity in phases:
        pairs = row_pairs(parity)
        first = lax.ppermute(asking, "seq", pairs)
        second = query_rows[:, chunk:]
        if cube:
            second = after(second, first)
            c0 = after(c0, lists)
            cz = swap_bit(after(c0, first), 4)
            first = after(first, c0)
            near = join(mz, my, c0, cost=WEIGHTY)
            x0 = swap_group(near, groups)
            second = after(second, near)
            pair = join(mz, after(c0, first))
            y1 = swap_bit(pair, 2)
        sent.append([first, lax.ppermute(second, "seq", pairs)])
    common = (key_rows, value_rows, kv_up, kv_down)
    others = []
    for parity, asked in zip(phases, sent):
        back = []
        for number, q in enumerate(asked):
            if number:
                q = after(q, part, cz) if cube else after(q, part)
            part = attend(asked[0][rows:, :HD], q, 0, chunk_heads, *common, number * chunk_heads, jnp.bfloat16)
            if cube and not number:
                cz = after(cz, part)
                cy = swap_bit(cz, 2)
                x1 = swap_group(cz, groups)
            sending = part if number else fence(after(part, asked[1]), 0)
            back.append(lax.ppermute(sending, "seq", row_pairs(parity)))
            last = part
        others.append(back)
    if cube:
        y1, cy = after(y1, last), after(cy, last)
        x2 = swap_group(y1, groups)
        x3 = swap_group(cy, groups)
        base = join(out_weight, near, after(x0, last), cz, after(x1, last))
    own = []
    for number in range(2):
        q, begin = query_rows, number * chunk_heads
        if phases:
            q = after(q, last, *own, *([cy] if cube and number else []))
        own.append(attend(lists, q, begin, chunk_heads, *common, begin, jnp.float32, 0))
    partner = jnp.stack(
        [
            jnp.where(row % 2 == parity, row + 1 < grid_rows, row > 0).astype(jnp.int32)
            for parity in phases
        ]
        or [jnp.int32(0)]
    )
    runs = [[own[n]] + [back[n] for back in others] for n in range(2)]
    merged = merge(partner, runs[0])
    if cube:
        tail = join(y1, after(x2, own[1]), cy, x3)
        at_base = [(0, None), (4, 0), (2, 0), (8, 0), (4, 1), (2, 1), (8, 1), (12, 0), (12, 1)]
        at_tail = [(6, 0), (10, 0), (6, 1), (10, 1), (14, 0), (14, 1)]
        for array, places in ((base, at_base), (tail, at_tail)):
            cube.add(array, *places)
            cube.add(swap_bit(array, 1), *[(bit ^ 1, turn) for bit, turn in places])
        pieces = cube.list
    else:
        gathered = lax.all_gather(out_weight, "seq", axis=0, tiled=True)
        pieces = [(gathered, [(0, gathered.shape[0], lambda: 0, 0)])]
    held = load(pieces[:2], features, merged)
    return project(pieces[2:], held, partner, runs[1], merged)


def solution(mesh):
    placed = (
        P(("group", "seq"), None),
        P(("group", "seq"), None),
        P(("group", "seq"), None),
        P(("group", "seq"), None),
        P("seq", None),
    )
    return jax.shard_map(
        functools.partial(body, mesh.shape["group"]),
        mesh=mesh,
        in_specs=placed,
        out_specs=P(("group", "seq"), None),
        check_vma=False,
    )
```
